32 devices in a mesh: ctx: 4 (over y, x), fsdp: 8 (over z, core).
Axes of the slice: x: 2, y: 2, z: 4, core: 2. Of those that a mesh axis runs over, the one named last changes fastest.
Arguments:
- tokens: bfloat16 [8, 512, 1536], P('fsdp', 'ctx'), may hold values from -6 to 6
- document_starts: int32 [8, 8], P('fsdp'), may hold values from 0 to 512, as said below
- attention_weights: float32 [3584, 1536], P('fsdp'), may hold values from -0.4 to 0.4
- projection_bias: float32 [2048], P('fsdp'), may hold values from -3 to 3
- norm_gains: float32 [2, 1536], P(None, 'fsdp'), may hold values from 0.25 to 1.75
- hidden_weights: float32 [8960, 4608], P('fsdp'), may hold values from -0.15625 to 0.15625
- cotangent: bfloat16 [8, 512, 1536], P('fsdp', 'ctx'), may hold values from -6 to 6
Outputs:
- output: bfloat16 [8, 512, 1536], P('fsdp', 'ctx')
- input_gradient: float32 [8, 512, 1536], P('fsdp', 'ctx')
- attention_gradient: float32 [3584, 1536], P(('fsdp', 'ctx'))
- bias_gradient: float32 [2048], P(('fsdp', 'ctx'))
- gain_gradient: float32 [2, 1536], P(None, ('fsdp', 'ctx'))
- hidden_gradient: float32 [8960, 4608], P(('fsdp', 'ctx'))
The draws below stay inside these ranges and needn't reach their ends.
Inputs may be any that keep to these rules, and one draw needn't show every extreme that they name: `document_starts`: each row rises strictly from 0 and then holds 512 as padding in its last slots; document j of a stream covers the positions from its entry up to the next entry.
All inputs are finite; a program needn't handle non-finite values.
Results may differ from the reference program's by a relative error of at most 0.024.
Values may be sent and summed in bfloat16 or wider, within the bound.
No kernel may reach another device: no remote copies, remote signals or barrier semaphores. Data moves between devices by JAX's collectives and lax.ppermute only.
A program may use at most 704 MiB of HBM per device.

```python
import jax
import jax.numpy as jnp
from jax import lax

D = 1536
FF = 8960
HEADS = 12
KV_HEADS = 2
HEAD_DIM = 128
TOK_DEV = 128
START_SLOTS = 8
PROJECTION_WIDTH = 2048
ATTENTION_ROWS = 3584
STREAMS = 8
SEQ = 512


output_spread = 0.08


def draw_document_starts(key, part):
    keys = jax.random.split(key, 3)
    leading = jax.random.randint(keys[0], (STREAMS, 1), 1, TOK_DEV)
    trailing = jax.random.randint(keys[1], (STREAMS, 1), 4, TOK_DEV)
    pieces = jax.random.randint(keys[2], (STREAMS, 1), 1, 5)
    tail = SEQ - trailing
    columns = [jnp.zeros((STREAMS, 1), jnp.int32), leading, tail]
    for step in range(1, 4):
        inside = tail + trailing * step // pieces
        columns.append(jnp.where(step < pieces, inside, SEQ))
    for step in range(START_SLOTS - 6):
        columns.append(jnp.full((STREAMS, 1), SEQ, jnp.int32))
    return jnp.concatenate(columns, axis=1).astype(jnp.int32)


def draw_attention_weights(key, part):
    rows = jnp.arange(ATTENTION_ROWS)[:, None]
    spread = jnp.where(rows < PROJECTION_WIDTH, D ** (-0.5), output_spread).astype(jnp.float32)
    base = jnp.clip(jax.random.normal(key, (ATTENTION_ROWS, D), jnp.float32), -5.0, 5.0)
    return (base * spread).astype(jnp.float32)


def levels(rng, dims, cuts, least, high):
    factor_of, own = 1.0, jax.random.fold_in(rng, 6)
    for dim, blocks in cuts:
        steps = jnp.exp(jax.random.uniform(jax.random.fold_in(own, dim), (blocks,), jnp.float32, least / len(cuts), high / len(cuts)))
        factor_of = factor_of * jnp.repeat(steps, dims[dim] // blocks).reshape([-1 if axis == dim else 1 for axis in range(len(dims))])
    return factor_of


def noise(own_key, shape, scale, most, cuts=(), kind=jnp.bfloat16):
    values = scale * jax.random.normal(own_key, shape, jnp.float32)
    if cuts:
        values = values * levels(own_key, shape, cuts, -0.22, 0.18)
    return jnp.clip(values, -most, most).astype(kind)


def setup_inputs(seed: int = 0) -> dict:
    arg_keys = jax.random.split(jax.random.key(seed), 8)
    tokens = noise(arg_keys[0], (STREAMS, SEQ, D), 1.0, 6.0, ((0, 8), (1, 4)))
    document_starts = draw_document_starts(jax.random.fold_in(arg_keys[7], 71), 0)
    attention_weights = draw_attention_weights(jax.random.fold_in(arg_keys[7], 71), 0)
    projection_bias = noise(arg_keys[3], (PROJECTION_WIDTH,), 0.5, 3.0, ((0, 8),), jnp.float32)
    norm_gains = jnp.clip(1.0 + 0.15 * jax.random.normal(arg_keys[4], (2, D), jnp.float32), 0.25, 1.75)
    hidden_weights = noise(arg_keys[5], (FF, 3 * D), D ** -0.5, 0.15625, ((0, 8),), jnp.float32)
    cotangent = noise(arg_keys[6], (STREAMS, SEQ, D), 1.0, 6.0, ((0, 8), (1, 4)))
    return dict(tokens=tokens, document_starts=document_starts, attention_weights=attention_weights, projection_bias=projection_bias, norm_gains=norm_gains, hidden_weights=hidden_weights, cotangent=cotangent)


@jax.custom_vjp
def low(v):
    return lax.optimization_barrier(v.astype(jnp.bfloat16)).astype(jnp.float32)

@jax.custom_vjp
def low_back(v):
    return v

def low_keep(v):
    return (low(v), None)

def low_pass(kept, grad):
    return (grad,)

def back_keep(v):
    return (v, None)

def back_low(kept, grad):
    return (low(grad),)
low.defvjp(low_keep, low_pass)
low_back.defvjp(back_keep, back_low)
EPSILON = 1e-06
THETA = 10000.0
EXACT = lax.Precision.HIGHEST

def rope_tables(positions):
    half = HEAD_DIM // 2
    frequency = THETA ** (-(jnp.arange(half, dtype=jnp.float32) * 2.0 / HEAD_DIM))
    angle = positions.astype(jnp.float32)[:, None] * frequency[None, :]
    cosine = jnp.concatenate([jnp.cos(angle), jnp.cos(angle)], axis=1)
    sine = jnp.concatenate([jnp.sin(angle), jnp.sin(angle)], axis=1)
    return (cosine, sine)

def rotate(vectors, cosine, sine):
    half = vectors.shape[-1] // 2
    turned = jnp.concatenate([-vectors[..., half:], vectors[..., :half]], axis=-1)
    return vectors * cosine[:, None, :] + turned * sine[:, None, :]

def stream_forward(inputs, starts, attention_weights, projection_bias, norm_gains, hidden_weights):
    weights = low(attention_weights)
    biases = low(projection_bias)
    gains = low(norm_gains)
    feed_weights = low(hidden_weights)
    query_width = HEADS * HEAD_DIM
    key_width = KV_HEADS * HEAD_DIM
    group = HEADS // KV_HEADS
    scale = HEAD_DIM ** (-0.5)
    positions = jnp.arange(SEQ, dtype=jnp.int32)
    segment = lax.optimization_barrier(jnp.sum((starts[None, :] <= positions[:, None]).astype(jnp.int32), axis=1)) - 1
    cosine, sine = rope_tables(positions)
    normed_one = low(inputs * lax.rsqrt(lax.optimization_barrier(jnp.mean(inputs * inputs, axis=-1, keepdims=True)) + EPSILON) * gains[0])
    projected = low_back(jnp.dot(normed_one, weights[:PROJECTION_WIDTH].T, precision=EXACT) + biases)
    queries = low(rotate(projected[:, :query_width].reshape(SEQ, HEADS, HEAD_DIM), cosine, sine))
    keys = low(rotate(projected[:, query_width:query_width + key_width].reshape(SEQ, KV_HEADS, HEAD_DIM), cosine, sine))
    values = low(projected[:, query_width + key_width:].reshape(SEQ, KV_HEADS, HEAD_DIM))
    block = min(512, SEQ)
    count = SEQ // block

    def attend(item):
        query_block, first = item
        query_positions = first + jnp.arange(block, dtype=jnp.int32)
        query_segment = lax.dynamic_slice_in_dim(segment, first, block)
        scores = low_back(jnp.einsum('tkgd,skd->kgts', query_block, keys, precision=EXACT) * scale)
        allowed = (query_segment[:, None] == segment[None, :]) & (positions[None, :] <= query_positions[:, None])
        scores = jnp.where(allowed, scores, -jnp.inf)
        top = lax.optimization_barrier(jnp.max(scores, axis=-1, keepdims=True))
        raised = jnp.exp(scores - top)
        probability = raised / lax.optimization_barrier(jnp.sum(raised, axis=-1, keepdims=True))
        return jnp.einsum('kgts,skd->tkgd', low(probability), values, precision=EXACT)
    blocks = queries.reshape(count, block, KV_HEADS, group, HEAD_DIM)
    firsts = jnp.arange(count, dtype=jnp.int32) * block
    mixed = lax.map(jax.checkpoint(attend), (blocks, firsts)).reshape(SEQ, query_width)
    mixed = low_back(low(mixed))
    branch = low_back(jnp.dot(mixed, weights[PROJECTION_WIDTH:], precision=EXACT))
    residual = inputs + branch
    normed_two = low(residual * lax.rsqrt(lax.optimization_barrier(jnp.mean(residual * residual, axis=-1, keepdims=True)) + EPSILON) * gains[1])
    gate_value = low_back(jnp.dot(normed_two, feed_weights[:, :D].T, precision=EXACT))
    up_value = low_back(jnp.dot(normed_two, feed_weights[:, D:2 * D].T, precision=EXACT))
    hidden = low(jax.nn.silu(gate_value) * up_value)
    return residual + jnp.dot(hidden, feed_weights[:, 2 * D:], precision=EXACT)

def reference(tokens, document_starts, attention_weights, projection_bias, norm_gains, hidden_weights, cotangent):

    def one_stream(totals, item):
        stream_tokens, starts, stream_upstream = item

        def forward(inputs, weights_one, bias_one, gains_one, weights_two):
            return stream_forward(inputs, starts, weights_one, bias_one, gains_one, weights_two)
        result, pullback = jax.vjp(forward, stream_tokens.astype(jnp.float32), attention_weights, projection_bias, norm_gains, hidden_weights)
        gradients = pullback(stream_upstream.astype(jnp.float32))
        totals = tuple((running + extra for running, extra in zip(totals, gradients[1:])))
        return (totals, (result.astype(jnp.bfloat16), gradients[0]))
    initial = (jnp.zeros_like(attention_weights), jnp.zeros_like(projection_bias), jnp.zeros_like(norm_gains), jnp.zeros_like(hidden_weights))
    totals, (outputs, input_gradient) = lax.scan(one_stream, initial, (tokens, document_starts, cotangent))
    return (outputs, input_gradient, totals[0], totals[1], totals[2], totals[3])
```

```python
import jax
import jax.numpy as jnp
from jax import lax
from jax.sharding import PartitionSpec as P

HEADS = 12
KV_HEADS = 2
HEAD_DIM = 128


EPSILON = 1e-06
THETA = 10000.0
LOWEST = -1e30


def rope_tables(positions, width):
    half = width // 2
    frequency = THETA ** (-(jnp.arange(half, dtype=jnp.float32) * 2.0 / width))
    angle = positions.astype(jnp.float32)[:, None] * frequency[None, :]
    cosine = jnp.concatenate([jnp.cos(angle), jnp.cos(angle)], axis=1)
    sine = jnp.concatenate([jnp.sin(angle), jnp.sin(angle)], axis=1)
    return (cosine, sine)


def rotate(vectors, cosine, sine):
    half = vectors.shape[-1] // 2
    turned = jnp.concatenate([-vectors[..., half:], vectors[..., :half]], axis=-1)
    return vectors * cosine[:, None, :] + turned * sine[:, None, :]


def unrotate(gradient, cosine, sine):
    half = gradient.shape[-1] // 2
    moved = gradient * sine[:, None, :]
    return gradient * cosine[:, None, :] + jnp.concatenate(
        [moved[..., half:], -moved[..., :half]], axis=-1
    )


def segments(starts, positions):
    return jnp.sum((starts[None, :] <= positions[:, None]).astype(jnp.int32), axis=1) - 1


def inverse_rms(values):
    return lax.rsqrt(jnp.mean(values * values, axis=-1, keepdims=True) + EPSILON)


def norm_backward(inputs, scale, gain, back_normed):
    weighted = back_normed * gain
    back_inputs = scale * weighted - inputs * scale * scale * scale * jnp.mean(
        inputs * weighted, axis=-1, keepdims=True
    )
    return (back_inputs, jnp.sum(back_normed * inputs * scale, axis=0))


def hidden_values(normed, weights, width):
    gate_value = jnp.einsum(
        "td,fd->tf", normed, weights[:, :width], preferred_element_type=jnp.float32
    )
    up_value = jnp.einsum(
        "td,fd->tf", normed, weights[:, width : 2 * width], preferred_element_type=jnp.float32
    )
    sigmoid_gate = jax.nn.sigmoid(gate_value)
    silu_gate = gate_value * sigmoid_gate
    hidden = (silu_gate * up_value).astype(jnp.bfloat16)
    return (gate_value, up_value, sigmoid_gate, silu_gate, hidden)


def hidden_backward(upstream, weights, width, kept):
    gate_value, up_value, sigmoid_gate, silu_gate = kept
    back_hidden = jnp.einsum(
        "td,fd->tf", upstream, weights[:, 2 * width :], preferred_element_type=jnp.float32
    )
    back_up = (back_hidden * silu_gate).astype(jnp.bfloat16)
    back_gate = (
        back_hidden * up_value * sigmoid_gate * (1.0 + gate_value * (1.0 - sigmoid_gate))
    ).astype(jnp.bfloat16)
    return (back_gate, back_up)


def per_device(
    tokens,
    document_starts,
    attention_weights,
    projection_bias,
    norm_gains,
    hidden_weights,
    cotangent,
):
    rows = tokens.shape[1]
    width = tokens.shape[2]
    group = HEADS // KV_HEADS
    query_width = HEADS * HEAD_DIM
    key_width = KV_HEADS * HEAD_DIM
    projection_width = query_width + 2 * key_width
    scale = HEAD_DIM ** (-0.5)
    starts = document_starts[0]
    positions = lax.axis_index("ctx") * rows + jnp.arange(rows, dtype=jnp.int32)
    query_segment = segments(starts, positions)
    cosine, sine = rope_tables(positions, HEAD_DIM)
    block_weights, bias_all, gains_all = (
        lax.all_gather(attention_weights.astype(jnp.bfloat16), "fsdp", axis=0, tiled=True),
        lax.all_gather(projection_bias.astype(jnp.bfloat16), "fsdp", axis=0, tiled=True),
        lax.all_gather(norm_gains.astype(jnp.bfloat16), "fsdp", axis=1, tiled=True),
    )
    w_project = block_weights[:projection_width]
    w_output = block_weights[projection_width:]
    gain_one = gains_all[0].astype(jnp.float32)
    gain_two = gains_all[1].astype(jnp.float32)
    upstream = cotangent[0]
    upstream_all = lax.all_gather(upstream, "fsdp", axis=0, tiled=True)
    hidden_low = hidden_weights.astype(jnp.bfloat16)
    inputs = tokens[0].astype(jnp.float32)
    scale_one = inverse_rms(inputs)
    normed_one = (inputs * scale_one * gain_one).astype(jnp.bfloat16)
    projected = jnp.einsum(
        "td,rd->tr", normed_one, w_project, preferred_element_type=jnp.float32
    ) + bias_all.astype(jnp.float32)
    queries = rotate(
        projected[:, :query_width].reshape(rows, HEADS, HEAD_DIM), cosine, sine
    ).astype(jnp.bfloat16)
    queries = queries.reshape(rows, KV_HEADS, group, HEAD_DIM)
    keys = rotate(
        projected[:, query_width : query_width + key_width].reshape(rows, KV_HEADS, HEAD_DIM),
        cosine,
        sine,
    )
    keys = keys.astype(jnp.bfloat16).reshape(rows, key_width)
    values = projected[:, query_width + key_width :].astype(jnp.bfloat16)

    def allowed(first_key, count):
        key_positions = first_key + jnp.arange(count, dtype=jnp.int32)
        same_document = query_segment[:, None] == segments(starts, key_positions)[None, :]
        return same_document & (key_positions[None, :] <= positions[:, None])

    def masked_scores(key_block, mask):
        count = key_block.shape[0]
        raw = (
            jnp.einsum(
                "tkgd,skd->kgts",
                queries,
                key_block.reshape(count, KV_HEADS, HEAD_DIM),
                preferred_element_type=jnp.float32,
            )
            * scale
        )
        return jnp.where(mask, raw, -jnp.inf)

    initial = (
        jnp.full((KV_HEADS, group, rows), LOWEST, jnp.float32),
        jnp.zeros((KV_HEADS, group, rows), jnp.float32),
        jnp.zeros((KV_HEADS, group, rows, HEAD_DIM), jnp.float32),
    )
    key_block = lax.all_gather(keys, "ctx", axis=0, tiled=True)
    value_block = lax.all_gather(values, "ctx", axis=0, tiled=True)
    count = key_block.shape[0]
    mask = allowed(jnp.int32(0), count)

    def absorb_compute(current):
        top, total, accumulated = current
        scores = masked_scores(key_block, mask)
        new_top = jnp.maximum(top, jnp.max(scores, axis=-1))
        raised = jnp.exp(scores - new_top[..., None])
        mixed_block = jnp.einsum(
            "kgts,skd->kgtd",
            raised.astype(jnp.bfloat16),
            value_block.reshape(count, KV_HEADS, HEAD_DIM),
            preferred_element_type=jnp.float32,
        )
        return (new_top, jnp.sum(raised, axis=-1), mixed_block)

    top, total, accumulated = lax.cond(
        jnp.any(mask), absorb_compute, lambda current: current, initial
    )
    log_total = top + jnp.log(total)
    attention_out = accumulated / total[..., None]
    mixed_low = attention_out.transpose(2, 0, 1, 3).reshape(rows, query_width).astype(jnp.bfloat16)
    branch = jnp.einsum("tf,fd->td", mixed_low, w_output, preferred_element_type=jnp.float32)
    residual = inputs + branch
    scale_two = inverse_rms(residual)
    normed_two = (residual * scale_two * gain_two).astype(jnp.bfloat16)
    normed_all = lax.all_gather(normed_two, "fsdp", axis=0, tiled=True)
    gate_value, up_value, sigmoid_gate, silu_gate, hidden = hidden_values(
        normed_all, hidden_low, width
    )
    back_gate, back_up = hidden_backward(
        upstream_all, hidden_low, width, (gate_value, up_value, sigmoid_gate, silu_gate)
    )
    back_normed_part = jnp.einsum(
        "tf,fd->td", back_gate, hidden_low[:, :width], preferred_element_type=jnp.float32
    ) + jnp.einsum(
        "tf,fd->td", back_up, hidden_low[:, width : 2 * width], preferred_element_type=jnp.float32
    )
    back_normed_two = lax.psum_scatter(
        back_normed_part.astype(jnp.bfloat16), "fsdp", scatter_dimension=0, tiled=True
    ).astype(jnp.float32)
    lifted_part = jnp.dot(hidden, hidden_low[:, 2 * width :], preferred_element_type=jnp.float32)
    lifted = lax.psum_scatter(
        lifted_part.astype(jnp.bfloat16), "fsdp", scatter_dimension=0, tiled=True
    ).astype(jnp.float32)
    output = (residual + lifted).astype(jnp.bfloat16)
    hidden_term = jnp.concatenate(
        [
            jnp.einsum("tf,td->fd", back_gate, normed_all, preferred_element_type=jnp.float32),
            jnp.einsum("tf,td->fd", back_up, normed_all, preferred_element_type=jnp.float32),
            jnp.einsum("tf,td->fd", hidden, upstream_all, preferred_element_type=jnp.float32),
        ],
        axis=1,
    ).astype(jnp.bfloat16)
    back_residual_part, back_gain_two = norm_backward(
        residual, scale_two, gain_two, back_normed_two
    )
    back_residual = upstream.astype(jnp.float32) + back_residual_part
    back_branch = back_residual.astype(jnp.bfloat16)
    back_mixed = jnp.einsum(
        "td,fd->tf", back_branch, w_output, preferred_element_type=jnp.float32
    ).astype(jnp.bfloat16)
    back_mixed = back_mixed.reshape(rows, KV_HEADS, group, HEAD_DIM)
    back_output = jnp.einsum(
        "tf,td->fd", mixed_low, back_branch, preferred_element_type=jnp.float32
    )
    delta = jnp.sum(back_mixed.transpose(1, 2, 0, 3).astype(jnp.float32) * attention_out, axis=-1)
    keys_all, values_all = (
        lax.all_gather(keys, "ctx", axis=0, tiled=True),
        lax.all_gather(values, "ctx", axis=0, tiled=True),
    )
    total_keys = keys_all.shape[0]
    key_span = min(512, total_keys)

    def back_step(back_query, index):
        first_key = index * key_span
        key_block = lax.dynamic_slice_in_dim(keys_all, first_key, key_span, 0)
        value_block = lax.dynamic_slice_in_dim(values_all, first_key, key_span, 0)
        mask = allowed(first_key, key_span)

        def back_compute(current):
            scores = masked_scores(key_block, mask)
            probability = jnp.exp(scores - log_total[..., None])
            back_probability = jnp.einsum(
                "tkgd,skd->kgts",
                back_mixed,
                value_block.reshape(key_span, KV_HEADS, HEAD_DIM),
                preferred_element_type=jnp.float32,
            )
            back_scores = (probability * (back_probability - delta[..., None])).astype(jnp.bfloat16)
            key_heads = key_block.reshape(key_span, KV_HEADS, HEAD_DIM)
            current = (
                current
                + jnp.einsum(
                    "kgts,skd->kgtd", back_scores, key_heads, preferred_element_type=jnp.float32
                )
                * scale
            )
            back_keys = (
                jnp.einsum(
                    "kgts,tkgd->skd", back_scores, queries, preferred_element_type=jnp.float32
                )
                * scale
            )
            back_values = jnp.einsum(
                "kgts,tkgd->skd",
                probability.astype(jnp.bfloat16),
                back_mixed,
                preferred_element_type=jnp.float32,
            )
            return (
                current,
                back_keys.reshape(key_span, key_width),
                back_values.reshape(key_span, key_width),
            )

        def skip(current):
            empty = jnp.zeros((key_span, key_width), jnp.float32)
            return (current, empty, empty)

        back_query, back_keys, back_values = lax.cond(jnp.any(mask), back_compute, skip, back_query)
        return (back_query, (back_keys, back_values))

    back_query, (key_terms, value_terms) = lax.scan(
        back_step,
        jnp.zeros((KV_HEADS, group, rows, HEAD_DIM), jnp.float32),
        jnp.arange(total_keys // key_span, dtype=jnp.int32),
    )
    back_keys_own, back_values_own = (
        lax.psum_scatter(
            key_terms.reshape(total_keys, key_width).astype(jnp.bfloat16),
            "ctx",
            scatter_dimension=0,
            tiled=True,
        ).astype(jnp.float32),
        lax.psum_scatter(
            value_terms.reshape(total_keys, key_width).astype(jnp.bfloat16),
            "ctx",
            scatter_dimension=0,
            tiled=True,
        ).astype(jnp.float32),
    )
    back_query_heads = back_query.transpose(2, 0, 1, 3).reshape(rows, HEADS, HEAD_DIM)
    back_query_pre = unrotate(back_query_heads, cosine, sine).reshape(rows, query_width)
    back_key_pre = unrotate(back_keys_own.reshape(rows, KV_HEADS, HEAD_DIM), cosine, sine).reshape(
        rows, key_width
    )
    back_projected = jnp.concatenate(
        [back_query_pre, back_key_pre, back_values_own], axis=1
    ).astype(jnp.bfloat16)
    back_bias = jnp.sum(back_projected.astype(jnp.float32), axis=0)
    back_normed_one = jnp.einsum(
        "tr,rd->td", back_projected, w_project, preferred_element_type=jnp.float32
    )
    back_project = jnp.einsum(
        "tr,td->rd", back_projected, normed_one, preferred_element_type=jnp.float32
    )
    back_inputs_part, back_gain_one = norm_backward(inputs, scale_one, gain_one, back_normed_one)
    back_inputs = back_residual + back_inputs_part
    attention_term = jnp.concatenate([back_project, back_output], axis=0)
    gain_term = jnp.stack([back_gain_one, back_gain_two])
    attention_shard, bias_shard, gain_shard = (
        lax.psum_scatter(
            attention_term.astype(jnp.bfloat16), "fsdp", scatter_dimension=0, tiled=True
        ).astype(jnp.float32),
        lax.psum_scatter(
            back_bias.astype(jnp.bfloat16), "fsdp", scatter_dimension=0, tiled=True
        ).astype(jnp.float32),
        lax.psum_scatter(
            gain_term.astype(jnp.bfloat16), "fsdp", scatter_dimension=1, tiled=True
        ).astype(jnp.float32),
    )
    attention_shard, bias_shard, gain_shard, hidden_shard = (
        lax.psum_scatter(
            attention_shard.astype(jnp.bfloat16), "ctx", scatter_dimension=0, tiled=True
        ).astype(jnp.float32),
        lax.psum_scatter(
            bias_shard.astype(jnp.bfloat16), "ctx", scatter_dimension=0, tiled=True
        ).astype(jnp.float32),
        lax.psum_scatter(
            gain_shard.astype(jnp.bfloat16), "ctx", scatter_dimension=1, tiled=True
        ).astype(jnp.float32),
        lax.psum_scatter(
            hidden_term, "ctx", scatter_dimension=0, tiled=True
        ).astype(jnp.float32),
    )
    return (output[None], back_inputs[None], attention_shard, bias_shard, gain_shard, hidden_shard)


def solution(mesh):
    placed = (
        P("fsdp", "ctx", None),
        P("fsdp", None),
        P("fsdp", None),
        P("fsdp"),
        P(None, "fsdp"),
        P("fsdp", None),
        P("fsdp", "ctx", None),
    )
    return jax.shard_map(
        per_device,
        mesh=mesh,
        in_specs=placed,
        out_specs=(
            P("fsdp", "ctx", None),
            P("fsdp", "ctx", None),
            P(("fsdp", "ctx"), None),
            P(("fsdp", "ctx")),
            P(None, ("fsdp", "ctx")),
            P(("fsdp", "ctx"), None),
        ),
        check_vma=False,
    )
```

```python
import jax
import jax.numpy as jnp
from jax import lax
from jax.sharding import PartitionSpec as P

HEADS = 12
KV_HEADS = 2
HEAD_DIM = 128


EPSILON = 1e-06
THETA = 10000.0
LOW = jnp.bfloat16
FULL = jnp.float32


def rope_tables(positions, width):
    half = width // 2
    frequency = THETA ** (-(jnp.arange(half, dtype=jnp.float32) * 2.0 / width))
    angle = positions.astype(jnp.float32)[:, None] * frequency[None, :]
    cosine = jnp.concatenate([jnp.cos(angle), jnp.cos(angle)], axis=1)
    sine = jnp.concatenate([jnp.sin(angle), jnp.sin(angle)], axis=1)
    return (cosine, sine)


def rotate(vectors, cosine, sine):
    half = vectors.shape[-1] // 2
    turned = jnp.concatenate([-vectors[..., half:], vectors[..., :half]], axis=-1)
    return vectors * cosine[:, None, :] + turned * sine[:, None, :]


def unrotate(gradient, cosine, sine):
    half = gradient.shape[-1] // 2
    moved = gradient * sine[:, None, :]
    return gradient * cosine[:, None, :] + jnp.concatenate(
        [moved[..., half:], -moved[..., :half]], axis=-1
    )


def segments(starts, positions):
    return jnp.sum((starts[None, :] <= positions[:, None]).astype(jnp.int32), axis=1) - 1


def inverse_rms(values):
    return lax.rsqrt(jnp.mean(values * values, axis=-1, keepdims=True) + EPSILON)


def norm_backward(inputs, scale, gain, back_normed):
    weighted = back_normed * gain
    back_inputs = scale * weighted - inputs * scale * scale * scale * jnp.mean(
        inputs * weighted, axis=-1, keepdims=True
    )
    return (back_inputs, jnp.sum(back_normed * inputs * scale, axis=0))


def matmul(equation, left, right):
    return jnp.einsum(equation, left, right, preferred_element_type=FULL)


class Ring:
    def __init__(self, size):
        self.size = size
        self.chips = size // 2

    def shift(self, block, chips):
        moves = [(i, (i + 2 * chips) % self.size) for i in range(self.size)]
        return lax.ppermute(block, "fsdp", moves)

    def swap(self, block):
        return lax.ppermute(block, "fsdp", [(i, i ^ 1) for i in range(self.size)])

    def gather(self, block):
        own = [block] + [self.shift(block, d) for d in range(1, self.chips)]
        return own + [self.swap(b) for b in own]

    def reduce(self, parts):
        other = self.swap(parts[self.chips :])
        summed = [
            (parts[d].astype(FULL) + other[d].astype(FULL)).astype(LOW) for d in range(self.chips)
        ]
        return [summed[0]] + [self.shift(summed[d], -d) for d in range(1, self.chips)]

    def exchange(self, pieces):
        index = lax.axis_index("fsdp")
        chip, core = index // 2, index % 2
        by_chip = pieces.reshape((self.chips, 2) + pieces.shape[1:])
        mine = lax.dynamic_index_in_dim(by_chip, core, 1, keepdims=False)
        theirs = self.swap(lax.dynamic_index_in_dim(by_chip, 1 - core, 1, keepdims=False))
        pair = jnp.stack([mine, theirs], axis=1)
        got = []
        for d in range(self.chips):
            target = lax.rem(chip + d, self.chips)
            block = lax.dynamic_index_in_dim(pair, target, 0, keepdims=False)
            got.append(self.shift(block, d) if d else block)
        return [g[0] for g in got] + [g[1] for g in got]


def ctx_scatter(pieces):
    count = pieces.shape[0]
    me = lax.axis_index("ctx")
    terms = [lax.dynamic_index_in_dim(pieces, me, 0, keepdims=False)]
    for d in range(1, count):
        moves = [(i, i ^ d) for i in range(count)]
        terms.append(
            lax.ppermute(
                lax.dynamic_index_in_dim(pieces, me ^ d, 0, keepdims=False), "ctx", moves
            )
        )
    return terms


def total_of(terms):
    result = terms[0].astype(FULL)
    for term in terms[1:]:
        result = result + term.astype(FULL)
    return result


def make(ring, contexts):
    def per_device(
        tokens,
        document_starts,
        attention_weights,
        projection_bias,
        norm_gains,
        hidden_weights,
        cotangent,
    ):
        rows = tokens.shape[1]
        width = tokens.shape[2]
        group = HEADS // KV_HEADS
        query_width = HEADS * HEAD_DIM
        key_width = KV_HEADS * HEAD_DIM
        projection_width = query_width + 2 * key_width
        scale = HEAD_DIM ** (-0.5)
        size = ring.size
        me = lax.axis_index("ctx")
        own_rows = attention_weights.shape[0]
        quarter = own_rows // contexts

        starts = document_starts[0]
        positions = me * rows + jnp.arange(rows, dtype=jnp.int32)
        query_segment = segments(starts, positions)
        cosine, sine = rope_tables(positions, HEAD_DIM)

        weight_piece = lax.dynamic_slice_in_dim(attention_weights, me * quarter, quarter, 0)
        block_weights = lax.all_gather(
            weight_piece.astype(LOW), ("fsdp", "ctx"), axis=0, tiled=True
        )
        gain_width = norm_gains.shape[1]
        packed = jnp.concatenate([projection_bias, norm_gains.reshape(-1)]).astype(LOW)
        packed_all = lax.all_gather(packed, "fsdp", axis=0)
        bias_width = projection_bias.shape[0]
        bias_all = packed_all[:, :bias_width].reshape(-1).astype(FULL)
        gain_one = packed_all[:, bias_width : bias_width + gain_width].reshape(-1).astype(FULL)
        gain_two = packed_all[:, bias_width + gain_width :].reshape(-1).astype(FULL)

        upstream = cotangent[0]
        upstream_all = jnp.concatenate(ring.gather(upstream), axis=0)
        tokens_all = jnp.concatenate(ring.gather(tokens[0]), axis=0)
        hidden_low = hidden_weights.astype(LOW)
        gate_rows = hidden_low[:, :width]
        up_rows = hidden_low[:, width : 2 * width]
        down_rows = hidden_low[:, 2 * width :]
        back_hidden = matmul("td,fd->tf", upstream_all, down_rows)
        inputs_all = tokens_all.astype(FULL)
        normed_one_all = (inputs_all * inverse_rms(inputs_all) * gain_one).astype(LOW)

        w_project = block_weights[:projection_width]
        w_output = block_weights[projection_width:]
        inputs = tokens[0].astype(FULL)
        scale_one = inverse_rms(inputs)
        normed_one = (inputs * scale_one * gain_one).astype(LOW)
        projected = matmul("td,rd->tr", normed_one, w_project) + bias_all
        queries = rotate(
            projected[:, :query_width].reshape(rows, HEADS, HEAD_DIM), cosine, sine
        ).astype(LOW)
        queries = queries.reshape(rows, KV_HEADS, group, HEAD_DIM)
        keys = rotate(
            projected[:, query_width : query_width + key_width].reshape(rows, KV_HEADS, HEAD_DIM),
            cosine,
            sine,
        )
        keys = keys.astype(LOW).reshape(rows, key_width)
        values = projected[:, query_width + key_width :].astype(LOW)
        both_all = lax.all_gather(
            jnp.concatenate([keys, values], axis=1), "ctx", axis=0, tiled=True
        )
        count = both_all.shape[0]
        keys_all = both_all[:, :key_width].reshape(count, KV_HEADS, HEAD_DIM)
        values_all = both_all[:, key_width:].reshape(count, KV_HEADS, HEAD_DIM)
        key_positions = jnp.arange(count, dtype=jnp.int32)
        mask = (query_segment[:, None] == segments(starts, key_positions)[None, :]) & (
            key_positions[None, :] <= positions[:, None]
        )
        scores = matmul("tkgd,skd->kgts", queries, keys_all) * scale
        scores = jnp.where(mask, scores, -jnp.inf)
        top = jnp.max(scores, axis=-1, keepdims=True)
        raised = jnp.exp(scores - top)
        probability = raised / jnp.sum(raised, axis=-1, keepdims=True)
        probability_low = probability.astype(LOW)
        attention_out = matmul("kgts,skd->kgtd", probability_low, values_all)
        mixed_low = attention_out.transpose(2, 0, 1, 3).reshape(rows, query_width).astype(LOW)
        residual = inputs + matmul("tf,fd->td", mixed_low, w_output)
        scale_two = inverse_rms(residual)
        normed_two = (residual * scale_two * gain_two).astype(LOW)

        normed_all = jnp.concatenate(ring.gather(normed_two), axis=0)
        gate_value = matmul("td,fd->tf", normed_all, gate_rows)
        up_value = matmul("td,fd->tf", normed_all, up_rows)
        sigmoid_gate = jax.nn.sigmoid(gate_value)
        silu_gate = gate_value * sigmoid_gate
        hidden = (silu_gate * up_value).astype(LOW)
        back_up = (back_hidden * silu_gate).astype(LOW)
        back_gate = (
            back_hidden * up_value * sigmoid_gate * (1.0 + gate_value * (1.0 - sigmoid_gate))
        ).astype(LOW)
        back_normed_part = matmul("tf,fd->td", back_gate, gate_rows) + matmul(
            "tf,fd->td", back_up, up_rows
        )
        back_normed_two = total_of(
            ring.reduce(back_normed_part.astype(LOW).reshape(size, rows, width))
        )
        lifted_part = matmul("tf,fd->td", hidden, down_rows)
        lifted = total_of(ring.reduce(lifted_part.astype(LOW).reshape(size, rows, width)))
        output = (residual + lifted).astype(LOW)
        hidden_term = jnp.concatenate(
            [
                matmul("tf,td->fd", back_gate, normed_all),
                matmul("tf,td->fd", back_up, normed_all),
                matmul("tf,td->fd", hidden, upstream_all),
            ],
            axis=1,
        ).astype(LOW)
        hidden_shard = lax.psum_scatter(
            hidden_term, "ctx", scatter_dimension=0, tiled=True
        ).astype(FULL)

        back_residual_part, back_gain_two = norm_backward(
            residual, scale_two, gain_two, back_normed_two
        )
        back_residual = upstream.astype(FULL) + back_residual_part
        back_branch = back_residual.astype(LOW)
        back_branch_all = jnp.concatenate(ring.gather(back_branch), axis=0)
        back_mixed = matmul("td,fd->tf", back_branch, w_output).astype(LOW)
        back_mixed = back_mixed.reshape(rows, KV_HEADS, group, HEAD_DIM)
        delta = jnp.sum(
            back_mixed.transpose(1, 2, 0, 3).astype(FULL) * attention_out, axis=-1, keepdims=True
        )
        back_probability = matmul("tkgd,skd->kgts", back_mixed, values_all)
        back_scores = (probability * (back_probability - delta)).astype(LOW)
        back_query = matmul("kgts,skd->kgtd", back_scores, keys_all) * scale
        back_keys = matmul("kgts,tkgd->skd", back_scores, queries) * scale
        back_values = matmul("kgts,tkgd->skd", probability_low, back_mixed)
        back_both = jnp.concatenate(
            [back_keys.reshape(count, key_width), back_values.reshape(count, key_width)], axis=1
        ).astype(LOW)
        back_both_own = total_of(ctx_scatter(back_both.reshape(contexts, rows, 2 * key_width)))
        back_query_heads = back_query.transpose(2, 0, 1, 3).reshape(rows, HEADS, HEAD_DIM)
        back_query_pre = unrotate(back_query_heads, cosine, sine).reshape(rows, query_width)
        back_key_pre = unrotate(
            back_both_own[:, :key_width].reshape(rows, KV_HEADS, HEAD_DIM), cosine, sine
        ).reshape(rows, key_width)
        back_projected = jnp.concatenate(
            [back_query_pre, back_key_pre, back_both_own[:, key_width:]], axis=1
        ).astype(LOW)
        back_bias = jnp.sum(back_projected.astype(FULL), axis=0)
        back_normed_one = matmul("tr,rd->td", back_projected, w_project)
        back_inputs_part, back_gain_one = norm_backward(
            inputs, scale_one, gain_one, back_normed_one
        )
        back_inputs = back_residual + back_inputs_part

        def by_owner(block):
            return block.reshape(rows, size, own_rows).transpose(1, 0, 2)

        mixed_pieces = by_owner(
            jnp.concatenate([jnp.zeros((rows, projection_width), LOW), mixed_low], axis=1)
        )
        mixed_columns = jnp.concatenate(ring.exchange(mixed_pieces), axis=0)
        projected_pieces = by_owner(
            jnp.concatenate([back_projected, jnp.zeros((rows, query_width), LOW)], axis=1)
        )
        small = jnp.concatenate(
            [
                back_bias.reshape(size, 1, bias_width),
                jnp.zeros((size, 1, own_rows - bias_width), FULL),
            ],
            axis=2,
        )
        gains_small = jnp.concatenate(
            [
                jnp.stack([back_gain_one, back_gain_two], axis=0)
                .reshape(2, size, gain_width)
                .transpose(1, 0, 2),
                jnp.zeros((size, 2, own_rows - gain_width), FULL),
            ],
            axis=2,
        )
        small = jnp.concatenate([small, gains_small, jnp.zeros((size, 13, own_rows), FULL)], axis=1)
        projected_got = ring.exchange(
            jnp.concatenate([projected_pieces, small.astype(LOW)], axis=1)
        )
        projected_columns = jnp.concatenate([g[:rows] for g in projected_got], axis=0)
        small_sum = total_of([g[rows : rows + 3] for g in projected_got])

        attention_term = (
            matmul("tr,td->rd", projected_columns, normed_one_all)
            + matmul("tr,td->rd", mixed_columns, back_branch_all)
        ).astype(LOW)
        own_bias = bias_width // contexts
        own_gain = gain_width // contexts
        tail = jnp.concatenate(
            [
                small_sum[0, :bias_width].reshape(contexts, 1, own_bias),
                small_sum[1, :gain_width].reshape(contexts, 1, own_gain),
                small_sum[2, :gain_width].reshape(contexts, 1, own_gain),
                jnp.zeros((contexts, 1, width - own_bias - 2 * own_gain), FULL),
            ],
            axis=2,
        )
        tail = jnp.concatenate([tail, jnp.zeros((contexts, 15, width), FULL)], axis=1).astype(LOW)
        shards = total_of(
            ctx_scatter(
                jnp.concatenate([attention_term.reshape(contexts, quarter, width), tail], axis=1)
            )
        )
        attention_shard = shards[:quarter]
        bias_shard = shards[quarter, :own_bias]
        gain_shard = shards[quarter, own_bias : own_bias + 2 * own_gain].reshape(2, own_gain)
        return (
            output[None],
            back_inputs[None],
            attention_shard,
            bias_shard,
            gain_shard,
            hidden_shard,
        )

    return per_device


def solution(mesh):
    placed = (
        P("fsdp", "ctx", None),
        P("fsdp", None),
        P("fsdp", None),
        P("fsdp"),
        P(None, "fsdp"),
        P("fsdp", None),
        P("fsdp", "ctx", None),
    )
    return jax.shard_map(
        make(Ring(mesh.shape["fsdp"]), mesh.shape["ctx"]),
        mesh=mesh,
        in_specs=placed,
        out_specs=(
            P("fsdp", "ctx", None),
            P("fsdp", "ctx", None),
            P(("fsdp", "ctx"), None),
            P(("fsdp", "ctx")),
            P(None, ("fsdp", "ctx")),
            P(("fsdp", "ctx"), None),
        ),
        check_vma=False,
    )
```

```python
import math

import jax
import jax.numpy as jnp
from jax import lax
from jax.experimental import pallas as pl
from jax.experimental.pallas import tpu as pltpu
from jax.sharding import PartitionSpec as P

HEADS = 12
KV_HEADS = 2
HEAD_DIM = 128
GROUP = HEADS // KV_HEADS
QUERY_WIDTH = HEADS * HEAD_DIM
KEY_WIDTH = KV_HEADS * HEAD_DIM
PROJECTION_WIDTH = QUERY_WIDTH + 2 * KEY_WIDTH
SCALE = HEAD_DIM ** (-0.5)
WEIGHT_BLOCK = 512

EPSILON = 1e-06
THETA = 10000.0
LOWEST = -1e30
LOW = jnp.bfloat16
FULL = jnp.float32
MIB = 2**20
COST = 1


def rope_tables(positions, width):
    half = width // 2
    frequency = THETA ** (-(jnp.arange(half, dtype=jnp.float32) * 2.0 / width))
    angle = positions.astype(jnp.float32)[:, None] * frequency[None, :]
    cosine = jnp.concatenate([jnp.cos(angle), jnp.cos(angle)], axis=1)
    sine = jnp.concatenate([jnp.sin(angle), jnp.sin(angle)], axis=1)
    return (cosine, sine)


def turn(vector):
    half = vector.shape[-1] // 2
    return jnp.concatenate([-vector[:, half:], vector[:, :half]], axis=1)


def rotate(vector, cosine, sine):
    return vector * cosine + turn(vector) * sine


def unrotate(gradient, cosine, sine):
    return gradient * cosine - turn(gradient * sine)


def segments(starts, positions):
    return jnp.sum((starts[None, :] <= positions[:, None]).astype(jnp.int32), axis=1) - 1


def inverse_rms(values):
    return lax.rsqrt(jnp.mean(values * values, axis=-1, keepdims=True) + EPSILON)


def norm_backward(inputs, scale, gain, back_normed):
    weighted = back_normed * gain
    return scale * weighted - inputs * (
        scale * scale * scale * jnp.mean(inputs * weighted, axis=-1, keepdims=True)
    )


def dot(left, right, left_dim=1, right_dim=0):
    return lax.dot_general(
        left, right, (((left_dim,), (right_dim,)), ((), ())), preferred_element_type=FULL
    )


def call(
    name, kernel, outs, ins, grid=None, in_specs=None, out_specs=None, scratch=(), flops=0, limit=48
):
    shapes = [jax.ShapeDtypeStruct(shape, kind) for shape, kind in outs]
    whole = pl.BlockSpec(memory_space=pltpu.VMEM)
    moved = sum(x.size * x.dtype.itemsize for x in ins) + sum(
        s.size * s.dtype.itemsize for s in shapes
    )
    options = dict(grid=grid) if grid else {}
    return pl.pallas_call(
        kernel,
        name=name,
        out_shape=shapes,
        in_specs=in_specs or [whole] * len(ins),
        out_specs=out_specs or [whole] * len(outs),
        scratch_shapes=list(scratch),
        compiler_params=pltpu.CompilerParams(vmem_limit_bytes=limit * MIB),
        cost_estimate=pl.CostEstimate(
            flops=flops // COST, bytes_accessed=moved // COST, transcendentals=0
        ),
        **options,
    )(*ins)


def after(value, *others):
    return lax.optimization_barrier((value, *others))[0]


def constant(shape):
    return pl.BlockSpec(shape, lambda *_: (0,) * len(shape))


class Ring:
    def __init__(self, size):
        self.size = size
        self.chips = size // 2

    def send(self, block, chips, cores=0):
        moves = [(i, i ^ (2 * chips + cores)) for i in range(self.size)]
        return lax.ppermute(block, "fsdp", moves)

    def both(self, block):
        pairs = [[i, i + 1] for i in range(0, self.size, 2)]
        return lax.all_gather(block, "fsdp", axis=0, tiled=True, axis_index_groups=pairs)

    def ahead(self, block):
        return [block] + [self.send(block, d) for d in range(1, self.chips)]

    def gather(self, block):
        return [self.both(b) for b in self.ahead(block)]

    def reduce(self, place, own, other):
        summed = add_parts(place, own, self.send(other, 0, 1), self.chips)
        return [summed[0]] + [self.send(summed[d], d) for d in range(1, self.chips)]


def add_parts(place, own, both, count):
    total, width = own.shape
    rows = total // count
    first = both.shape[0] - total

    def kernel(place_ref, own_ref, both_ref, *out_refs):
        for d, out_ref in enumerate(out_refs):
            at = pl.multiple_of((1 - place_ref[2]) * first + d * rows, 16)
            got = both_ref[pl.ds(at, rows), :].astype(FULL)
            out_ref[...] = (own_ref[d * rows : (d + 1) * rows, :].astype(FULL) + got).astype(LOW)

    return call(
        "add_parts",
        kernel,
        [((rows, width), LOW)] * count,
        [place, own, both],
        in_specs=[pl.BlockSpec(memory_space=pltpu.SMEM)]
        + [pl.BlockSpec(memory_space=pltpu.VMEM)] * 2,
        limit=24,
    )


def context_send(blocks, count):
    return [blocks[0]] + [
        lax.ppermute(blocks[d], "ctx", [(i, i ^ d) for i in range(count)]) for d in range(1, count)
    ]


def cast_call(hidden_weights):
    units, width = hidden_weights.shape[0], hidden_weights.shape[1] // 3
    chunk = max(c for c in range(16, 257, 16) if units % c == 0)

    def kernel(w_ref, *out_refs):
        for i, ref in enumerate(out_refs):
            ref[...] = w_ref[:, i * width : (i + 1) * width].astype(LOW)

    return call(
        "cast",
        kernel,
        [((units, width), LOW)] * 3,
        [hidden_weights],
        grid=(units // chunk,),
        in_specs=[pl.BlockSpec((chunk, 3 * width), lambda j: (j, 0))],
        out_specs=[pl.BlockSpec((chunk, width), lambda j: (j, 0))] * 3,
        limit=24,
    )


def back_hidden_call(pairs, down, rows):
    pair_rows, width = pairs[0].shape
    units = down.shape[0]
    chips = len(pairs)
    second = pair_rows // 2

    def kernel(*refs):
        down_ref, e_ref, all_ref = refs[-3:]
        for d in range(chips):

            @pl.when(pl.program_id(0) == d)
            def _():
                all_ref[:rows, :] = refs[d][:rows, :]
                all_ref[rows:, :] = refs[d][second : second + rows, :]

        e_ref[...] = dot(all_ref[...], down_ref[...], 1, 1).astype(LOW)

    return call(
        "back_hidden",
        kernel,
        [((2 * chips * rows, units), LOW), ((2 * chips * rows, width), LOW)],
        [*pairs, down],
        grid=(chips,),
        in_specs=[constant((pair_rows, width))] * chips + [constant((units, width))],
        out_specs=[
            pl.BlockSpec((2 * rows, units), lambda j: (j, 0)),
            pl.BlockSpec((2 * rows, width), lambda j: (j, 0)),
        ],
        flops=4 * chips * rows * width * units,
        limit=32,
    )


def feed_call(d, chips, place, tokens, back_hidden, gate_rows, up_rows, kept):
    pair, width = tokens.shape
    units = gate_rows.shape[0]
    rows = pair // 2

    def kernel(*refs):
        place_ref, tokens_ref, e_ref, gate_ref, up_ref = refs[:5]
        back_ref, all_ref, own_ref, other_ref, sum_ref = refs[-5:]
        normed = tokens_ref[...]
        all_ref[...] = normed
        gate = dot(normed, gate_ref[...], 1, 1)
        up = dot(normed, up_ref[...], 1, 1)
        back = e_ref[...].astype(FULL)
        sigmoid = jax.nn.sigmoid(gate)
        silu = gate * sigmoid
        back_ref[2] = (silu * up).astype(LOW)
        back_ref[1] = (back * silu).astype(LOW)
        back_ref[0] = (back * up * (sigmoid * (1.0 + gate * (1.0 - sigmoid)))).astype(LOW)
        sum_ref[...] = (dot(back_ref[0], gate_ref[...]) + dot(back_ref[1], up_ref[...])).astype(LOW)
        core = place_ref[2]
        own_ref[...] = sum_ref[pl.ds(pl.multiple_of(core * rows, 16), rows), :]
        other_ref[...] = sum_ref[pl.ds(pl.multiple_of((1 - core) * rows, 16), rows), :]

    ins = [place, tokens, back_hidden, gate_rows, up_rows, *kept]
    outs = [
        ((3, chips * pair, units), LOW),
        ((chips * pair, width), LOW),
        ((rows, width), LOW),
        ((rows, width), LOW),
    ]
    return pl.pallas_call(
        kernel,
        name="feed",
        grid=(1,),
        out_shape=[jax.ShapeDtypeStruct(shape, kind) for shape, kind in outs],
        in_specs=[
            pl.BlockSpec(memory_space=pltpu.SMEM),
            constant((pair, width)),
            pl.BlockSpec((pair, units), lambda j: (d, 0)),
        ]
        + [constant((units, width))] * 2
        + [pl.BlockSpec(memory_space=pl.ANY)] * len(kept),
        out_specs=[
            pl.BlockSpec((3, pair, units), lambda j: (0, d, 0)),
            pl.BlockSpec((pair, width), lambda j: (d, 0)),
            constant((rows, width)),
            constant((rows, width)),
        ],
        scratch_shapes=[pltpu.VMEM((pair, width), LOW)],
        input_output_aliases={5 + i: i for i in range(len(kept))},
        compiler_params=pltpu.CompilerParams(vmem_limit_bytes=36 * MIB),
        cost_estimate=pl.CostEstimate(
            flops=8 * pair * width * units // COST,
            bytes_accessed=(4 * units * width + 16 * pair * width) // COST,
            transcendentals=0,
        ),
    )(*ins)


def weight_gradient_call(back, normed_all, upstream_all):
    _, total, units = back.shape
    width = normed_all.shape[1]
    steps = 3
    part = width // steps

    def kernel(back_ref, normed_ref, upstream_ref, out_ref):
        step = pl.program_id(0)

        @pl.when(step < 2 * steps)
        def _():
            out_ref[...] = dot(back_ref[0], normed_ref[...], 0, 0).astype(LOW)

        @pl.when(step >= 2 * steps)
        def _():
            out_ref[...] = dot(back_ref[0], upstream_ref[...], 0, 0).astype(LOW)

    return call(
        "weight_gradient",
        kernel,
        [((units, 3 * width), LOW)],
        [back, normed_all, upstream_all],
        grid=(3 * steps,),
        in_specs=[
            pl.BlockSpec((1, total, units), lambda j: (j // steps, 0, 0)),
            pl.BlockSpec((total, part), lambda j: (0, jnp.where(j < 2 * steps, j % steps, 2))),
            pl.BlockSpec((total, part), lambda j: (0, jnp.maximum(j - 2 * steps, 0))),
        ],
        out_specs=[pl.BlockSpec((units, part), lambda j: (0, j))],
        flops=6 * total * width * units,
        limit=32,
    )[0]


def lifted_call(place, back, down, chips):
    _, total, units = back.shape
    width = down.shape[1]
    rows = total // (2 * chips)

    def kernel(place_ref, z_ref, down_ref, own_ref, other_ref, sum_ref):
        sum_ref[...] = dot(z_ref[0], down_ref[...]).astype(LOW)
        core = place_ref[2]
        own_ref[...] = sum_ref[pl.ds(pl.multiple_of(core * rows, 16), rows), :]
        other_ref[...] = sum_ref[pl.ds(pl.multiple_of((1 - core) * rows, 16), rows), :]

    return call(
        "lifted",
        kernel,
        [((total // 2, width), LOW)] * 2,
        [place, back, down],
        grid=(chips,),
        in_specs=[
            pl.BlockSpec(memory_space=pltpu.SMEM),
            pl.BlockSpec((1, 2 * rows, units), lambda j: (2, j, 0)),
            constant((units, width)),
        ],
        out_specs=[pl.BlockSpec((rows, width), lambda j: (j, 0))] * 2,
        scratch=[pltpu.VMEM((2 * rows, width), LOW)],
        flops=2 * total * width * units,
        limit=32,
    )


def project_call(tokens, gain, weights, bias, cosine, sine):
    rows, width = tokens.shape
    steps = PROJECTION_WIDTH // WEIGHT_BLOCK
    heads = WEIGHT_BLOCK // HEAD_DIM

    def kernel(x_ref, gain_ref, w_ref, bias_ref, cos_ref, sin_ref, q_ref, kv_ref, n_ref):
        step = pl.program_id(0)

        @pl.when(step == 0)
        def _():
            x = x_ref[...].astype(FULL)
            n_ref[...] = (x * inverse_rms(x) * gain_ref[...]).astype(LOW)

        a = dot(n_ref[...], w_ref[...], 1, 1) + bias_ref[...]
        parts = []
        for h in range(heads):
            one = a[:, h * HEAD_DIM : (h + 1) * HEAD_DIM]
            turned = rotate(one, cos_ref[...], sin_ref[...])
            is_value = step * heads + h >= HEADS + KV_HEADS
            parts.append(jnp.where(is_value, one, turned).astype(LOW))

        @pl.when(step < steps - 1)
        def _():
            for h in range(heads):
                q_ref[:, h * HEAD_DIM : (h + 1) * HEAD_DIM] = parts[h]

        @pl.when(step == steps - 1)
        def _():
            for h in range(heads):
                kv_ref[:, h * HEAD_DIM : (h + 1) * HEAD_DIM] = parts[h]

    return call(
        "project",
        kernel,
        [((rows, QUERY_WIDTH), LOW), ((rows, 2 * KEY_WIDTH), LOW)],
        [tokens, gain, weights, bias, cosine, sine],
        grid=(steps,),
        in_specs=[
            constant((rows, width)),
            constant((1, width)),
            pl.BlockSpec((WEIGHT_BLOCK, width), lambda j: (j, 0)),
            pl.BlockSpec((1, WEIGHT_BLOCK), lambda j: (0, j)),
            constant((rows, HEAD_DIM)),
            constant((rows, HEAD_DIM)),
        ],
        out_specs=[
            pl.BlockSpec((rows, WEIGHT_BLOCK), lambda j: (0, jnp.minimum(j, steps - 2))),
            constant((rows, 2 * KEY_WIDTH)),
        ],
        scratch=[pltpu.VMEM((rows, width), LOW)],
        flops=2 * rows * width * PROJECTION_WIDTH,
    )


def stacked(ref, kv_head):
    return jnp.concatenate(
        [
            ref[:, h * HEAD_DIM : (h + 1) * HEAD_DIM]
            for h in range(kv_head * GROUP, (kv_head + 1) * GROUP)
        ],
        axis=0,
    )


def masked_scores(query, key, mask):
    rows = mask.shape[0]
    raw = dot(query, key, 1, 1) * SCALE
    return (raw.reshape(GROUP, rows, -1) + mask[None]).reshape(raw.shape)


def output_weight_specs(width):
    first = PROJECTION_WIDTH // WEIGHT_BLOCK
    return [
        pl.BlockSpec((WEIGHT_BLOCK, width), lambda j, i=i: (first + i, 0))
        for i in range(QUERY_WIDTH // WEIGHT_BLOCK)
    ]


class Pieces:
    def __init__(self, own_rows, size):
        self.own_rows, self.size = own_rows, size
        starts = [f * own_rows // 128 * 128 for f in range(size)]
        self.wide = max(-(-((f + 1) * own_rows) // 128) * 128 - starts[f] for f in range(size))
        self.padded = max(starts) + self.wide

    def start_of(self, owner):
        return owner * self.own_rows // 128 * 128

    def start(self, owner):
        return pl.multiple_of(owner * self.own_rows // 128 * 128, 128)


def owner_at(place_ref, place):
    return (place_ref[1] ^ (place // 2)) * 2 + place % 2


def attend_call(query, kv_blocks, mask, tokens, weights, gain):
    rows, width = tokens.shape
    parts = len(kv_blocks)
    count = rows * parts
    weight_specs = output_weight_specs(width)
    blocks = len(weight_specs)

    def kernel(*refs):
        q_ref = refs[0]
        kv_refs = refs[1 : 1 + parts]
        mask_ref, x_ref, gain_ref = refs[1 + parts : 4 + parts]
        w_refs = refs[4 + parts : 4 + parts + blocks]
        lse_ref, h_ref, n_ref, kv_ref, m_ref = refs[4 + parts + blocks :]
        for i, ref in enumerate(kv_refs):
            kv_ref[pl.ds(i * rows, rows), :] = ref[...]
        for g in range(KV_HEADS):
            key = kv_ref[:, g * HEAD_DIM : (g + 1) * HEAD_DIM]
            value = kv_ref[:, KEY_WIDTH + g * HEAD_DIM : KEY_WIDTH + (g + 1) * HEAD_DIM]
            scores = masked_scores(stacked(q_ref, g), key, mask_ref[...])
            top = jnp.max(scores, axis=-1, keepdims=True)
            raised = jnp.exp(scores - top)
            total = jnp.sum(raised, axis=-1, keepdims=True)
            lse_ref[g] = top + jnp.log(total)
            mixed = dot((raised / total).astype(LOW), value).astype(LOW)
            for i in range(GROUP):
                at = (g * GROUP + i) * HEAD_DIM
                m_ref[:, at : at + HEAD_DIM] = mixed[i * rows : (i + 1) * rows]
        h = x_ref[...].astype(FULL)
        for i, w_ref in enumerate(w_refs):
            at = i * WEIGHT_BLOCK
            h = h + dot(m_ref[:, at : at + WEIGHT_BLOCK], w_ref[...])
        h_ref[...] = h
        n_ref[...] = (h * inverse_rms(h) * gain_ref[...]).astype(LOW)

    full = [constant((rows, QUERY_WIDTH))] + [constant((rows, 2 * KEY_WIDTH))] * parts
    return call(
        "attend",
        kernel,
        [
            ((KV_HEADS, GROUP * rows, 1), FULL),
            ((rows, width), FULL),
            ((rows, width), LOW),
            ((count, 2 * KEY_WIDTH), LOW),
            ((rows, QUERY_WIDTH), LOW),
        ],
        [query, *kv_blocks, mask, tokens, gain] + [weights] * blocks,
        grid=(1,),
        in_specs=full
        + [constant((rows, count)), constant((rows, width)), constant((1, width))]
        + weight_specs,
        out_specs=[
            constant((KV_HEADS, GROUP * rows, 1)),
            constant((rows, width)),
            constant((rows, width)),
            constant((count, 2 * KEY_WIDTH)),
            constant((rows, QUERY_WIDTH)),
        ],
        flops=2 * rows * width * QUERY_WIDTH + 4 * rows * count * QUERY_WIDTH,
    )


def back_attend_call(terms, residual, upstream, gain, weights, query, kv, mask, lse, cosine, sine):
    rows, width = residual.shape
    count = kv.shape[0]
    parts = count // rows
    given = len(terms)
    weight_specs = output_weight_specs(width)
    blocks = len(weight_specs)

    def kernel(*refs):
        term_refs = refs[:given]
        h_ref, c_ref, gain_ref, q_ref, kv_ref, mask_ref, lse_ref, cos_ref, sin_ref = refs[
            given : given + 9
        ]
        w_refs = refs[given + 9 : given + 9 + blocks]
        dh_ref, db_ref, gain_back_ref, da_ref = refs[given + 9 + blocks : given + 13 + blocks]
        kv_back_refs = refs[given + 13 + blocks : given + 13 + blocks + parts]
        dm_ref = refs[-1]
        back = term_refs[0][...].astype(FULL)
        for ref in term_refs[1:]:
            back = back + ref[...].astype(FULL)
        h = h_ref[...]
        scale = inverse_rms(h)
        dh = c_ref[...].astype(FULL) + norm_backward(h, scale, gain_ref[...], back)
        gain_back_ref[...] = jnp.sum(back * h * scale, axis=0, keepdims=True)
        dh_ref[...] = dh
        db = dh.astype(LOW)
        db_ref[...] = db
        for i, w_ref in enumerate(w_refs):
            at = i * WEIGHT_BLOCK
            dm_ref[:, at : at + WEIGHT_BLOCK] = dot(db, w_ref[...], 1, 1).astype(LOW)
        for g in range(KV_HEADS):
            key = kv_ref[:, g * HEAD_DIM : (g + 1) * HEAD_DIM]
            value = kv_ref[:, KEY_WIDTH + g * HEAD_DIM : KEY_WIDTH + (g + 1) * HEAD_DIM]
            q = stacked(q_ref, g)
            dm = stacked(dm_ref, g)
            scores = masked_scores(q, key, mask_ref[...])
            probability = jnp.exp(scores - lse_ref[g])
            low = probability.astype(LOW)
            back_probability = dot(dm, value, 1, 1)
            delta = jnp.sum(low.astype(FULL) * back_probability, axis=-1, keepdims=True)
            back_scores = (probability * (back_probability - delta)).astype(LOW)
            back_query = dot(back_scores, key) * SCALE
            for i in range(GROUP):
                at = (g * GROUP + i) * HEAD_DIM
                da_ref[:, at : at + HEAD_DIM] = unrotate(
                    back_query[i * rows : (i + 1) * rows], cos_ref[...], sin_ref[...]
                ).astype(LOW)
            back_key = (dot(back_scores, q, 0, 0) * SCALE).astype(LOW)
            back_value = dot(low, dm, 0, 0).astype(LOW)
            for i, ref in enumerate(kv_back_refs):
                ref[:, g * HEAD_DIM : (g + 1) * HEAD_DIM] = back_key[i * rows : (i + 1) * rows]
                ref[:, KEY_WIDTH + g * HEAD_DIM : KEY_WIDTH + (g + 1) * HEAD_DIM] = back_value[
                    i * rows : (i + 1) * rows
                ]

    ins = [*terms, residual, upstream, gain, query, kv, mask, lse, cosine, sine]
    outs = [
        ((rows, width), FULL),
        ((rows, width), LOW),
        ((1, width), FULL),
        ((rows, QUERY_WIDTH), LOW),
    ] + [((rows, 2 * KEY_WIDTH), LOW)] * parts
    return call(
        "back_attend",
        kernel,
        outs,
        ins + [weights] * blocks,
        grid=(1,),
        in_specs=[constant(x.shape) for x in ins] + weight_specs,
        out_specs=[constant(shape) for shape, _ in outs],
        scratch=[pltpu.VMEM((rows, QUERY_WIDTH), LOW)],
        flops=2 * rows * width * QUERY_WIDTH + 10 * rows * count * QUERY_WIDTH,
    )


def back_project_call(
    terms, da_query, mixed, weights, tokens, back_residual, gain, gain_back, cosine, sine, pieces,
    bias_width, gain_width,
):
    rows, width = tokens.shape
    given = len(terms)
    owners = pieces.size
    span = 256

    def kernel(*refs):
        term_refs = refs[:given]
        daq_ref, m_ref, w_ref, x_ref, dh_ref, gain_ref, gain_back_ref, cos_ref, sin_ref = refs[
            given : 9 + given
        ]
        dx_ref, piece_ref = refs[9 + given : 11 + given]
        da_ref, small_ref = refs[-2:]
        back = term_refs[0][...].astype(FULL)
        for ref in term_refs[1:]:
            back = back + ref[...].astype(FULL)
        used = PROJECTION_WIDTH + QUERY_WIDTH
        da_ref[:, PROJECTION_WIDTH:used] = m_ref[...]
        if da_ref.shape[1] > used:
            da_ref[:, used:] = jnp.zeros_like(da_ref[:, used:])
        da_ref[:, :QUERY_WIDTH] = daq_ref[...]
        for g in range(KV_HEADS):
            at = QUERY_WIDTH + g * HEAD_DIM
            da_ref[:, at : at + HEAD_DIM] = unrotate(
                back[:, g * HEAD_DIM : (g + 1) * HEAD_DIM], cos_ref[...], sin_ref[...]
            ).astype(LOW)
        da_ref[:, QUERY_WIDTH + KEY_WIDTH : PROJECTION_WIDTH] = back[:, KEY_WIDTH:].astype(LOW)
        da = da_ref[:, :PROJECTION_WIDTH]
        x = x_ref[...].astype(FULL)
        scale = inverse_rms(x)
        back_normed = dot(da, w_ref[...])
        dx_ref[...] = dh_ref[...] + norm_backward(x, scale, gain_ref[...], back_normed)
        small_ref[...] = jnp.zeros_like(small_ref)
        small_ref[0:1, :PROJECTION_WIDTH] = jnp.sum(da.astype(FULL), axis=0, keepdims=True)
        small_ref[1:2, :width] = jnp.sum(back_normed * x * scale, axis=0, keepdims=True)
        small_ref[2:3, :width] = gain_back_ref[...]
        for owner in range(owners):
            start = pieces.start_of(owner)
            piece_ref[owner, :rows, :] = da_ref[:, start : start + pieces.wide]
            piece_ref[owner, rows:, :] = jnp.zeros_like(piece_ref[owner, rows:, :])
            bias_at = owner * bias_width // 128 * 128
            gain_at = owner * gain_width // 128 * 128
            small = jnp.concatenate(
                [
                    small_ref[0:1, bias_at : bias_at + span],
                    small_ref[1:3, gain_at : gain_at + span],
                    jnp.zeros((13, span), FULL),
                ],
                axis=0,
            )
            piece_ref[owner, rows:, :span] = small.astype(LOW)

    ins = [*terms, da_query, mixed]
    more = [tokens, back_residual, gain, gain_back, cosine, sine]
    outs = [((rows, width), FULL)] + [((owners, rows + 16, pieces.wide), LOW)]
    return call(
        "back_project",
        kernel,
        outs,
        [*ins, weights, *more],
        grid=(1,),
        in_specs=[constant(x.shape) for x in ins]
        + [pl.BlockSpec((PROJECTION_WIDTH, width), lambda j: (0, 0))]
        + [constant(x.shape) for x in more],
        out_specs=[constant(shape) for shape, _ in outs],
        scratch=[
            pltpu.VMEM((rows, max(pieces.padded, PROJECTION_WIDTH + QUERY_WIDTH)), LOW),
            pltpu.VMEM((8, PROJECTION_WIDTH + span), FULL),
        ],
        flops=2 * rows * width * PROJECTION_WIDTH,
    )


def normed_call(tokens_all, gain, steps):
    total, width = tokens_all.shape
    rows = total // steps

    def kernel(x_ref, gain_ref, out_ref):
        x = x_ref[...].astype(FULL)
        out_ref[...] = (x * inverse_rms(x) * gain_ref[...]).astype(LOW)

    block = pl.BlockSpec((rows, width), lambda j: (j, 0))
    return call(
        "normed",
        kernel,
        [((total, width), LOW)],
        [tokens_all, gain],
        grid=(steps,),
        in_specs=[block, constant((1, width))],
        out_specs=[block],
        limit=24,
    )[0]


def attention_gradient_call(place, columns, normed_all, db_pairs, pieces, contexts):
    pair, width = db_pairs[0].shape
    rows = pair // 2
    chips = len(db_pairs)
    count = 2 * chips
    quarter = pieces.own_rows // contexts
    total = rows * count
    wide = pieces.wide

    def kernel(*refs):
        place_ref = refs[0]
        columns_ref, n_ref = refs[1:3]
        db_refs = refs[3 : 3 + chips]
        out_refs = refs[3 + chips : 3 + chips + contexts]
        left_ref, right_ref, sum_ref, cut_ref = refs[3 + chips + contexts :]
        owner = place_ref[1] * 2 + place_ref[2]
        start = pieces.start(owner)
        small = jnp.zeros((16, wide), FULL)
        for i in range(count):
            left_ref[pl.ds(i * rows, rows), :] = columns_ref[i, :rows, :]
            small = small + columns_ref[i, rows:, :].astype(FULL)
        for d, ref in enumerate(db_refs):
            at = pl.multiple_of((place_ref[1] ^ d) * pair, 16)
            right_ref[pl.ds(at, pair), :] = ref[...]
        of_project = start + lax.broadcasted_iota(jnp.int32, (wide, width), 0) < PROJECTION_WIDTH
        sum_ref[...] = jnp.where(
            of_project, dot(left_ref[...], n_ref[...], 0, 0), dot(left_ref[...], right_ref[...], 0, 0)
        )
        offset = pl.multiple_of(
            owner * pieces.own_rows - start, math.gcd(pieces.own_rows, 128)
        )
        own = sum_ref[pl.ds(offset, pieces.own_rows), :].astype(LOW)
        for c in range(contexts):
            cut_ref[c] = own[c * quarter : (c + 1) * quarter]
        for d, out_ref in enumerate(out_refs):
            out_ref[:quarter, :] = cut_ref[place_ref[0] ^ d]
            out_ref[quarter:, :] = jnp.zeros_like(out_ref[quarter:, :])
            out_ref[quarter:, :wide] = small.astype(LOW)

    ins = [columns, normed_all, *db_pairs]
    outs = [((quarter + 16, width), LOW)] * contexts
    return call(
        "attention_gradient",
        kernel,
        outs,
        [place, *ins],
        in_specs=[pl.BlockSpec(memory_space=pltpu.SMEM)]
        + [pl.BlockSpec(memory_space=pltpu.VMEM)] * len(ins),
        scratch=[
            pltpu.VMEM((total, wide), LOW),
            pltpu.VMEM((total, width), LOW),
            pltpu.VMEM((wide, width), FULL),
            pltpu.VMEM((contexts, quarter, width), LOW),
        ],
        flops=4 * total * wide * width,
    )


def total_of(terms):
    result = terms[0].astype(FULL)
    for term in terms[1:]:
        result = result + term.astype(FULL)
    return result


def make(ring, contexts):
    def per_device(
        tokens,
        document_starts,
        attention_weights,
        projection_bias,
        norm_gains,
        hidden_weights,
        cotangent,
    ):
        rows, width = tokens.shape[1:]
        chips = ring.chips
        me = lax.axis_index("ctx")
        index = lax.axis_index("fsdp")
        place = jnp.stack([me, index // 2, index % 2]).astype(jnp.int32)
        own_rows = attention_weights.shape[0]
        quarter = own_rows // contexts
        pieces = Pieces(own_rows, ring.size)
        bias_width = projection_bias.shape[0]
        gain_width = norm_gains.shape[1]

        weight_piece = lax.dynamic_slice_in_dim(attention_weights, me * quarter, quarter, 0)
        weights = lax.all_gather(weight_piece.astype(LOW), ("fsdp", "ctx"), axis=0, tiled=True)

        packed = jnp.concatenate([projection_bias, norm_gains.reshape(-1)]).astype(LOW)
        packed = jnp.pad(packed[None], ((0, 15), (0, width - packed.shape[0])))
        upstream = cotangent[0]
        upstream_pairs = ring.gather(jnp.concatenate([upstream, packed], axis=0))
        params = jnp.stack([p.reshape(2, -1, width)[:, rows] for p in upstream_pairs])
        params = params.reshape(ring.size, width)
        owners = jnp.arange(ring.size, dtype=jnp.int32)
        at = owners ^ (index // 2 * 2)
        params = jnp.dot(
            (at[:, None] == owners[None, :]).astype(LOW), params, preferred_element_type=FULL
        )
        bias = params[:, :bias_width].reshape(1, -1)
        gain_one = params[:, bias_width : bias_width + gain_width].reshape(1, -1)
        gain_two = params[:, bias_width + gain_width : bias_width + 2 * gain_width].reshape(1, -1)

        starts = document_starts[0]
        within = jnp.arange(rows, dtype=jnp.int32)
        positions = me * rows + within
        cosine, sine = rope_tables(positions, HEAD_DIM)
        key_positions = jnp.concatenate([(me ^ d) * rows + within for d in range(contexts)])
        mask = jnp.where(
            (segments(starts, positions)[:, None] == segments(starts, key_positions)[None, :])
            & (key_positions[None, :] <= positions[:, None]),
            0.0,
            LOWEST,
        ).astype(FULL)

        gate_rows, up_rows, down_rows = cast_call(hidden_weights)
        back_hidden, upstream_all = back_hidden_call(upstream_pairs, down_rows, rows)
        weights, back_hidden, mask, cosine, sine, bias, gain_one, gain_two = (
            lax.optimization_barrier(
                (weights, back_hidden, mask, cosine, sine, bias, gain_one, gain_two)
            )
        )
        tokens_all = lax.all_gather(after(tokens[0], weights), "fsdp", axis=0, tiled=True)
        query, kv = project_call(tokens[0], gain_one, weights, bias, cosine, sine)
        kv_blocks = context_send([kv] * contexts, contexts)
        lse, residual, normed_two, kv_all, mixed = attend_call(
            query, kv_blocks, mask, tokens[0], weights, gain_two
        )

        kept, back_normed_terms = (), []
        ahead = ring.ahead(normed_two)
        done = ()
        for d in range(chips):
            *kept, own, other = feed_call(
                d, chips, place, ring.both(after(ahead[d], *done)), back_hidden, gate_rows,
                up_rows, kept,
            )
            summed = add_parts(place, own, ring.both(other), 1)[0]
            back_normed_terms.append(ring.send(summed, d) if d else summed)
            done = (summed,)
        back, normed_all = kept
        back = after(back, *done)
        hidden_term = weight_gradient_call(back, normed_all, upstream_all)
        hidden_shard = lax.psum_scatter(
            hidden_term, "ctx", scatter_dimension=0, tiled=True
        ).astype(FULL)
        lifted_parts = lifted_call(place, after(back, hidden_term), down_rows, chips)
        back_normed_terms[0] = after(back_normed_terms[0], lifted_parts[0])

        back_residual, back_branch, back_gain_two, da_query, *kv_back = back_attend_call(
            back_normed_terms, residual, upstream, gain_two, weights, query, kv_all, mask, lse,
            cosine, sine,
        )
        kv_terms = context_send(kv_back, contexts)
        back_inputs, projected_pieces = back_project_call(
            kv_terms, da_query, mixed, weights, tokens[0], back_residual, gain_one,
            back_gain_two, cosine, sine, pieces, bias_width, gain_width,
        )
        columns = lax.all_to_all(projected_pieces, "fsdp", 0, 0, tiled=True)
        branch_pairs = ring.gather(back_branch)
        lifted_parts = [after(part, columns) for part in lifted_parts]
        lifted_terms = ring.reduce(place, *lifted_parts)
        output = (residual + total_of(lifted_terms)).astype(LOW)
        normed_one_all = normed_call(tokens_all, after(gain_one, back_inputs), ring.size)
        attention_terms = attention_gradient_call(
            place, columns, normed_one_all, branch_pairs, pieces, contexts
        )
        shards = total_of(context_send(attention_terms, contexts))
        own_bias = bias_width // contexts
        own_gain = gain_width // contexts
        bias_at = index * bias_width % 128 + me * own_bias
        gain_at = index * gain_width % 128 + me * own_gain
        bias_shard = lax.dynamic_slice(shards, (quarter, bias_at), (1, own_bias))[0]
        gain_shard = lax.dynamic_slice(shards, (quarter + 1, gain_at), (2, own_gain))
        return (
            output[None],
            back_inputs[None],
            shards[:quarter],
            bias_shard,
            gain_shard,
            hidden_shard,
        )

    return per_device


def solution(mesh):
    placed = (
        P("fsdp", "ctx", None),
        P("fsdp", None),
        P("fsdp", None),
        P("fsdp"),
        P(None, "fsdp"),
        P("fsdp", None),
        P("fsdp", "ctx", None),
    )
    return jax.shard_map(
        make(Ring(mesh.shape["fsdp"]), mesh.shape["ctx"]),
        mesh=mesh,
        in_specs=placed,
        out_specs=(
            P("fsdp", "ctx", None),
            P("fsdp", "ctx", None),
            P(("fsdp", "ctx"), None),
            P(("fsdp", "ctx")),
            P(None, ("fsdp", "ctx")),
            P(("fsdp", "ctx"), None),
        ),
        check_vma=False,
    )
```

```python
import math

import jax
import jax.numpy as jnp
from jax import lax
from jax.experimental import pallas as pl
from jax.experimental.pallas import tpu as pltpu
from jax.sharding import PartitionSpec as P

HEADS = 12
KV_HEADS = 2
HEAD_DIM = 128
GROUP = HEADS // KV_HEADS
QUERY_WIDTH = HEADS * HEAD_DIM
KEY_WIDTH = KV_HEADS * HEAD_DIM
PROJECTION_WIDTH = QUERY_WIDTH + 2 * KEY_WIDTH
SCALE = HEAD_DIM ** (-0.5)
WEIGHT_BLOCK = 512

EPSILON = 1e-06
THETA = 10000.0
LOWEST = -1e30
LOW = jnp.bfloat16
FULL = jnp.float32
MIB = 2**20
COST = 1


def rope_tables(positions, width):
    half = width // 2
    frequency = THETA ** (-(jnp.arange(half, dtype=jnp.float32) * 2.0 / width))
    angle = positions.astype(jnp.float32)[:, None] * frequency[None, :]
    cosine = jnp.concatenate([jnp.cos(angle), jnp.cos(angle)], axis=1)
    sine = jnp.concatenate([jnp.sin(angle), jnp.sin(angle)], axis=1)
    return (cosine, sine)


def turn(vector):
    half = vector.shape[-1] // 2
    return jnp.concatenate([-vector[:, half:], vector[:, :half]], axis=1)


def rotate(vector, cosine, sine):
    return vector * cosine + turn(vector) * sine


def unrotate(gradient, cosine, sine):
    return gradient * cosine - turn(gradient * sine)


def segments(starts, positions):
    return jnp.sum((starts[None, :] <= positions[:, None]).astype(jnp.int32), axis=1) - 1


def inverse_rms(values):
    return lax.rsqrt(jnp.mean(values * values, axis=-1, keepdims=True) + EPSILON)


def norm_backward(inputs, scale, gain, back_normed):
    weighted = back_normed * gain
    return scale * weighted - inputs * (
        scale * scale * scale * jnp.mean(inputs * weighted, axis=-1, keepdims=True)
    )


def dot(left, right, left_dim=1, right_dim=0):
    return lax.dot_general(
        left, right, (((left_dim,), (right_dim,)), ((), ())), preferred_element_type=FULL
    )


def call(
    name, kernel, outs, ins, grid=None, in_specs=None, out_specs=None, scratch=(), flops=0, limit=60,
    far=(),
):
    shapes = [
        pltpu.HBM(shape, kind) if i in far else jax.ShapeDtypeStruct(shape, kind)
        for i, (shape, kind) in enumerate(outs)
    ]
    whole = pl.BlockSpec(memory_space=pltpu.VMEM)
    moved = sum(x.size * x.dtype.itemsize for x in ins) + sum(
        math.prod(shape) * jnp.dtype(kind).itemsize for shape, kind in outs
    )
    options = dict(grid=grid) if grid else {}
    return pl.pallas_call(
        kernel,
        name=name,
        out_shape=shapes,
        in_specs=in_specs or [whole] * len(ins),
        out_specs=out_specs or [whole] * len(outs),
        scratch_shapes=list(scratch),
        compiler_params=pltpu.CompilerParams(vmem_limit_bytes=limit * MIB),
        cost_estimate=pl.CostEstimate(
            flops=flops // COST, bytes_accessed=moved // COST, transcendentals=0
        ),
        **options,
    )(*ins)


def after(value, *others):
    return lax.optimization_barrier((value, *others))[0]


def constant(shape):
    return pl.BlockSpec(shape, lambda *_: (0,) * len(shape))


class Ring:
    def __init__(self, size):
        self.size = size
        self.chips = size // 2

    def send(self, block, chips, cores=0, to=None):
        moves = [(i, i ^ (2 * chips + cores)) for i in range(self.size)]
        if to is not None:
            moves = [(i, j) for i, j in moves if j // 2 in to]
        return lax.ppermute(block, "fsdp", moves)

    def both(self, block):
        pairs = [[i, i + 1] for i in range(0, self.size, 2)]
        return lax.all_gather(block, "fsdp", axis=0, tiled=True, axis_index_groups=pairs)

    def ahead(self, block, to=None):
        return [block] + [self.send(block, d, 0, to) for d in range(1, self.chips)]

    def chained(self, block):
        if self.chips != 4:
            return self.ahead(block)
        two = self.send(block, 2)
        return [block, self.send(block, 1), two, self.send(two, 1)]


def add_parts(place, own, both, count):
    total, width = own.shape
    rows = total // count
    first = both.shape[0] - total

    def kernel(place_ref, own_ref, both_ref, *out_refs):
        for d, out_ref in enumerate(out_refs):
            at = pl.multiple_of((1 - place_ref[2]) * first + d * rows, 16)
            got = both_ref[pl.ds(at, rows), :].astype(FULL)
            out_ref[...] = (own_ref[d * rows : (d + 1) * rows, :].astype(FULL) + got).astype(LOW)

    return call(
        "add_parts",
        kernel,
        [((rows, width), LOW)] * count,
        [place, own, both],
        in_specs=[pl.BlockSpec(memory_space=pltpu.SMEM)]
        + [pl.BlockSpec(memory_space=pltpu.VMEM)] * 2,
        limit=24,
        far=range(count),
    )


def context_send(blocks, count):
    return [blocks[0]] + [
        lax.ppermute(blocks[d], "ctx", [(i, i ^ d) for i in range(count)]) for d in range(1, count)
    ]


def cast_call(hidden_weights):
    units, width = hidden_weights.shape[0], hidden_weights.shape[1] // 3
    chunk = max(c for c in range(16, 257, 16) if units % c == 0)

    def kernel(w_ref, *out_refs):
        for i, ref in enumerate(out_refs):
            ref[...] = w_ref[:, i * width : (i + 1) * width].astype(LOW)

    return call(
        "cast",
        kernel,
        [((units, width), LOW)] * 3,
        [hidden_weights],
        grid=(units // chunk,),
        in_specs=[pl.BlockSpec((chunk, 3 * width), lambda j: (j, 0))],
        out_specs=[pl.BlockSpec((chunk, width), lambda j: (j, 0))] * 3,
        limit=24,
    )


def back_hidden_call(pairs, down, rows):
    pair_rows, width = pairs[0].shape
    units = down.shape[0]
    chips = len(pairs)
    second = pair_rows // 2

    def kernel(*refs):
        down_ref, e_ref, all_ref = refs[-3:]
        for d in range(chips):

            @pl.when(pl.program_id(0) == d)
            def _():
                all_ref[:rows, :] = refs[d][:rows, :]
                all_ref[rows:, :] = refs[d][second : second + rows, :]

        e_ref[...] = dot(all_ref[...], down_ref[...], 1, 1).astype(LOW)

    return call(
        "back_hidden",
        kernel,
        [((2 * chips * rows, units), LOW), ((2 * chips * rows, width), LOW)],
        [*pairs, down],
        grid=(chips,),
        in_specs=[constant((pair_rows, width))] * chips + [constant((units, width))],
        out_specs=[
            pl.BlockSpec((2 * rows, units), lambda j: (j, 0)),
            pl.BlockSpec((2 * rows, width), lambda j: (j, 0)),
        ],
        flops=4 * chips * rows * width * units,
        limit=32,
    )


def feed_call(d, chips, place, tokens, back_hidden, gate_rows, up_rows, kept):
    pair, width = tokens.shape
    units = gate_rows.shape[0]
    rows = pair // 2

    def kernel(*refs):
        place_ref, tokens_ref, e_ref, gate_ref, up_ref = refs[:5]
        back_ref, all_ref, own_ref, other_ref, sum_ref = refs[-5:]
        normed = tokens_ref[...]
        all_ref[...] = normed
        gate = dot(normed, gate_ref[...], 1, 1)
        up = dot(normed, up_ref[...], 1, 1)
        back = e_ref[...].astype(FULL)
        sigmoid = jax.nn.sigmoid(gate)
        silu = gate * sigmoid
        back_ref[2] = (silu * up).astype(LOW)
        back_ref[1] = (back * silu).astype(LOW)
        back_ref[0] = (back * up * (sigmoid * (1.0 + gate * (1.0 - sigmoid)))).astype(LOW)
        sum_ref[...] = (dot(back_ref[0], gate_ref[...]) + dot(back_ref[1], up_ref[...])).astype(LOW)
        core = place_ref[2]
        own_ref[...] = sum_ref[pl.ds(pl.multiple_of(core * rows, 16), rows), :]
        other_ref[...] = sum_ref[pl.ds(pl.multiple_of((1 - core) * rows, 16), rows), :]

    ins = [place, tokens, back_hidden, gate_rows, up_rows, *kept]
    outs = [
        ((3, chips * pair, units), LOW),
        ((chips * pair, width), LOW),
        ((rows, width), LOW),
        ((rows, width), LOW),
    ]
    return pl.pallas_call(
        kernel,
        name="feed",
        grid=(1,),
        out_shape=[jax.ShapeDtypeStruct(shape, kind) for shape, kind in outs],
        in_specs=[
            pl.BlockSpec(memory_space=pltpu.SMEM),
            constant((pair, width)),
            pl.BlockSpec((pair, units), lambda j: (d, 0)),
        ]
        + [constant((units, width))] * 2
        + [pl.BlockSpec(memory_space=pl.ANY)] * len(kept),
        out_specs=[
            pl.BlockSpec((3, pair, units), lambda j: (0, d, 0)),
            pl.BlockSpec((pair, width), lambda j: (d, 0)),
            constant((rows, width)),
            constant((rows, width)),
        ],
        scratch_shapes=[pltpu.VMEM((pair, width), LOW)],
        input_output_aliases={5 + i: i for i in range(len(kept))},
        compiler_params=pltpu.CompilerParams(vmem_limit_bytes=36 * MIB),
        cost_estimate=pl.CostEstimate(
            flops=8 * pair * width * units // COST,
            bytes_accessed=(4 * units * width + 16 * pair * width) // COST,
            transcendentals=0,
        ),
    )(*ins)


def weight_gradient_call(back, normed_all, upstream_all):
    _, total, units = back.shape
    width = normed_all.shape[1]
    steps = 3
    part = width // steps

    def kernel(back_ref, normed_ref, upstream_ref, out_ref):
        step = pl.program_id(0)

        @pl.when(step < 2 * steps)
        def _():
            out_ref[...] = dot(back_ref[0], normed_ref[...], 0, 0).astype(LOW)

        @pl.when(step >= 2 * steps)
        def _():
            out_ref[...] = dot(back_ref[0], upstream_ref[...], 0, 0).astype(LOW)

    return call(
        "weight_gradient",
        kernel,
        [((units, 3 * width), LOW)],
        [back, normed_all, upstream_all],
        grid=(3 * steps,),
        in_specs=[
            pl.BlockSpec((1, total, units), lambda j: (j // steps, 0, 0)),
            pl.BlockSpec((total, part), lambda j: (0, jnp.where(j < 2 * steps, j % steps, 2))),
            pl.BlockSpec((total, part), lambda j: (0, jnp.maximum(j - 2 * steps, 0))),
        ],
        out_specs=[pl.BlockSpec((units, part), lambda j: (0, j))],
        flops=6 * total * width * units,
        limit=32,
    )[0]


def lifted_call(place, back, down, chips):
    _, total, units = back.shape
    width = down.shape[1]
    rows = total // (2 * chips)

    def kernel(place_ref, z_ref, down_ref, own_ref, other_ref, sum_ref):
        sum_ref[...] = dot(z_ref[0], down_ref[...]).astype(LOW)
        core = place_ref[2]
        own_ref[...] = sum_ref[pl.ds(pl.multiple_of(core * rows, 16), rows), :]
        other_ref[...] = sum_ref[pl.ds(pl.multiple_of((1 - core) * rows, 16), rows), :]

    return call(
        "lifted",
        kernel,
        [((total // 2, width), LOW)] * 2,
        [place, back, down],
        grid=(chips,),
        in_specs=[
            pl.BlockSpec(memory_space=pltpu.SMEM),
            pl.BlockSpec((1, 2 * rows, units), lambda j: (2, j, 0)),
            constant((units, width)),
        ],
        out_specs=[pl.BlockSpec((rows, width), lambda j: (j, 0))] * 2,
        scratch=[pltpu.VMEM((2 * rows, width), LOW)],
        flops=2 * total * width * units,
        limit=32,
        far=(1,),
    )


def project_call(tokens, gain, weights, bias, cosine, sine):
    rows, width = tokens.shape
    steps = PROJECTION_WIDTH // WEIGHT_BLOCK
    heads = WEIGHT_BLOCK // HEAD_DIM

    def kernel(x_ref, gain_ref, w_ref, bias_ref, cos_ref, sin_ref, q_ref, kv_ref, n_ref):
        step = pl.program_id(0)

        @pl.when(step == 0)
        def _():
            x = x_ref[...].astype(FULL)
            n_ref[...] = (x * inverse_rms(x) * gain_ref[...]).astype(LOW)

        a = dot(n_ref[...], w_ref[...], 1, 1) + bias_ref[...]
        parts = []
        for h in range(heads):
            one = a[:, h * HEAD_DIM : (h + 1) * HEAD_DIM]
            turned = rotate(one, cos_ref[...], sin_ref[...])
            is_value = step * heads + h >= HEADS + KV_HEADS
            parts.append(jnp.where(is_value, one, turned).astype(LOW))

        @pl.when(step < steps - 1)
        def _():
            for h in range(heads):
                q_ref[:, h * HEAD_DIM : (h + 1) * HEAD_DIM] = parts[h]

        @pl.when(step == steps - 1)
        def _():
            for h in range(heads):
                kv_ref[:, h * HEAD_DIM : (h + 1) * HEAD_DIM] = parts[h]

    return call(
        "project",
        kernel,
        [((rows, QUERY_WIDTH), LOW), ((rows, 2 * KEY_WIDTH), LOW)],
        [tokens, gain, weights, bias, cosine, sine],
        grid=(steps,),
        in_specs=[
            constant((rows, width)),
            constant((1, width)),
            pl.BlockSpec((WEIGHT_BLOCK, width), lambda j: (j, 0)),
            pl.BlockSpec((1, WEIGHT_BLOCK), lambda j: (0, j)),
            constant((rows, HEAD_DIM)),
            constant((rows, HEAD_DIM)),
        ],
        out_specs=[
            pl.BlockSpec((rows, WEIGHT_BLOCK), lambda j: (0, jnp.minimum(j, steps - 2))),
            constant((rows, 2 * KEY_WIDTH)),
        ],
        scratch=[pltpu.VMEM((rows, width), LOW)],
        flops=2 * rows * width * PROJECTION_WIDTH,
        far=(1,),
    )


def stacked(ref, kv_head):
    return jnp.concatenate(
        [
            ref[:, h * HEAD_DIM : (h + 1) * HEAD_DIM]
            for h in range(kv_head * GROUP, (kv_head + 1) * GROUP)
        ],
        axis=0,
    )


def masked_scores(query, key, mask):
    rows = mask.shape[0]
    raw = dot(query, key, 1, 1) * SCALE
    return (raw.reshape(GROUP, rows, -1) + mask[None]).reshape(raw.shape)


def output_weight_specs(width):
    first = PROJECTION_WIDTH // WEIGHT_BLOCK
    return [
        pl.BlockSpec((WEIGHT_BLOCK, width), lambda j, i=i: (first + i, 0))
        for i in range(QUERY_WIDTH // WEIGHT_BLOCK)
    ]


class Pieces:
    def __init__(self, own_rows, size):
        self.own_rows, self.size = own_rows, size
        starts = [f * own_rows // 128 * 128 for f in range(size)]
        self.wide = max(-(-((f + 1) * own_rows) // 128) * 128 - starts[f] for f in range(size))
        self.padded = max(starts) + self.wide

    def start_of(self, owner):
        return owner * self.own_rows // 128 * 128

    def start(self, owner):
        return pl.multiple_of(owner * self.own_rows // 128 * 128, 128)


def owner_at(place_ref, place):
    return (place_ref[1] ^ (place // 2)) * 2 + place % 2


def attend_call(query, kv_blocks, mask, tokens, weights, gain):
    rows, width = tokens.shape
    parts = len(kv_blocks)
    count = rows * parts
    weight_specs = output_weight_specs(width)
    blocks = len(weight_specs)

    def kernel(*refs):
        q_ref = refs[0]
        kv_refs = refs[1 : 1 + parts]
        mask_ref, x_ref, gain_ref = refs[1 + parts : 4 + parts]
        w_refs = refs[4 + parts : 4 + parts + blocks]
        lse_ref, h_ref, n_ref, kv_ref, m_ref = refs[4 + parts + blocks :]
        for i, ref in enumerate(kv_refs):
            kv_ref[pl.ds(i * rows, rows), :] = ref[...]
        for g in range(KV_HEADS):
            key = kv_ref[:, g * HEAD_DIM : (g + 1) * HEAD_DIM]
            value = kv_ref[:, KEY_WIDTH + g * HEAD_DIM : KEY_WIDTH + (g + 1) * HEAD_DIM]
            scores = masked_scores(stacked(q_ref, g), key, mask_ref[...])
            top = jnp.max(scores, axis=-1, keepdims=True)
            raised = jnp.exp(scores - top)
            total = jnp.sum(raised, axis=-1, keepdims=True)
            lse_ref[g] = top + jnp.log(total)
            mixed = dot((raised / total).astype(LOW), value).astype(LOW)
            for i in range(GROUP):
                at = (g * GROUP + i) * HEAD_DIM
                m_ref[:, at : at + HEAD_DIM] = mixed[i * rows : (i + 1) * rows]
        h = x_ref[...].astype(FULL)
        for i, w_ref in enumerate(w_refs):
            at = i * WEIGHT_BLOCK
            h = h + dot(m_ref[:, at : at + WEIGHT_BLOCK], w_ref[...])
        h_ref[...] = h
        n_ref[...] = (h * inverse_rms(h) * gain_ref[...]).astype(LOW)

    full = [constant((rows, QUERY_WIDTH))] + [constant((rows, 2 * KEY_WIDTH))] * parts
    return call(
        "attend",
        kernel,
        [
            ((KV_HEADS, GROUP * rows, 1), FULL),
            ((rows, width), FULL),
            ((rows, width), LOW),
            ((count, 2 * KEY_WIDTH), LOW),
            ((rows, QUERY_WIDTH), LOW),
        ],
        [query, *kv_blocks, mask, tokens, gain] + [weights] * blocks,
        grid=(1,),
        in_specs=full
        + [constant((rows, count)), constant((rows, width)), constant((1, width))]
        + weight_specs,
        out_specs=[
            constant((KV_HEADS, GROUP * rows, 1)),
            constant((rows, width)),
            constant((rows, width)),
            constant((count, 2 * KEY_WIDTH)),
            constant((rows, QUERY_WIDTH)),
        ],
        far=(2,),
        flops=2 * rows * width * QUERY_WIDTH + 4 * rows * count * QUERY_WIDTH,
    )


def back_attend_call(terms, residual, upstream, gain, weights, query, kv, mask, lse, cosine, sine):
    rows, width = residual.shape
    count = kv.shape[0]
    parts = count // rows
    given = len(terms)
    weight_specs = output_weight_specs(width)
    blocks = len(weight_specs)

    def kernel(*refs):
        term_refs = refs[:given]
        h_ref, c_ref, gain_ref, q_ref, kv_ref, mask_ref, lse_ref, cos_ref, sin_ref = refs[
            given : given + 9
        ]
        w_refs = refs[given + 9 : given + 9 + blocks]
        dh_ref, db_ref, gain_back_ref, da_ref = refs[given + 9 + blocks : given + 13 + blocks]
        kv_back_refs = refs[given + 13 + blocks : given + 13 + blocks + parts]
        dm_ref = refs[-1]
        back = term_refs[0][...].astype(FULL)
        for ref in term_refs[1:]:
            back = back + ref[...].astype(FULL)
        h = h_ref[...]
        scale = inverse_rms(h)
        dh = c_ref[...].astype(FULL) + norm_backward(h, scale, gain_ref[...], back)
        gain_back_ref[...] = jnp.sum(back * h * scale, axis=0, keepdims=True)
        dh_ref[...] = dh
        db = dh.astype(LOW)
        db_ref[...] = db
        for i, w_ref in enumerate(w_refs):
            at = i * WEIGHT_BLOCK
            dm_ref[:, at : at + WEIGHT_BLOCK] = dot(db, w_ref[...], 1, 1).astype(LOW)
        for g in range(KV_HEADS):
            key = kv_ref[:, g * HEAD_DIM : (g + 1) * HEAD_DIM]
            value = kv_ref[:, KEY_WIDTH + g * HEAD_DIM : KEY_WIDTH + (g + 1) * HEAD_DIM]
            q = stacked(q_ref, g)
            dm = stacked(dm_ref, g)
            scores = masked_scores(q, key, mask_ref[...])
            probability = jnp.exp(scores - lse_ref[g])
            low = probability.astype(LOW)
            back_probability = dot(dm, value, 1, 1)
            delta = jnp.sum(low.astype(FULL) * back_probability, axis=-1, keepdims=True)
            back_scores = (probability * (back_probability - delta)).astype(LOW)
            back_query = dot(back_scores, key) * SCALE
            for i in range(GROUP):
                at = (g * GROUP + i) * HEAD_DIM
                da_ref[:, at : at + HEAD_DIM] = unrotate(
                    back_query[i * rows : (i + 1) * rows], cos_ref[...], sin_ref[...]
                ).astype(LOW)
            back_key = (dot(back_scores, q, 0, 0) * SCALE).astype(LOW)
            back_value = dot(low, dm, 0, 0).astype(LOW)
            for i, ref in enumerate(kv_back_refs):
                ref[:, g * HEAD_DIM : (g + 1) * HEAD_DIM] = back_key[i * rows : (i + 1) * rows]
                ref[:, KEY_WIDTH + g * HEAD_DIM : KEY_WIDTH + (g + 1) * HEAD_DIM] = back_value[
                    i * rows : (i + 1) * rows
                ]

    ins = [*terms, residual, upstream, gain, query, kv, mask, lse, cosine, sine]
    outs = [
        ((rows, width), FULL),
        ((rows, width), LOW),
        ((1, width), FULL),
        ((rows, QUERY_WIDTH), LOW),
    ] + [((rows, 2 * KEY_WIDTH), LOW)] * parts
    return call(
        "back_attend",
        kernel,
        outs,
        ins + [weights] * blocks,
        grid=(1,),
        in_specs=[constant(x.shape) for x in ins] + weight_specs,
        out_specs=[constant(shape) for shape, _ in outs],
        scratch=[pltpu.VMEM((rows, QUERY_WIDTH), LOW)],
        far=[1, *range(4, 4 + parts)],
        flops=2 * rows * width * QUERY_WIDTH + 10 * rows * count * QUERY_WIDTH,
    )


def back_project_call(
    terms, da_query, mixed, weights, tokens, back_residual, gain, gain_back, cosine, sine, pieces,
    bias_width, gain_width,
):
    rows, width = tokens.shape
    given = len(terms)
    owners = pieces.size
    span = 256

    def kernel(*refs):
        term_refs = refs[:given]
        daq_ref, m_ref, w_ref, x_ref, dh_ref, gain_ref, gain_back_ref, cos_ref, sin_ref = refs[
            given : 9 + given
        ]
        dx_ref, piece_ref = refs[9 + given : 11 + given]
        da_ref, small_ref = refs[-2:]
        back = term_refs[0][...].astype(FULL)
        for ref in term_refs[1:]:
            back = back + ref[...].astype(FULL)
        used = PROJECTION_WIDTH + QUERY_WIDTH
        da_ref[:, PROJECTION_WIDTH:used] = m_ref[...]
        if da_ref.shape[1] > used:
            da_ref[:, used:] = jnp.zeros_like(da_ref[:, used:])
        da_ref[:, :QUERY_WIDTH] = daq_ref[...]
        for g in range(KV_HEADS):
            at = QUERY_WIDTH + g * HEAD_DIM
            da_ref[:, at : at + HEAD_DIM] = unrotate(
                back[:, g * HEAD_DIM : (g + 1) * HEAD_DIM], cos_ref[...], sin_ref[...]
            ).astype(LOW)
        da_ref[:, QUERY_WIDTH + KEY_WIDTH : PROJECTION_WIDTH] = back[:, KEY_WIDTH:].astype(LOW)
        da = da_ref[:, :PROJECTION_WIDTH]
        x = x_ref[...].astype(FULL)
        scale = inverse_rms(x)
        back_normed = dot(da, w_ref[...])
        dx_ref[...] = dh_ref[...] + norm_backward(x, scale, gain_ref[...], back_normed)
        small_ref[...] = jnp.zeros_like(small_ref)
        small_ref[0:1, :PROJECTION_WIDTH] = jnp.sum(da.astype(FULL), axis=0, keepdims=True)
        small_ref[1:2, :width] = jnp.sum(back_normed * x * scale, axis=0, keepdims=True)
        small_ref[2:3, :width] = gain_back_ref[...]
        for owner in range(owners):
            start = pieces.start_of(owner)
            piece_ref[owner, :rows, :] = da_ref[:, start : start + pieces.wide]
            piece_ref[owner, rows:, :] = jnp.zeros_like(piece_ref[owner, rows:, :])
            bias_at = owner * bias_width // 128 * 128
            gain_at = owner * gain_width // 128 * 128
            small = jnp.concatenate(
                [
                    small_ref[0:1, bias_at : bias_at + span],
                    small_ref[1:3, gain_at : gain_at + span],
                    jnp.zeros((13, span), FULL),
                ],
                axis=0,
            )
            piece_ref[owner, rows:, :span] = small.astype(LOW)

    ins = [*terms, da_query, mixed]
    more = [tokens, back_residual, gain, gain_back, cosine, sine]
    outs = [((rows, width), FULL)] + [((owners, rows + 16, pieces.wide), LOW)]
    return call(
        "back_project",
        kernel,
        outs,
        [*ins, weights, *more],
        grid=(1,),
        in_specs=[constant(x.shape) for x in ins]
        + [pl.BlockSpec((PROJECTION_WIDTH, width), lambda j: (0, 0))]
        + [constant(x.shape) for x in more],
        out_specs=[constant(shape) for shape, _ in outs],
        scratch=[
            pltpu.VMEM((rows, max(pieces.padded, PROJECTION_WIDTH + QUERY_WIDTH)), LOW),
            pltpu.VMEM((8, PROJECTION_WIDTH + span), FULL),
        ],
        flops=2 * rows * width * PROJECTION_WIDTH,
        far=(1,),
    )


def normed_call(tokens_all, gain, steps):
    total, width = tokens_all.shape
    rows = total // steps

    def kernel(x_ref, gain_ref, out_ref):
        x = x_ref[...].astype(FULL)
        out_ref[...] = (x * inverse_rms(x) * gain_ref[...]).astype(LOW)

    block = pl.BlockSpec((rows, width), lambda j: (j, 0))
    return call(
        "normed",
        kernel,
        [((total, width), LOW)],
        [tokens_all, gain],
        grid=(steps,),
        in_specs=[block, constant((1, width))],
        out_specs=[block],
        limit=24,
    )[0]


def attention_gradient_call(place, columns, normed_all, db_pairs, pieces, contexts):
    pair, width = db_pairs[0].shape
    rows = pair // 2
    chips = len(db_pairs)
    count = 2 * chips
    quarter = pieces.own_rows // contexts
    total = rows * count
    wide = pieces.wide

    def kernel(*refs):
        place_ref = refs[0]
        columns_ref, n_ref = refs[1:3]
        db_refs = refs[3 : 3 + chips]
        out_refs = refs[3 + chips : 3 + chips + contexts]
        left_ref, right_ref, sum_ref, cut_ref = refs[3 + chips + contexts :]
        owner = place_ref[1] * 2 + place_ref[2]
        start = pieces.start(owner)
        small = jnp.zeros((16, wide), FULL)
        for i in range(count):
            left_ref[pl.ds(i * rows, rows), :] = columns_ref[i, :rows, :]
            small = small + columns_ref[i, rows:, :].astype(FULL)
        for d, ref in enumerate(db_refs):
            at = pl.multiple_of((place_ref[1] ^ d) * pair, 16)
            right_ref[pl.ds(at, pair), :] = ref[...]
        of_project = start + lax.broadcasted_iota(jnp.int32, (wide, width), 0) < PROJECTION_WIDTH
        sum_ref[...] = jnp.where(
            of_project, dot(left_ref[...], n_ref[...], 0, 0), dot(left_ref[...], right_ref[...], 0, 0)
        )
        offset = pl.multiple_of(
            owner * pieces.own_rows - start, math.gcd(pieces.own_rows, 128)
        )
        own = sum_ref[pl.ds(offset, pieces.own_rows), :].astype(LOW)
        for c in range(contexts):
            cut_ref[c] = own[c * quarter : (c + 1) * quarter]
        for d, out_ref in enumerate(out_refs):
            out_ref[:quarter, :] = cut_ref[place_ref[0] ^ d]
            out_ref[quarter:, :] = jnp.zeros_like(out_ref[quarter:, :])
            out_ref[quarter:, :wide] = small.astype(LOW)

    ins = [columns, normed_all, *db_pairs]
    outs = [((quarter + 16, width), LOW)] * contexts
    return call(
        "attention_gradient",
        kernel,
        outs,
        [place, *ins],
        in_specs=[pl.BlockSpec(memory_space=pltpu.SMEM)]
        + [pl.BlockSpec(memory_space=pltpu.VMEM)] * len(ins),
        scratch=[
            pltpu.VMEM((total, wide), LOW),
            pltpu.VMEM((total, width), LOW),
            pltpu.VMEM((wide, width), FULL),
            pltpu.VMEM((contexts, quarter, width), LOW),
        ],
        flops=4 * total * wide * width,
        far=range(contexts),
    )


def total_of(terms):
    result = terms[0].astype(FULL)
    for term in terms[1:]:
        result = result + term.astype(FULL)
    return result


def make(ring, contexts):
    def per_device(
        tokens,
        document_starts,
        attention_weights,
        projection_bias,
        norm_gains,
        hidden_weights,
        cotangent,
    ):
        rows, width = tokens.shape[1:]
        chips = ring.chips
        me = lax.axis_index("ctx")
        index = lax.axis_index("fsdp")
        place = jnp.stack([me, index // 2, index % 2]).astype(jnp.int32)
        own_rows = attention_weights.shape[0]
        quarter = own_rows // contexts
        pieces = Pieces(own_rows, ring.size)
        bias_width = projection_bias.shape[0]
        gain_width = norm_gains.shape[1]

        weight_piece = lax.dynamic_slice_in_dim(attention_weights, me * quarter, quarter, 0)
        weights = lax.all_gather(weight_piece.astype(LOW), ("fsdp", "ctx"), axis=0, tiled=True)

        packed = jnp.concatenate([projection_bias, norm_gains.reshape(-1)]).astype(LOW)
        packed = jnp.pad(packed[None], ((0, 15), (0, width - packed.shape[0])))
        upstream = cotangent[0]
        upstream_pairs = [
            ring.both(b) for b in ring.chained(jnp.concatenate([upstream, packed], axis=0))
        ]
        params = jnp.stack([p.reshape(2, -1, width)[:, rows] for p in upstream_pairs])
        params = params.reshape(ring.size, width)
        owners = jnp.arange(ring.size, dtype=jnp.int32)
        at = owners ^ (index // 2 * 2)
        params = jnp.dot(
            (at[:, None] == owners[None, :]).astype(LOW), params, preferred_element_type=FULL
        )
        bias = params[:, :bias_width].reshape(1, -1)
        gain_one = params[:, bias_width : bias_width + gain_width].reshape(1, -1)
        gain_two = params[:, bias_width + gain_width : bias_width + 2 * gain_width].reshape(1, -1)

        starts = document_starts[0]
        within = jnp.arange(rows, dtype=jnp.int32)
        positions = me * rows + within
        cosine, sine = rope_tables(positions, HEAD_DIM)
        key_positions = jnp.concatenate([(me ^ d) * rows + within for d in range(contexts)])
        mask = jnp.where(
            (segments(starts, positions)[:, None] == segments(starts, key_positions)[None, :])
            & (key_positions[None, :] <= positions[:, None]),
            0.0,
            LOWEST,
        ).astype(FULL)

        gate_rows, up_rows, down_rows = cast_call(hidden_weights)
        back_hidden, upstream_all = back_hidden_call(upstream_pairs, down_rows, rows)
        weights, back_hidden, mask, cosine, sine, bias, gain_one, gain_two = (
            lax.optimization_barrier(
                (weights, back_hidden, mask, cosine, sine, bias, gain_one, gain_two)
            )
        )
        tokens_all = lax.all_gather(after(tokens[0], weights), "fsdp", axis=0, tiled=True)
        query, kv = project_call(tokens[0], gain_one, weights, bias, cosine, sine)
        kv_blocks = context_send([kv] * contexts, contexts)
        lse, residual, normed_two, kv_all, mixed = attend_call(
            query, kv_blocks, mask, tokens[0], weights, gain_two
        )

        kept, back_normed_terms = (), []
        ahead = ring.ahead(normed_two)
        done = ()
        for d in range(chips):
            *kept, own, other = feed_call(
                d, chips, place, ring.both(after(ahead[d], *done)), back_hidden, gate_rows,
                up_rows, kept,
            )
            summed = add_parts(place, own, ring.both(other), 1)[0]
            done = (summed, *back_normed_terms[1:][-1:])
            back_normed_terms.append(ring.send(summed, d) if d else summed)
        back, normed_all = kept
        normed_one_all = normed_call(tokens_all, after(gain_one, summed), ring.size)
        back = after(back, *done, normed_one_all)
        hidden_term = weight_gradient_call(back, normed_all, upstream_all)
        hidden_shard = lax.psum_scatter(
            after(hidden_term, back_normed_terms[-1]), "ctx", scatter_dimension=0, tiled=True
        ).astype(FULL)
        back_normed_terms[0] = after(back_normed_terms[0], hidden_term)
        back_residual, back_branch, back_gain_two, da_query, *kv_back = back_attend_call(
            back_normed_terms, residual, upstream, gain_two, weights, query, kv_all, mask, lse,
            cosine, sine,
        )
        kv_terms = context_send(kv_back, contexts)
        branch_ahead = ring.ahead(back_branch)
        back_inputs, projected_pieces = back_project_call(
            kv_terms, da_query, mixed, weights, tokens[0], back_residual, gain_one,
            back_gain_two, cosine, sine, pieces, bias_width, gain_width,
        )
        columns = lax.all_to_all(
            after(projected_pieces, *branch_ahead[1:]), "fsdp", 0, 0, tiled=True
        )
        lifted_own, lifted_other = lifted_call(place, after(back, projected_pieces), down_rows, chips)
        lifted_terms = add_parts(place, lifted_own, ring.send(lifted_other, 0, 1), chips)
        branch_pairs = [ring.both(after(b, lifted_terms[0])) for b in branch_ahead]
        lifted_terms = [ring.send(block, d) if d else block for d, block in enumerate(lifted_terms)]
        output = (residual + total_of(lifted_terms)).astype(LOW)
        attention_terms = attention_gradient_call(
            place, columns, normed_one_all, branch_pairs, pieces, contexts
        )
        attention_terms = context_send(attention_terms, contexts)
        shards = total_of([after(attention_terms[0], output, hidden_shard), *attention_terms[1:]])
        own_bias = bias_width // contexts
        own_gain = gain_width // contexts
        bias_at = index * bias_width % 128 + me * own_bias
        gain_at = index * gain_width % 128 + me * own_gain
        bias_shard = lax.dynamic_slice(shards, (quarter, bias_at), (1, own_bias))[0]
        gain_shard = lax.dynamic_slice(shards, (quarter + 1, gain_at), (2, own_gain))
        return (
            output[None],
            back_inputs[None],
            shards[:quarter],
            bias_shard,
            gain_shard,
            hidden_shard,
        )

    return per_device


def solution(mesh):
    placed = (
        P("fsdp", "ctx", None),
        P("fsdp", None),
        P("fsdp", None),
        P("fsdp"),
        P(None, "fsdp"),
        P("fsdp", None),
        P("fsdp", "ctx", None),
    )
    return jax.shard_map(
        make(Ring(mesh.shape["fsdp"]), mesh.shape["ctx"]),
        mesh=mesh,
        in_specs=placed,
        out_specs=(
            P("fsdp", "ctx", None),
            P("fsdp", "ctx", None),
            P(("fsdp", "ctx"), None),
            P(("fsdp", "ctx")),
            P(None, ("fsdp", "ctx")),
            P(("fsdp", "ctx"), None),
        ),
        check_vma=False,
    )
```

```python
import math

import jax
import jax.numpy as jnp
from jax import lax
from jax.experimental import pallas as pl
from jax.experimental.pallas import tpu as pltpu
from jax.sharding import PartitionSpec as P

HEADS = 12
KV_HEADS = 2
HEAD_DIM = 128
GROUP = HEADS // KV_HEADS
QUERY_WIDTH = HEADS * HEAD_DIM
KEY_WIDTH = KV_HEADS * HEAD_DIM
PROJECTION_WIDTH = QUERY_WIDTH + 2 * KEY_WIDTH
SCALE = HEAD_DIM ** (-0.5)
WEIGHT_BLOCK = 512

EPSILON = 1e-06
THETA = 10000.0
LOWEST = -1e30
LOW = jnp.bfloat16
FULL = jnp.float32
MIB = 2**20
COST = 1


def rope_tables(positions, width):
    half = width // 2
    frequency = THETA ** (-(jnp.arange(half, dtype=jnp.float32) * 2.0 / width))
    angle = positions.astype(jnp.float32)[:, None] * frequency[None, :]
    cosine = jnp.concatenate([jnp.cos(angle), jnp.cos(angle)], axis=1)
    sine = jnp.concatenate([jnp.sin(angle), jnp.sin(angle)], axis=1)
    return (cosine, sine)


def turn(vector):
    half = vector.shape[-1] // 2
    return jnp.concatenate([-vector[:, half:], vector[:, :half]], axis=1)


def rotate(vector, cosine, sine):
    return vector * cosine + turn(vector) * sine


def unrotate(gradient, cosine, sine):
    return gradient * cosine - turn(gradient * sine)


def segments(starts, positions):
    return jnp.sum((starts[None, :] <= positions[:, None]).astype(jnp.int32), axis=1) - 1


def inverse_rms(values):
    return lax.rsqrt(jnp.mean(values * values, axis=-1, keepdims=True) + EPSILON)


def norm_backward(inputs, scale, gain, back_normed):
    weighted = back_normed * gain
    return scale * weighted - inputs * (
        scale * scale * scale * jnp.mean(inputs * weighted, axis=-1, keepdims=True)
    )


def dot(left, right, left_dim=1, right_dim=0):
    return lax.dot_general(
        left, right, (((left_dim,), (right_dim,)), ((), ())), preferred_element_type=FULL
    )


def call(
    name, kernel, outs, ins, grid=None, in_specs=None, out_specs=None, scratch=(), flops=0, limit=60,
    far=(),
):
    shapes = [
        pltpu.HBM(shape, kind) if i in far else jax.ShapeDtypeStruct(shape, kind)
        for i, (shape, kind) in enumerate(outs)
    ]
    whole = pl.BlockSpec(memory_space=pltpu.VMEM)
    moved = sum(x.size * x.dtype.itemsize for x in ins) + sum(
        math.prod(shape) * jnp.dtype(kind).itemsize for shape, kind in outs
    )
    options = dict(grid=grid) if grid else {}
    return pl.pallas_call(
        kernel,
        name=name,
        out_shape=shapes,
        in_specs=in_specs or [whole] * len(ins),
        out_specs=out_specs or [whole] * len(outs),
        scratch_shapes=list(scratch),
        compiler_params=pltpu.CompilerParams(vmem_limit_bytes=limit * MIB),
        cost_estimate=pl.CostEstimate(
            flops=flops // COST, bytes_accessed=moved // COST, transcendentals=0
        ),
        **options,
    )(*ins)


def after(value, *others):
    return lax.optimization_barrier((value, *others))[0]


def constant(shape):
    return pl.BlockSpec(shape, lambda *_: (0,) * len(shape))


class Ring:
    def __init__(self, size):
        self.size = size
        self.chips = size // 2

    def send(self, block, chips, cores=0, to=None):
        moves = [(i, i ^ (2 * chips + cores)) for i in range(self.size)]
        if to is not None:
            moves = [(i, j) for i, j in moves if j // 2 in to]
        return lax.ppermute(block, "fsdp", moves)

    def both(self, block):
        pairs = [[i, i + 1] for i in range(0, self.size, 2)]
        return lax.all_gather(block, "fsdp", axis=0, tiled=True, axis_index_groups=pairs)

    def ahead(self, block, to=None):
        return [block] + [self.send(block, d, 0, to) for d in range(1, self.chips)]

    def chained(self, block):
        if self.chips != 4:
            return self.ahead(block)
        two = self.send(block, 2)
        return [block, self.send(block, 1), two, self.send(two, 1)]


def add_parts(place, own, both, count):
    total, width = own.shape
    rows = total // count
    first = both.shape[0] - total

    def kernel(place_ref, own_ref, both_ref, *out_refs):
        for d, out_ref in enumerate(out_refs):
            at = pl.multiple_of((1 - place_ref[2]) * first + d * rows, 16)
            got = both_ref[pl.ds(at, rows), :].astype(FULL)
            out_ref[...] = (own_ref[d * rows : (d + 1) * rows, :].astype(FULL) + got).astype(LOW)

    return call(
        "add_parts",
        kernel,
        [((rows, width), LOW)] * count,
        [place, own, both],
        in_specs=[pl.BlockSpec(memory_space=pltpu.SMEM)]
        + [pl.BlockSpec(memory_space=pltpu.VMEM)] * 2,
        limit=24,
        far=range(count),
    )


def context_send(blocks, count):
    return [blocks[0]] + [
        lax.ppermute(blocks[d], "ctx", [(i, i ^ d) for i in range(count)]) for d in range(1, count)
    ]


def cast_call(hidden_weights):
    units, width = hidden_weights.shape[0], hidden_weights.shape[1] // 3
    chunk = max(c for c in range(16, 257, 16) if units % c == 0)

    def kernel(w_ref, *out_refs):
        for i, ref in enumerate(out_refs):
            ref[...] = w_ref[:, i * width : (i + 1) * width].astype(LOW)

    return call(
        "cast",
        kernel,
        [((units, width), LOW)] * 3,
        [hidden_weights],
        grid=(units // chunk,),
        in_specs=[pl.BlockSpec((chunk, 3 * width), lambda j: (j, 0))],
        out_specs=[pl.BlockSpec((chunk, width), lambda j: (j, 0))] * 3,
        limit=24,
    )


def back_hidden_call(pairs, down, rows):
    pair_rows, width = pairs[0].shape
    units = down.shape[0]
    chips = len(pairs)
    second = pair_rows // 2

    def kernel(*refs):
        down_ref, e_ref, all_ref = refs[-3:]
        for d in range(chips):

            @pl.when(pl.program_id(0) == d)
            def _():
                all_ref[:rows, :] = refs[d][:rows, :]
                all_ref[rows:, :] = refs[d][second : second + rows, :]

        e_ref[...] = dot(all_ref[...], down_ref[...], 1, 1).astype(LOW)

    return call(
        "back_hidden",
        kernel,
        [((2 * chips * rows, units), LOW), ((2 * chips * rows, width), LOW)],
        [*pairs, down],
        grid=(chips,),
        in_specs=[constant((pair_rows, width))] * chips + [constant((units, width))],
        out_specs=[
            pl.BlockSpec((2 * rows, units), lambda j: (j, 0)),
            pl.BlockSpec((2 * rows, width), lambda j: (j, 0)),
        ],
        flops=4 * chips * rows * width * units,
        limit=32,
    )


def feed_call(d, chips, place, tokens, back_hidden, gate_rows, up_rows, kept):
    pair, width = tokens.shape
    units = gate_rows.shape[0]
    rows = pair // 2

    def kernel(*refs):
        place_ref, tokens_ref, e_ref, gate_ref, up_ref = refs[:5]
        back_ref, all_ref, own_ref, other_ref, sum_ref = refs[-5:]
        normed = tokens_ref[...]
        all_ref[...] = normed
        gate = dot(normed, gate_ref[...], 1, 1)
        up = dot(normed, up_ref[...], 1, 1)
        back = e_ref[...].astype(FULL)
        sigmoid = jax.nn.sigmoid(gate)
        silu = gate * sigmoid
        back_ref[2] = (silu * up).astype(LOW)
        back_ref[1] = (back * silu).astype(LOW)
        back_ref[0] = (back * up * (sigmoid * (1.0 + gate * (1.0 - sigmoid)))).astype(LOW)
        sum_ref[...] = (dot(back_ref[0], gate_ref[...]) + dot(back_ref[1], up_ref[...])).astype(LOW)
        core = place_ref[2]
        own_ref[...] = sum_ref[pl.ds(pl.multiple_of(core * rows, 16), rows), :]
        other_ref[...] = sum_ref[pl.ds(pl.multiple_of((1 - core) * rows, 16), rows), :]

    ins = [place, tokens, back_hidden, gate_rows, up_rows, *kept]
    outs = [
        ((3, chips * pair, units), LOW),
        ((chips * pair, width), LOW),
        ((rows, width), LOW),
        ((rows, width), LOW),
    ]
    return pl.pallas_call(
        kernel,
        name="feed",
        grid=(1,),
        out_shape=[jax.ShapeDtypeStruct(shape, kind) for shape, kind in outs],
        in_specs=[
            pl.BlockSpec(memory_space=pltpu.SMEM),
            constant((pair, width)),
            pl.BlockSpec((pair, units), lambda j: (d, 0)),
        ]
        + [constant((units, width))] * 2
        + [pl.BlockSpec(memory_space=pl.ANY)] * len(kept),
        out_specs=[
            pl.BlockSpec((3, pair, units), lambda j: (0, d, 0)),
            pl.BlockSpec((pair, width), lambda j: (d, 0)),
            constant((rows, width)),
            constant((rows, width)),
        ],
        scratch_shapes=[pltpu.VMEM((pair, width), LOW)],
        input_output_aliases={5 + i: i for i in range(len(kept))},
        compiler_params=pltpu.CompilerParams(vmem_limit_bytes=36 * MIB),
        cost_estimate=pl.CostEstimate(
            flops=8 * pair * width * units // COST,
            bytes_accessed=(4 * units * width + 16 * pair * width) // COST,
            transcendentals=0,
        ),
    )(*ins)


def weight_gradient_call(back, normed_all, upstream_all):
    _, total, units = back.shape
    width = normed_all.shape[1]
    steps = 1
    part = width // steps

    def kernel(back_ref, normed_ref, upstream_ref, out_ref):
        step = pl.program_id(0)

        @pl.when(step < 2 * steps)
        def _():
            out_ref[...] = dot(back_ref[0], normed_ref[...], 0, 0).astype(LOW)

        @pl.when(step >= 2 * steps)
        def _():
            out_ref[...] = dot(back_ref[0], upstream_ref[...], 0, 0).astype(LOW)

    return call(
        "weight_gradient",
        kernel,
        [((units, 3 * width), LOW)],
        [back, normed_all, upstream_all],
        grid=(3 * steps,),
        in_specs=[
            pl.BlockSpec((1, total, units), lambda j: (j // steps, 0, 0)),
            pl.BlockSpec((total, part), lambda j: (0, jnp.where(j < 2 * steps, j % steps, steps - 1))),
            pl.BlockSpec((total, part), lambda j: (0, jnp.maximum(j - 2 * steps, 0))),
        ],
        out_specs=[pl.BlockSpec((units, part), lambda j: (0, j))],
        flops=6 * total * width * units,
        limit=32,
    )[0]


def lifted_call(place, back, down, chips):
    _, total, units = back.shape
    width = down.shape[1]
    rows = total // (2 * chips)

    def kernel(place_ref, z_ref, down_ref, own_ref, other_ref, sum_ref):
        sum_ref[...] = dot(z_ref[0], down_ref[...]).astype(LOW)
        core = place_ref[2]
        own_ref[...] = sum_ref[pl.ds(pl.multiple_of(core * rows, 16), rows), :]
        other_ref[...] = sum_ref[pl.ds(pl.multiple_of((1 - core) * rows, 16), rows), :]

    return call(
        "lifted",
        kernel,
        [((total // 2, width), LOW)] * 2,
        [place, back, down],
        grid=(chips,),
        in_specs=[
            pl.BlockSpec(memory_space=pltpu.SMEM),
            pl.BlockSpec((1, 2 * rows, units), lambda j: (2, j, 0)),
            constant((units, width)),
        ],
        out_specs=[pl.BlockSpec((rows, width), lambda j: (j, 0))] * 2,
        scratch=[pltpu.VMEM((2 * rows, width), LOW)],
        flops=2 * total * width * units,
        limit=32,
        far=(1,),
    )


def project_call(tokens, gain, weights, bias, cosine, sine):
    rows, width = tokens.shape
    steps = PROJECTION_WIDTH // WEIGHT_BLOCK
    heads = WEIGHT_BLOCK // HEAD_DIM

    def kernel(x_ref, gain_ref, w_ref, bias_ref, cos_ref, sin_ref, q_ref, kv_ref, n_ref):
        step = pl.program_id(0)

        @pl.when(step == 0)
        def _():
            x = x_ref[...].astype(FULL)
            n_ref[...] = (x * inverse_rms(x) * gain_ref[...]).astype(LOW)

        a = dot(n_ref[...], w_ref[...], 1, 1) + bias_ref[...]
        parts = []
        for h in range(heads):
            one = a[:, h * HEAD_DIM : (h + 1) * HEAD_DIM]
            turned = rotate(one, cos_ref[...], sin_ref[...])
            is_value = step * heads + h >= HEADS + KV_HEADS
            parts.append(jnp.where(is_value, one, turned).astype(LOW))

        @pl.when(step < steps - 1)
        def _():
            for h in range(heads):
                q_ref[:, h * HEAD_DIM : (h + 1) * HEAD_DIM] = parts[h]

        @pl.when(step == steps - 1)
        def _():
            for h in range(heads):
                kv_ref[:, h * HEAD_DIM : (h + 1) * HEAD_DIM] = parts[h]

    return call(
        "project",
        kernel,
        [((rows, QUERY_WIDTH), LOW), ((rows, 2 * KEY_WIDTH), LOW)],
        [tokens, gain, weights, bias, cosine, sine],
        grid=(steps,),
        in_specs=[
            constant((rows, width)),
            constant((1, width)),
            pl.BlockSpec((WEIGHT_BLOCK, width), lambda j: (j, 0)),
            pl.BlockSpec((1, WEIGHT_BLOCK), lambda j: (0, j)),
            constant((rows, HEAD_DIM)),
            constant((rows, HEAD_DIM)),
        ],
        out_specs=[
            pl.BlockSpec((rows, WEIGHT_BLOCK), lambda j: (0, jnp.minimum(j, steps - 2))),
            constant((rows, 2 * KEY_WIDTH)),
        ],
        scratch=[pltpu.VMEM((rows, width), LOW)],
        flops=2 * rows * width * PROJECTION_WIDTH,
        far=(1,),
    )


def stacked(ref, kv_head):
    return jnp.concatenate(
        [
            ref[:, h * HEAD_DIM : (h + 1) * HEAD_DIM]
            for h in range(kv_head * GROUP, (kv_head + 1) * GROUP)
        ],
        axis=0,
    )


def masked_scores(query, key, mask):
    rows = mask.shape[0]
    raw = dot(query, key, 1, 1) * SCALE
    return (raw.reshape(GROUP, rows, -1) + mask[None]).reshape(raw.shape)


def output_weight_specs(width):
    first = PROJECTION_WIDTH // WEIGHT_BLOCK
    return [
        pl.BlockSpec((WEIGHT_BLOCK, width), lambda j, i=i: (first + i, 0))
        for i in range(QUERY_WIDTH // WEIGHT_BLOCK)
    ]


class Pieces:
    def __init__(self, own_rows, size):
        self.own_rows, self.size = own_rows, size
        starts = [f * own_rows // 128 * 128 for f in range(size)]
        self.wide = max(-(-((f + 1) * own_rows) // 128) * 128 - starts[f] for f in range(size))
        self.padded = max(starts) + self.wide

    def start_of(self, owner):
        return owner * self.own_rows // 128 * 128

    def start(self, owner):
        return pl.multiple_of(owner * self.own_rows // 128 * 128, 128)


def owner_at(place_ref, place):
    return (place_ref[1] ^ (place // 2)) * 2 + place % 2


def attend_call(query, kv_blocks, mask, tokens, weights, gain):
    rows, width = tokens.shape
    parts = len(kv_blocks)
    count = rows * parts
    weight_specs = output_weight_specs(width)
    blocks = len(weight_specs)

    def kernel(*refs):
        q_ref = refs[0]
        kv_refs = refs[1 : 1 + parts]
        mask_ref, x_ref, gain_ref = refs[1 + parts : 4 + parts]
        w_refs = refs[4 + parts : 4 + parts + blocks]
        lse_ref, h_ref, n_ref, kv_ref, m_ref = refs[4 + parts + blocks :]
        for i, ref in enumerate(kv_refs):
            kv_ref[pl.ds(i * rows, rows), :] = ref[...]
        for g in range(KV_HEADS):
            key = kv_ref[:, g * HEAD_DIM : (g + 1) * HEAD_DIM]
            value = kv_ref[:, KEY_WIDTH + g * HEAD_DIM : KEY_WIDTH + (g + 1) * HEAD_DIM]
            scores = masked_scores(stacked(q_ref, g), key, mask_ref[...])
            top = jnp.max(scores, axis=-1, keepdims=True)
            raised = jnp.exp(scores - top)
            total = jnp.sum(raised, axis=-1, keepdims=True)
            lse_ref[g] = top + jnp.log(total)
            mixed = dot((raised / total).astype(LOW), value).astype(LOW)
            for i in range(GROUP):
                at = (g * GROUP + i) * HEAD_DIM
                m_ref[:, at : at + HEAD_DIM] = mixed[i * rows : (i + 1) * rows]
        h = x_ref[...].astype(FULL)
        for i, w_ref in enumerate(w_refs):
            at = i * WEIGHT_BLOCK
            h = h + dot(m_ref[:, at : at + WEIGHT_BLOCK], w_ref[...])
        h_ref[...] = h
        n_ref[...] = (h * inverse_rms(h) * gain_ref[...]).astype(LOW)

    full = [constant((rows, QUERY_WIDTH))] + [constant((rows, 2 * KEY_WIDTH))] * parts
    return call(
        "attend",
        kernel,
        [
            ((KV_HEADS, GROUP * rows, 1), FULL),
            ((rows, width), FULL),
            ((rows, width), LOW),
            ((count, 2 * KEY_WIDTH), LOW),
            ((rows, QUERY_WIDTH), LOW),
        ],
        [query, *kv_blocks, mask, tokens, gain] + [weights] * blocks,
        grid=(1,),
        in_specs=full
        + [constant((rows, count)), constant((rows, width)), constant((1, width))]
        + weight_specs,
        out_specs=[
            constant((KV_HEADS, GROUP * rows, 1)),
            constant((rows, width)),
            constant((rows, width)),
            constant((count, 2 * KEY_WIDTH)),
            constant((rows, QUERY_WIDTH)),
        ],
        far=(2,),
        flops=2 * rows * width * QUERY_WIDTH + 4 * rows * count * QUERY_WIDTH,
    )


def back_attend_call(terms, residual, upstream, gain, weights, query, kv, mask, lse, cosine, sine):
    rows, width = residual.shape
    count = kv.shape[0]
    parts = count // rows
    given = len(terms)
    weight_specs = output_weight_specs(width)
    blocks = len(weight_specs)

    def kernel(*refs):
        term_refs = refs[:given]
        h_ref, c_ref, gain_ref, q_ref, kv_ref, mask_ref, lse_ref, cos_ref, sin_ref = refs[
            given : given + 9
        ]
        w_refs = refs[given + 9 : given + 9 + blocks]
        dh_ref, db_ref, gain_back_ref, da_ref = refs[given + 9 + blocks : given + 13 + blocks]
        kv_back_refs = refs[given + 13 + blocks : given + 13 + blocks + parts]
        dm_ref = refs[-1]
        back = term_refs[0][...].astype(FULL)
        for ref in term_refs[1:]:
            back = back + ref[...].astype(FULL)
        h = h_ref[...]
        scale = inverse_rms(h)
        dh = c_ref[...].astype(FULL) + norm_backward(h, scale, gain_ref[...], back)
        gain_back_ref[...] = jnp.sum(back * h * scale, axis=0, keepdims=True)
        dh_ref[...] = dh
        db = dh.astype(LOW)
        db_ref[...] = db
        for i, w_ref in enumerate(w_refs):
            at = i * WEIGHT_BLOCK
            dm_ref[:, at : at + WEIGHT_BLOCK] = dot(db, w_ref[...], 1, 1).astype(LOW)
        for g in range(KV_HEADS):
            key = kv_ref[:, g * HEAD_DIM : (g + 1) * HEAD_DIM]
            value = kv_ref[:, KEY_WIDTH + g * HEAD_DIM : KEY_WIDTH + (g + 1) * HEAD_DIM]
            q = stacked(q_ref, g)
            dm = stacked(dm_ref, g)
            scores = masked_scores(q, key, mask_ref[...])
            probability = jnp.exp(scores - lse_ref[g])
            low = probability.astype(LOW)
            back_probability = dot(dm, value, 1, 1)
            delta = jnp.sum(low.astype(FULL) * back_probability, axis=-1, keepdims=True)
            back_scores = (probability * (back_probability - delta)).astype(LOW)
            back_query = dot(back_scores, key) * SCALE
            for i in range(GROUP):
                at = (g * GROUP + i) * HEAD_DIM
                da_ref[:, at : at + HEAD_DIM] = unrotate(
                    back_query[i * rows : (i + 1) * rows], cos_ref[...], sin_ref[...]
                ).astype(LOW)
            back_key = (dot(back_scores, q, 0, 0) * SCALE).astype(LOW)
            back_value = dot(low, dm, 0, 0).astype(LOW)
            for i, ref in enumerate(kv_back_refs):
                ref[:, g * HEAD_DIM : (g + 1) * HEAD_DIM] = back_key[i * rows : (i + 1) * rows]
                ref[:, KEY_WIDTH + g * HEAD_DIM : KEY_WIDTH + (g + 1) * HEAD_DIM] = back_value[
                    i * rows : (i + 1) * rows
                ]

    ins = [*terms, residual, upstream, gain, query, kv, mask, lse, cosine, sine]
    outs = [
        ((rows, width), FULL),
        ((rows, width), LOW),
        ((1, width), FULL),
        ((rows, QUERY_WIDTH), LOW),
    ] + [((rows, 2 * KEY_WIDTH), LOW)] * parts
    return call(
        "back_attend",
        kernel,
        outs,
        ins + [weights] * blocks,
        grid=(1,),
        in_specs=[constant(x.shape) for x in ins] + weight_specs,
        out_specs=[constant(shape) for shape, _ in outs],
        scratch=[pltpu.VMEM((rows, QUERY_WIDTH), LOW)],
        far=[1, *range(4, 4 + parts)],
        flops=2 * rows * width * QUERY_WIDTH + 10 * rows * count * QUERY_WIDTH,
    )


def back_project_call(
    terms, da_query, mixed, weights, tokens, back_residual, gain, gain_back, cosine, sine, pieces,
    bias_width, gain_width,
):
    rows, width = tokens.shape
    given = len(terms)
    owners = pieces.size
    span = 256

    def kernel(*refs):
        term_refs = refs[:given]
        daq_ref, m_ref, w_ref, x_ref, dh_ref, gain_ref, gain_back_ref, cos_ref, sin_ref = refs[
            given : 9 + given
        ]
        dx_ref, piece_ref = refs[9 + given : 11 + given]
        da_ref, small_ref = refs[-2:]
        back = term_refs[0][...].astype(FULL)
        for ref in term_refs[1:]:
            back = back + ref[...].astype(FULL)
        used = PROJECTION_WIDTH + QUERY_WIDTH
        da_ref[:, PROJECTION_WIDTH:used] = m_ref[...]
        if da_ref.shape[1] > used:
            da_ref[:, used:] = jnp.zeros_like(da_ref[:, used:])
        da_ref[:, :QUERY_WIDTH] = daq_ref[...]
        for g in range(KV_HEADS):
            at = QUERY_WIDTH + g * HEAD_DIM
            da_ref[:, at : at + HEAD_DIM] = unrotate(
                back[:, g * HEAD_DIM : (g + 1) * HEAD_DIM], cos_ref[...], sin_ref[...]
            ).astype(LOW)
        da_ref[:, QUERY_WIDTH + KEY_WIDTH : PROJECTION_WIDTH] = back[:, KEY_WIDTH:].astype(LOW)
        da = da_ref[:, :PROJECTION_WIDTH]
        x = x_ref[...].astype(FULL)
        scale = inverse_rms(x)
        back_normed = dot(da, w_ref[...])
        dx_ref[...] = dh_ref[...] + norm_backward(x, scale, gain_ref[...], back_normed)
        small_ref[...] = jnp.zeros_like(small_ref)
        small_ref[0:1, :PROJECTION_WIDTH] = jnp.sum(da.astype(FULL), axis=0, keepdims=True)
        small_ref[1:2, :width] = jnp.sum(back_normed * x * scale, axis=0, keepdims=True)
        small_ref[2:3, :width] = gain_back_ref[...]
        for owner in range(owners):
            start = pieces.start_of(owner)
            piece_ref[owner, :rows, :] = da_ref[:, start : start + pieces.wide]
            piece_ref[owner, rows:, :] = jnp.zeros_like(piece_ref[owner, rows:, :])
            bias_at = owner * bias_width // 128 * 128
            gain_at = owner * gain_width // 128 * 128
            small = jnp.concatenate(
                [
                    small_ref[0:1, bias_at : bias_at + span],
                    small_ref[1:3, gain_at : gain_at + span],
                    jnp.zeros((13, span), FULL),
                ],
                axis=0,
            )
            piece_ref[owner, rows:, :span] = small.astype(LOW)

    ins = [*terms, da_query, mixed]
    more = [tokens, back_residual, gain, gain_back, cosine, sine]
    outs = [((rows, width), FULL)] + [((owners, rows + 16, pieces.wide), LOW)]
    return call(
        "back_project",
        kernel,
        outs,
        [*ins, weights, *more],
        grid=(1,),
        in_specs=[constant(x.shape) for x in ins]
        + [pl.BlockSpec((PROJECTION_WIDTH, width), lambda j: (0, 0))]
        + [constant(x.shape) for x in more],
        out_specs=[constant(shape) for shape, _ in outs],
        scratch=[
            pltpu.VMEM((rows, max(pieces.padded, PROJECTION_WIDTH + QUERY_WIDTH)), LOW),
            pltpu.VMEM((8, PROJECTION_WIDTH + span), FULL),
        ],
        flops=2 * rows * width * PROJECTION_WIDTH,
        far=(1,),
    )


def normed_call(place, pairs, gain):
    pair, width = pairs[0].shape
    chips = len(pairs)

    def kernel(place_ref, *refs):
        gain_ref, out_ref = refs[-2:]
        for d in range(chips):
            x = refs[d][...].astype(FULL)
            at = pl.ds(pl.multiple_of((place_ref[1] ^ d) * pair, 16), pair)
            out_ref[at, :] = (x * inverse_rms(x) * gain_ref[...]).astype(LOW)

    return call(
        "normed",
        kernel,
        [((pair * chips, width), LOW)],
        [place, *pairs, gain],
        in_specs=[pl.BlockSpec(memory_space=pltpu.SMEM)]
        + [pl.BlockSpec(memory_space=pltpu.VMEM)] * (chips + 1),
    )[0]


def attention_gradient_call(place, columns, normed_all, db_pairs, pieces, contexts):
    pair, width = db_pairs[0].shape
    rows = pair // 2
    chips = len(db_pairs)
    count = 2 * chips
    quarter = pieces.own_rows // contexts
    total = rows * count
    wide = pieces.wide

    def kernel(*refs):
        place_ref = refs[0]
        columns_ref, n_ref = refs[1:3]
        db_refs = refs[3 : 3 + chips]
        out_refs = refs[3 + chips : 3 + chips + contexts]
        left_ref, right_ref, sum_ref, cut_ref = refs[3 + chips + contexts :]
        owner = place_ref[1] * 2 + place_ref[2]
        start = pieces.start(owner)
        small = jnp.zeros((16, wide), FULL)
        for i in range(count):
            left_ref[pl.ds(i * rows, rows), :] = columns_ref[i, :rows, :]
            small = small + columns_ref[i, rows:, :].astype(FULL)
        for d, ref in enumerate(db_refs):
            at = pl.multiple_of((place_ref[1] ^ d) * pair, 16)
            right_ref[pl.ds(at, pair), :] = ref[...]
        of_project = start + lax.broadcasted_iota(jnp.int32, (wide, width), 0) < PROJECTION_WIDTH
        sum_ref[...] = jnp.where(
            of_project, dot(left_ref[...], n_ref[...], 0, 0), dot(left_ref[...], right_ref[...], 0, 0)
        )
        offset = pl.multiple_of(
            owner * pieces.own_rows - start, math.gcd(pieces.own_rows, 128)
        )
        own = sum_ref[pl.ds(offset, pieces.own_rows), :].astype(LOW)
        for c in range(contexts):
            cut_ref[c] = own[c * quarter : (c + 1) * quarter]
        for d, out_ref in enumerate(out_refs):
            out_ref[:quarter, :] = cut_ref[place_ref[0] ^ d]
            out_ref[quarter:, :] = jnp.zeros_like(out_ref[quarter:, :])
            out_ref[quarter:, :wide] = small.astype(LOW)

    ins = [columns, normed_all, *db_pairs]
    outs = [((quarter + 16, width), LOW)] * contexts
    return call(
        "attention_gradient",
        kernel,
        outs,
        [place, *ins],
        in_specs=[pl.BlockSpec(memory_space=pltpu.SMEM)]
        + [pl.BlockSpec(memory_space=pltpu.VMEM)] * len(ins),
        scratch=[
            pltpu.VMEM((total, wide), LOW),
            pltpu.VMEM((total, width), LOW),
            pltpu.VMEM((wide, width), FULL),
            pltpu.VMEM((contexts, quarter, width), LOW),
        ],
        flops=4 * total * wide * width,
        far=range(contexts),
    )


def total_of(terms):
    result = terms[0].astype(FULL)
    for term in terms[1:]:
        result = result + term.astype(FULL)
    return result


def make(ring, contexts):
    def per_device(
        tokens,
        document_starts,
        attention_weights,
        projection_bias,
        norm_gains,
        hidden_weights,
        cotangent,
    ):
        rows, width = tokens.shape[1:]
        chips = ring.chips
        me = lax.axis_index("ctx")
        index = lax.axis_index("fsdp")
        place = jnp.stack([me, index // 2, index % 2]).astype(jnp.int32)
        own_rows = attention_weights.shape[0]
        quarter = own_rows // contexts
        pieces = Pieces(own_rows, ring.size)
        bias_width = projection_bias.shape[0]
        gain_width = norm_gains.shape[1]

        weight_piece = lax.dynamic_slice_in_dim(attention_weights, me * quarter, quarter, 0)
        weights = lax.all_gather(weight_piece.astype(LOW), ("fsdp", "ctx"), axis=0, tiled=True)

        packed = jnp.concatenate([projection_bias, norm_gains.reshape(-1)]).astype(LOW)
        packed = jnp.pad(packed[None], ((0, 15), (0, width - packed.shape[0])))
        upstream = cotangent[0]
        upstream_pairs = [
            ring.both(b) for b in ring.chained(jnp.concatenate([upstream, packed], axis=0))
        ]
        params = jnp.stack([p.reshape(2, -1, width)[:, rows] for p in upstream_pairs])
        params = params.reshape(ring.size, width)
        owners = jnp.arange(ring.size, dtype=jnp.int32)
        at = owners ^ (index // 2 * 2)
        params = jnp.dot(
            (at[:, None] == owners[None, :]).astype(LOW), params, preferred_element_type=FULL
        )
        bias = params[:, :bias_width].reshape(1, -1)
        gain_one = params[:, bias_width : bias_width + gain_width].reshape(1, -1)
        gain_two = params[:, bias_width + gain_width : bias_width + 2 * gain_width].reshape(1, -1)

        starts = document_starts[0]
        within = jnp.arange(rows, dtype=jnp.int32)
        positions = me * rows + within
        cosine, sine = rope_tables(positions, HEAD_DIM)
        key_positions = jnp.concatenate([(me ^ d) * rows + within for d in range(contexts)])
        mask = jnp.where(
            (segments(starts, positions)[:, None] == segments(starts, key_positions)[None, :])
            & (key_positions[None, :] <= positions[:, None]),
            0.0,
            LOWEST,
        ).astype(FULL)

        gate_rows, up_rows, down_rows = cast_call(hidden_weights)
        back_hidden, upstream_all = back_hidden_call(upstream_pairs, down_rows, rows)
        weights, back_hidden, mask, cosine, sine, bias, gain_one, gain_two = (
            lax.optimization_barrier(
                (weights, back_hidden, mask, cosine, sine, bias, gain_one, gain_two)
            )
        )
        tokens_ahead = ring.chained(after(tokens[0], weights))
        query, kv = project_call(tokens[0], gain_one, weights, bias, cosine, sine)
        kv_blocks = context_send([kv] * contexts, contexts)
        lse, residual, normed_two, kv_all, mixed = attend_call(
            query, kv_blocks, mask, after(tokens[0], tokens_ahead[1]), weights, gain_two
        )

        kept, back_normed_terms = (), []
        ahead = ring.chained(after(normed_two, tokens_ahead[2 % chips]))
        done = ()
        for d in range(chips):
            *kept, own, other = feed_call(
                d, chips, place, ring.both(after(ahead[d], *done)), back_hidden, gate_rows,
                up_rows, kept,
            )
            summed = add_parts(place, own, ring.both(other), 1)[0]
            done = (summed, *back_normed_terms[1:][-1:])
            back_normed_terms.append(ring.send(summed, d) if d else summed)
        back, normed_all = kept
        back = after(back, *done, tokens_ahead[-1])
        hidden_term = weight_gradient_call(back, normed_all, upstream_all)
        hidden_shard = lax.psum_scatter(
            after(hidden_term, back_normed_terms[-1]), "ctx", scatter_dimension=0, tiled=True
        ).astype(FULL)
        back_normed_terms[0] = after(back_normed_terms[0], hidden_term)
        back_residual, back_branch, back_gain_two, da_query, *kv_back = back_attend_call(
            back_normed_terms, residual, upstream, gain_two, weights, query, kv_all, mask, lse,
            cosine, sine,
        )
        kv_terms = context_send(kv_back, contexts)
        branch_ahead = ring.ahead(back_branch)
        token_pairs = [ring.both(after(b, da_query)) for b in tokens_ahead]
        da_query = after(da_query, *token_pairs, *branch_ahead[1:3])
        back_inputs, projected_pieces = back_project_call(
            kv_terms, da_query, mixed, weights, tokens[0], back_residual, gain_one,
            back_gain_two, cosine, sine, pieces, bias_width, gain_width,
        )
        columns = lax.all_to_all(
            after(projected_pieces, *branch_ahead[1:]), "fsdp", 0, 0, tiled=True
        )
        lifted_own, lifted_other = lifted_call(place, after(back, projected_pieces), down_rows, chips)
        lifted_terms = add_parts(place, lifted_own, ring.send(lifted_other, 0, 1), chips)
        normed_one_all = normed_call(place, token_pairs, after(gain_one, lifted_terms[0]))
        branch_pairs = [ring.both(after(b, lifted_terms[0])) for b in branch_ahead]
        lifted_terms = [ring.send(block, d) if d else block for d, block in enumerate(lifted_terms)]
        output = (residual + total_of(lifted_terms)).astype(LOW)
        attention_terms = attention_gradient_call(
            place, columns, normed_one_all, branch_pairs, pieces, contexts
        )
        attention_terms = context_send(attention_terms, contexts)
        shards = total_of([after(attention_terms[0], output), *attention_terms[1:]])
        own_bias = bias_width // contexts
        own_gain = gain_width // contexts
        bias_at = index * bias_width % 128 + me * own_bias
        gain_at = index * gain_width % 128 + me * own_gain
        bias_shard = lax.dynamic_slice(shards, (quarter, bias_at), (1, own_bias))[0]
        gain_shard = lax.dynamic_slice(shards, (quarter + 1, gain_at), (2, own_gain))
        return (
            output[None],
            back_inputs[None],
            shards[:quarter],
            bias_shard,
            gain_shard,
            hidden_shard,
        )

    return per_device


def solution(mesh):
    placed = (
        P("fsdp", "ctx", None),
        P("fsdp", None),
        P("fsdp", None),
        P("fsdp"),
        P(None, "fsdp"),
        P("fsdp", None),
        P("fsdp", "ctx", None),
    )
    return jax.shard_map(
        make(Ring(mesh.shape["fsdp"]), mesh.shape["ctx"]),
        mesh=mesh,
        in_specs=placed,
        out_specs=(
            P("fsdp", "ctx", None),
            P("fsdp", "ctx", None),
            P(("fsdp", "ctx"), None),
            P(("fsdp", "ctx")),
            P(None, ("fsdp", "ctx")),
            P(("fsdp", "ctx"), None),
        ),
        check_vma=False,
    )
```

```python
import math

import jax
import jax.numpy as jnp
from jax import lax
from jax.experimental import pallas as pl
from jax.experimental.pallas import tpu as pltpu
from jax.sharding import PartitionSpec as P

HEADS = 12
KV_HEADS = 2
HEAD_DIM = 128
GROUP = HEADS // KV_HEADS
QUERY_WIDTH = HEADS * HEAD_DIM
KEY_WIDTH = KV_HEADS * HEAD_DIM
PROJECTION_WIDTH = QUERY_WIDTH + 2 * KEY_WIDTH
SCALE = HEAD_DIM ** (-0.5)
WEIGHT_BLOCK = 512

EPSILON = 1e-06
THETA = 10000.0
LOWEST = -1e30
LOW = jnp.bfloat16
FULL = jnp.float32
MIB = 2**20
COST = 1


def rope_tables(positions, width):
    half = width // 2
    frequency = THETA ** (-(jnp.arange(half, dtype=jnp.float32) * 2.0 / width))
    angle = positions.astype(jnp.float32)[:, None] * frequency[None, :]
    cosine = jnp.concatenate([jnp.cos(angle), jnp.cos(angle)], axis=1)
    sine = jnp.concatenate([jnp.sin(angle), jnp.sin(angle)], axis=1)
    return (cosine, sine)


def turn(vector):
    half = vector.shape[-1] // 2
    return jnp.concatenate([-vector[:, half:], vector[:, :half]], axis=1)


def rotate(vector, cosine, sine):
    return vector * cosine + turn(vector) * sine


def unrotate(gradient, cosine, sine):
    return gradient * cosine - turn(gradient * sine)


def segments(starts, positions):
    return jnp.sum((starts[None, :] <= positions[:, None]).astype(jnp.int32), axis=1) - 1


def inverse_rms(values):
    return lax.rsqrt(jnp.mean(values * values, axis=-1, keepdims=True) + EPSILON)


def norm_backward(inputs, scale, gain, back_normed):
    weighted = back_normed * gain
    return scale * weighted - inputs * (
        scale * scale * scale * jnp.mean(inputs * weighted, axis=-1, keepdims=True)
    )


def dot(left, right, left_dim=1, right_dim=0):
    return lax.dot_general(
        left, right, (((left_dim,), (right_dim,)), ((), ())), preferred_element_type=FULL
    )


def call(
    name, kernel, outs, ins, grid=None, in_specs=None, out_specs=None, scratch=(), flops=0, limit=60,
    far=(),
):
    shapes = [
        pltpu.HBM(shape, kind) if i in far else jax.ShapeDtypeStruct(shape, kind)
        for i, (shape, kind) in enumerate(outs)
    ]
    whole = pl.BlockSpec(memory_space=pltpu.VMEM)
    moved = sum(x.size * x.dtype.itemsize for x in ins) + sum(
        math.prod(shape) * jnp.dtype(kind).itemsize for shape, kind in outs
    )
    options = dict(grid=grid) if grid else {}
    return pl.pallas_call(
        kernel,
        name=name,
        out_shape=shapes,
        in_specs=in_specs or [whole] * len(ins),
        out_specs=out_specs or [whole] * len(outs),
        scratch_shapes=list(scratch),
        compiler_params=pltpu.CompilerParams(vmem_limit_bytes=limit * MIB),
        cost_estimate=pl.CostEstimate(
            flops=flops // COST, bytes_accessed=moved // COST, transcendentals=0
        ),
        **options,
    )(*ins)


def after(value, *others):
    return lax.optimization_barrier((value, *others))[0]


def constant(shape):
    return pl.BlockSpec(shape, lambda *_: (0,) * len(shape))


class Ring:
    def __init__(self, size):
        self.size = size
        self.chips = size // 2

    def send(self, block, chips, cores=0, to=None):
        moves = [(i, i ^ (2 * chips + cores)) for i in range(self.size)]
        if to is not None:
            moves = [(i, j) for i, j in moves if j // 2 in to]
        return lax.ppermute(block, "fsdp", moves)

    def both(self, block):
        pairs = [[i, i + 1] for i in range(0, self.size, 2)]
        return lax.all_gather(block, "fsdp", axis=0, tiled=True, axis_index_groups=pairs)

    def ahead(self, block, to=None):
        return [block] + [self.send(block, d, 0, to) for d in range(1, self.chips)]

    def chained(self, block):
        blocks = self.begun(block)
        return blocks + self.rest(blocks)

    def begun(self, block):
        if self.chips != 4:
            return self.ahead(block)
        two = self.send(block, 2)
        return [block, self.send(block, 1), two]

    def rest(self, blocks, *others):
        return [] if len(blocks) == self.chips else [self.send(after(blocks[2], *others), 1)]


def add_parts(place, own, both, count):
    total, width = own.shape
    rows = total // count
    first = both.shape[0] - total

    def kernel(place_ref, own_ref, both_ref, *out_refs):
        for d, out_ref in enumerate(out_refs):
            at = pl.multiple_of((1 - place_ref[2]) * first + d * rows, 16)
            got = both_ref[pl.ds(at, rows), :].astype(FULL)
            out_ref[...] = (own_ref[d * rows : (d + 1) * rows, :].astype(FULL) + got).astype(LOW)

    return call(
        "add_parts",
        kernel,
        [((rows, width), LOW)] * count,
        [place, own, both],
        in_specs=[pl.BlockSpec(memory_space=pltpu.SMEM)]
        + [pl.BlockSpec(memory_space=pltpu.VMEM)] * 2,
        limit=24,
        far=range(count),
    )


def context_send(blocks, count):
    return [blocks[0]] + [
        lax.ppermute(blocks[d], "ctx", [(i, i ^ d) for i in range(count)]) for d in range(1, count)
    ]


def cast_call(hidden_weights):
    units, width = hidden_weights.shape[0], hidden_weights.shape[1] // 3
    chunk = max(c for c in range(16, 257, 16) if units % c == 0)

    def kernel(w_ref, *out_refs):
        for i, ref in enumerate(out_refs):
            ref[...] = w_ref[:, i * width : (i + 1) * width].astype(LOW)

    return call(
        "cast",
        kernel,
        [((units, width), LOW)] * 3,
        [hidden_weights],
        grid=(units // chunk,),
        in_specs=[pl.BlockSpec((chunk, 3 * width), lambda j: (j, 0))],
        out_specs=[pl.BlockSpec((chunk, width), lambda j: (j, 0))] * 3,
        limit=24,
    )


def back_hidden_call(pairs, down, rows):
    pair_rows, width = pairs[0].shape
    units = down.shape[0]
    chips = len(pairs)
    second = pair_rows // 2

    def kernel(*refs):
        down_ref, e_ref, all_ref = refs[-3:]
        for d in range(chips):

            @pl.when(pl.program_id(0) == d)
            def _():
                all_ref[:rows, :] = refs[d][:rows, :]
                all_ref[rows:, :] = refs[d][second : second + rows, :]

        e_ref[...] = dot(all_ref[...], down_ref[...], 1, 1).astype(LOW)

    return call(
        "back_hidden",
        kernel,
        [((2 * chips * rows, units), LOW), ((2 * chips * rows, width), LOW)],
        [*pairs, down],
        grid=(chips,),
        in_specs=[constant((pair_rows, width))] * chips + [constant((units, width))],
        out_specs=[
            pl.BlockSpec((2 * rows, units), lambda j: (j, 0)),
            pl.BlockSpec((2 * rows, width), lambda j: (j, 0)),
        ],
        flops=4 * chips * rows * width * units,
        limit=32,
    )


def feed_call(d, chips, place, tokens, back_hidden, gate_rows, up_rows, kept):
    pair, width = tokens.shape
    units = gate_rows.shape[0]
    rows = pair // 2

    def kernel(*refs):
        place_ref, tokens_ref, e_ref, gate_ref, up_ref = refs[:5]
        back_ref, all_ref, own_ref, other_ref, sum_ref = refs[-5:]
        normed = tokens_ref[...]
        all_ref[...] = normed
        gate = dot(normed, gate_ref[...], 1, 1)
        up = dot(normed, up_ref[...], 1, 1)
        back = e_ref[...].astype(FULL)
        sigmoid = jax.nn.sigmoid(gate)
        silu = gate * sigmoid
        back_ref[2] = (silu * up).astype(LOW)
        back_ref[1] = (back * silu).astype(LOW)
        back_ref[0] = (back * up * (sigmoid * (1.0 + gate * (1.0 - sigmoid)))).astype(LOW)
        sum_ref[...] = (dot(back_ref[0], gate_ref[...]) + dot(back_ref[1], up_ref[...])).astype(LOW)
        core = place_ref[2]
        own_ref[...] = sum_ref[pl.ds(pl.multiple_of(core * rows, 16), rows), :]
        other_ref[...] = sum_ref[pl.ds(pl.multiple_of((1 - core) * rows, 16), rows), :]

    ins = [place, tokens, back_hidden, gate_rows, up_rows, *kept]
    outs = [
        ((3, chips * pair, units), LOW),
        ((chips * pair, width), LOW),
        ((rows, width), LOW),
        ((rows, width), LOW),
    ]
    return pl.pallas_call(
        kernel,
        name="feed",
        grid=(1,),
        out_shape=[jax.ShapeDtypeStruct(shape, kind) for shape, kind in outs],
        in_specs=[
            pl.BlockSpec(memory_space=pltpu.SMEM),
            constant((pair, width)),
            pl.BlockSpec((pair, units), lambda j: (d, 0)),
        ]
        + [constant((units, width))] * 2
        + [pl.BlockSpec(memory_space=pl.ANY)] * len(kept),
        out_specs=[
            pl.BlockSpec((3, pair, units), lambda j: (0, d, 0)),
            pl.BlockSpec((pair, width), lambda j: (d, 0)),
            constant((rows, width)),
            constant((rows, width)),
        ],
        scratch_shapes=[pltpu.VMEM((pair, width), LOW)],
        input_output_aliases={5 + i: i for i in range(len(kept))},
        compiler_params=pltpu.CompilerParams(vmem_limit_bytes=36 * MIB),
        cost_estimate=pl.CostEstimate(
            flops=8 * pair * width * units // COST,
            bytes_accessed=(4 * units * width + 16 * pair * width) // COST,
            transcendentals=0,
        ),
    )(*ins)


def weight_gradient_call(back, normed_all, upstream_all):
    _, total, units = back.shape
    width = normed_all.shape[1]
    steps = 1
    part = width // steps

    def kernel(back_ref, normed_ref, upstream_ref, out_ref):
        step = pl.program_id(0)

        @pl.when(step < 2 * steps)
        def _():
            out_ref[...] = dot(back_ref[0], normed_ref[...], 0, 0).astype(LOW)

        @pl.when(step >= 2 * steps)
        def _():
            out_ref[...] = dot(back_ref[0], upstream_ref[...], 0, 0).astype(LOW)

    return call(
        "weight_gradient",
        kernel,
        [((units, 3 * width), LOW)],
        [back, normed_all, upstream_all],
        grid=(3 * steps,),
        in_specs=[
            pl.BlockSpec((1, total, units), lambda j: (j // steps, 0, 0)),
            pl.BlockSpec((total, part), lambda j: (0, jnp.where(j < 2 * steps, j % steps, steps - 1))),
            pl.BlockSpec((total, part), lambda j: (0, jnp.maximum(j - 2 * steps, 0))),
        ],
        out_specs=[pl.BlockSpec((units, part), lambda j: (0, j))],
        flops=6 * total * width * units,
        limit=32,
    )[0]


def lifted_call(place, back, down, chips):
    _, total, units = back.shape
    width = down.shape[1]
    rows = total // (2 * chips)

    def kernel(place_ref, z_ref, down_ref, own_ref, other_ref, sum_ref):
        sum_ref[...] = dot(z_ref[0], down_ref[...]).astype(LOW)
        core = place_ref[2]
        own_ref[...] = sum_ref[pl.ds(pl.multiple_of(core * rows, 16), rows), :]
        other_ref[...] = sum_ref[pl.ds(pl.multiple_of((1 - core) * rows, 16), rows), :]

    return call(
        "lifted",
        kernel,
        [((total // 2, width), LOW)] * 2,
        [place, back, down],
        grid=(chips,),
        in_specs=[
            pl.BlockSpec(memory_space=pltpu.SMEM),
            pl.BlockSpec((1, 2 * rows, units), lambda j: (2, j, 0)),
            constant((units, width)),
        ],
        out_specs=[pl.BlockSpec((rows, width), lambda j: (j, 0))] * 2,
        scratch=[pltpu.VMEM((2 * rows, width), LOW)],
        flops=2 * total * width * units,
        far=(1,),
    )


def project_call(tokens, gain, weights, bias, cosine, sine, first, count, far=()):
    rows, width = tokens.shape
    heads = WEIGHT_BLOCK // HEAD_DIM

    def kernel(x_ref, gain_ref, w_ref, bias_ref, cos_ref, sin_ref, out_ref, n_ref):
        step = pl.program_id(0)

        @pl.when(step == 0)
        def _():
            x = x_ref[...].astype(FULL)
            n_ref[...] = (x * inverse_rms(x) * gain_ref[...]).astype(LOW)

        a = dot(n_ref[...], w_ref[...], 1, 1) + bias_ref[...]
        for h in range(heads):
            one = a[:, h * HEAD_DIM : (h + 1) * HEAD_DIM]
            turned = rotate(one, cos_ref[...], sin_ref[...])
            is_value = (first + step) * heads + h >= HEADS + KV_HEADS
            out_ref[:, h * HEAD_DIM : (h + 1) * HEAD_DIM] = jnp.where(
                is_value, one, turned
            ).astype(LOW)

    return call(
        "project",
        kernel,
        [((rows, count * WEIGHT_BLOCK), LOW)],
        [tokens, gain, weights, bias, cosine, sine],
        grid=(count,),
        in_specs=[
            constant((rows, width)),
            constant((1, width)),
            pl.BlockSpec((WEIGHT_BLOCK, width), lambda j: (first + j, 0)),
            pl.BlockSpec((1, WEIGHT_BLOCK), lambda j: (0, first + j)),
            constant((rows, HEAD_DIM)),
            constant((rows, HEAD_DIM)),
        ],
        out_specs=[pl.BlockSpec((rows, WEIGHT_BLOCK), lambda j: (0, j))],
        scratch=[pltpu.VMEM((rows, width), LOW)],
        flops=2 * rows * width * count * WEIGHT_BLOCK,
        far=far,
    )[0]


def stacked(ref, kv_head):
    return jnp.concatenate(
        [
            ref[:, h * HEAD_DIM : (h + 1) * HEAD_DIM]
            for h in range(kv_head * GROUP, (kv_head + 1) * GROUP)
        ],
        axis=0,
    )


def masked_scores(query, key, mask):
    rows = mask.shape[0]
    raw = dot(query, key, 1, 1) * SCALE
    return (raw.reshape(GROUP, rows, -1) + mask[None]).reshape(raw.shape)


def output_weight_specs(width):
    first = PROJECTION_WIDTH // WEIGHT_BLOCK
    return [
        pl.BlockSpec((WEIGHT_BLOCK, width), lambda j, i=i: (first + i, 0))
        for i in range(QUERY_WIDTH // WEIGHT_BLOCK)
    ]


class Pieces:
    def __init__(self, own_rows, size):
        self.own_rows, self.size = own_rows, size
        starts = [f * own_rows // 128 * 128 for f in range(size)]
        self.wide = max(-(-((f + 1) * own_rows) // 128) * 128 - starts[f] for f in range(size))
        self.padded = max(starts) + self.wide

    def start_of(self, owner):
        return owner * self.own_rows // 128 * 128

    def start(self, owner):
        return pl.multiple_of(owner * self.own_rows // 128 * 128, 128)


def owner_at(place_ref, place):
    return (place_ref[1] ^ (place // 2)) * 2 + place % 2


def attend_call(query, kv_blocks, mask, tokens, weights, gain):
    rows, width = tokens.shape
    parts = len(kv_blocks)
    count = rows * parts
    weight_specs = output_weight_specs(width)
    blocks = len(weight_specs)

    def kernel(*refs):
        q_ref = refs[0]
        kv_refs = refs[1 : 1 + parts]
        mask_ref, x_ref, gain_ref = refs[1 + parts : 4 + parts]
        w_refs = refs[4 + parts : 4 + parts + blocks]
        lse_ref, h_ref, n_ref, kv_ref, m_ref = refs[4 + parts + blocks :]
        for i, ref in enumerate(kv_refs):
            kv_ref[pl.ds(i * rows, rows), :] = ref[...]
        for g in range(KV_HEADS):
            key = kv_ref[:, g * HEAD_DIM : (g + 1) * HEAD_DIM]
            value = kv_ref[:, KEY_WIDTH + g * HEAD_DIM : KEY_WIDTH + (g + 1) * HEAD_DIM]
            scores = masked_scores(stacked(q_ref, g), key, mask_ref[...])
            top = jnp.max(scores, axis=-1, keepdims=True)
            raised = jnp.exp(scores - top)
            total = jnp.sum(raised, axis=-1, keepdims=True)
            lse_ref[g] = top + jnp.log(total)
            mixed = dot((raised / total).astype(LOW), value).astype(LOW)
            for i in range(GROUP):
                at = (g * GROUP + i) * HEAD_DIM
                m_ref[:, at : at + HEAD_DIM] = mixed[i * rows : (i + 1) * rows]
        h = x_ref[...].astype(FULL)
        for i, w_ref in enumerate(w_refs):
            at = i * WEIGHT_BLOCK
            h = h + dot(m_ref[:, at : at + WEIGHT_BLOCK], w_ref[...])
        h_ref[...] = h
        n_ref[...] = (h * inverse_rms(h) * gain_ref[...]).astype(LOW)

    full = [constant((rows, QUERY_WIDTH))] + [constant((rows, 2 * KEY_WIDTH))] * parts
    return call(
        "attend",
        kernel,
        [
            ((KV_HEADS, GROUP * rows, 1), FULL),
            ((rows, width), FULL),
            ((rows, width), LOW),
            ((count, 2 * KEY_WIDTH), LOW),
            ((rows, QUERY_WIDTH), LOW),
        ],
        [query, *kv_blocks, mask, tokens, gain] + [weights] * blocks,
        grid=(1,),
        in_specs=full
        + [constant((rows, count)), constant((rows, width)), constant((1, width))]
        + weight_specs,
        out_specs=[
            constant((KV_HEADS, GROUP * rows, 1)),
            constant((rows, width)),
            constant((rows, width)),
            constant((count, 2 * KEY_WIDTH)),
            constant((rows, QUERY_WIDTH)),
        ],
        far=(2,),
        flops=2 * rows * width * QUERY_WIDTH + 4 * rows * count * QUERY_WIDTH,
    )


def back_attend_call(terms, residual, upstream, gain, weights, query, kv, mask, lse, cosine, sine):
    rows, width = residual.shape
    count = kv.shape[0]
    parts = count // rows
    given = len(terms)
    weight_specs = output_weight_specs(width)
    blocks = len(weight_specs)

    def kernel(*refs):
        term_refs = refs[:given]
        h_ref, c_ref, gain_ref, q_ref, kv_ref, mask_ref, lse_ref, cos_ref, sin_ref = refs[
            given : given + 9
        ]
        w_refs = refs[given + 9 : given + 9 + blocks]
        dh_ref, db_ref, gain_back_ref, da_ref = refs[given + 9 + blocks : given + 13 + blocks]
        kv_back_refs = refs[given + 13 + blocks : given + 13 + blocks + parts]
        dm_ref = refs[-1]
        back = term_refs[0][...].astype(FULL)
        for ref in term_refs[1:]:
            back = back + ref[...].astype(FULL)
        h = h_ref[...]
        scale = inverse_rms(h)
        dh = c_ref[...].astype(FULL) + norm_backward(h, scale, gain_ref[...], back)
        gain_back_ref[...] = jnp.sum(back * h * scale, axis=0, keepdims=True)
        dh_ref[...] = dh
        db = dh.astype(LOW)
        db_ref[...] = db
        for i, w_ref in enumerate(w_refs):
            at = i * WEIGHT_BLOCK
            dm_ref[:, at : at + WEIGHT_BLOCK] = dot(db, w_ref[...], 1, 1).astype(LOW)
        for g in range(KV_HEADS):
            key = kv_ref[:, g * HEAD_DIM : (g + 1) * HEAD_DIM]
            value = kv_ref[:, KEY_WIDTH + g * HEAD_DIM : KEY_WIDTH + (g + 1) * HEAD_DIM]
            q = stacked(q_ref, g)
            dm = stacked(dm_ref, g)
            scores = masked_scores(q, key, mask_ref[...])
            probability = jnp.exp(scores - lse_ref[g])
            low = probability.astype(LOW)
            back_probability = dot(dm, value, 1, 1)
            delta = jnp.sum(low.astype(FULL) * back_probability, axis=-1, keepdims=True)
            back_scores = (probability * (back_probability - delta)).astype(LOW)
            back_query = dot(back_scores, key) * SCALE
            for i in range(GROUP):
                at = (g * GROUP + i) * HEAD_DIM
                da_ref[:, at : at + HEAD_DIM] = unrotate(
                    back_query[i * rows : (i + 1) * rows], cos_ref[...], sin_ref[...]
                ).astype(LOW)
            back_key = (dot(back_scores, q, 0, 0) * SCALE).astype(LOW)
            back_value = dot(low, dm, 0, 0).astype(LOW)
            for i, ref in enumerate(kv_back_refs):
                ref[:, g * HEAD_DIM : (g + 1) * HEAD_DIM] = back_key[i * rows : (i + 1) * rows]
                ref[:, KEY_WIDTH + g * HEAD_DIM : KEY_WIDTH + (g + 1) * HEAD_DIM] = back_value[
                    i * rows : (i + 1) * rows
                ]

    ins = [*terms, residual, upstream, gain, query, kv, mask, lse, cosine, sine]
    outs = [
        ((rows, width), FULL),
        ((rows, width), LOW),
        ((1, width), FULL),
        ((rows, QUERY_WIDTH), LOW),
    ] + [((rows, 2 * KEY_WIDTH), LOW)] * parts
    return call(
        "back_attend",
        kernel,
        outs,
        ins + [weights] * blocks,
        grid=(1,),
        in_specs=[constant(x.shape) for x in ins] + weight_specs,
        out_specs=[constant(shape) for shape, _ in outs],
        scratch=[pltpu.VMEM((rows, QUERY_WIDTH), LOW)],
        far=[1, *range(4, 4 + parts)],
        flops=2 * rows * width * QUERY_WIDTH + 10 * rows * count * QUERY_WIDTH,
    )


def back_project_call(
    terms, da_query, mixed, weights, tokens, back_residual, gain, gain_back, cosine, sine, pieces,
    bias_width, gain_width,
):
    rows, width = tokens.shape
    given = len(terms)
    owners = pieces.size
    span = 256

    def kernel(*refs):
        term_refs = refs[:given]
        daq_ref, m_ref, w_ref, x_ref, dh_ref, gain_ref, gain_back_ref, cos_ref, sin_ref = refs[
            given : 9 + given
        ]
        dx_ref, piece_ref = refs[9 + given : 11 + given]
        da_ref, small_ref = refs[-2:]
        back = term_refs[0][...].astype(FULL)
        for ref in term_refs[1:]:
            back = back + ref[...].astype(FULL)
        used = PROJECTION_WIDTH + QUERY_WIDTH
        da_ref[:, PROJECTION_WIDTH:used] = m_ref[...]
        if da_ref.shape[1] > used:
            da_ref[:, used:] = jnp.zeros_like(da_ref[:, used:])
        da_ref[:, :QUERY_WIDTH] = daq_ref[...]
        for g in range(KV_HEADS):
            at = QUERY_WIDTH + g * HEAD_DIM
            da_ref[:, at : at + HEAD_DIM] = unrotate(
                back[:, g * HEAD_DIM : (g + 1) * HEAD_DIM], cos_ref[...], sin_ref[...]
            ).astype(LOW)
        da_ref[:, QUERY_WIDTH + KEY_WIDTH : PROJECTION_WIDTH] = back[:, KEY_WIDTH:].astype(LOW)
        da = da_ref[:, :PROJECTION_WIDTH]
        x = x_ref[...].astype(FULL)
        scale = inverse_rms(x)
        back_normed = dot(da, w_ref[...])
        dx_ref[...] = dh_ref[...] + norm_backward(x, scale, gain_ref[...], back_normed)
        small_ref[...] = jnp.zeros_like(small_ref)
        small_ref[0:1, :PROJECTION_WIDTH] = jnp.sum(da.astype(FULL), axis=0, keepdims=True)
        small_ref[1:2, :width] = jnp.sum(back_normed * x * scale, axis=0, keepdims=True)
        small_ref[2:3, :width] = gain_back_ref[...]
        for owner in range(owners):
            start = pieces.start_of(owner)
            piece_ref[owner, :rows, :] = da_ref[:, start : start + pieces.wide]
            piece_ref[owner, rows:, :] = jnp.zeros_like(piece_ref[owner, rows:, :])
            bias_at = owner * bias_width // 128 * 128
            gain_at = owner * gain_width // 128 * 128
            small = jnp.concatenate(
                [
                    small_ref[0:1, bias_at : bias_at + span],
                    small_ref[1:3, gain_at : gain_at + span],
                    jnp.zeros((13, span), FULL),
                ],
                axis=0,
            )
            piece_ref[owner, rows:, :span] = small.astype(LOW)

    ins = [*terms, da_query, mixed]
    more = [tokens, back_residual, gain, gain_back, cosine, sine]
    outs = [((rows, width), FULL)] + [((owners, rows + 16, pieces.wide), LOW)]
    return call(
        "back_project",
        kernel,
        outs,
        [*ins, weights, *more],
        grid=(1,),
        in_specs=[constant(x.shape) for x in ins]
        + [pl.BlockSpec((PROJECTION_WIDTH, width), lambda j: (0, 0))]
        + [constant(x.shape) for x in more],
        out_specs=[constant(shape) for shape, _ in outs],
        scratch=[
            pltpu.VMEM((rows, max(pieces.padded, PROJECTION_WIDTH + QUERY_WIDTH)), LOW),
            pltpu.VMEM((8, PROJECTION_WIDTH + span), FULL),
        ],
        flops=2 * rows * width * PROJECTION_WIDTH,
        far=(1,),
    )


def normed_call(place, pairs, gain):
    pair, width = pairs[0].shape
    chips = len(pairs)

    def kernel(place_ref, *refs):
        gain_ref, out_ref = refs[-2:]
        for d in range(chips):
            x = refs[d][...].astype(FULL)
            at = pl.ds(pl.multiple_of((place_ref[1] ^ d) * pair, 16), pair)
            out_ref[at, :] = (x * inverse_rms(x) * gain_ref[...]).astype(LOW)

    return call(
        "normed",
        kernel,
        [((pair * chips, width), LOW)],
        [place, *pairs, gain],
        in_specs=[pl.BlockSpec(memory_space=pltpu.SMEM)]
        + [pl.BlockSpec(memory_space=pltpu.VMEM)] * (chips + 1),
    )[0]


def attention_gradient_call(place, columns, normed_all, db_pairs, pieces, contexts):
    pair, width = db_pairs[0].shape
    rows = pair // 2
    chips = len(db_pairs)
    count = 2 * chips
    quarter = pieces.own_rows // contexts
    total = rows * count
    wide = pieces.wide

    def kernel(*refs):
        place_ref = refs[0]
        columns_ref, n_ref = refs[1:3]
        db_refs = refs[3 : 3 + chips]
        out_refs = refs[3 + chips : 3 + chips + contexts]
        left_ref, right_ref, sum_ref, cut_ref = refs[3 + chips + contexts :]
        owner = place_ref[1] * 2 + place_ref[2]
        start = pieces.start(owner)
        small = jnp.zeros((16, wide), FULL)
        for i in range(count):
            left_ref[pl.ds(i * rows, rows), :] = columns_ref[i, :rows, :]
            small = small + columns_ref[i, rows:, :].astype(FULL)
        for d, ref in enumerate(db_refs):
            at = pl.multiple_of((place_ref[1] ^ d) * pair, 16)
            right_ref[pl.ds(at, pair), :] = ref[...]
        of_project = start + lax.broadcasted_iota(jnp.int32, (wide, width), 0) < PROJECTION_WIDTH
        sum_ref[...] = jnp.where(
            of_project, dot(left_ref[...], n_ref[...], 0, 0), dot(left_ref[...], right_ref[...], 0, 0)
        )
        offset = pl.multiple_of(
            owner * pieces.own_rows - start, math.gcd(pieces.own_rows, 128)
        )
        own = sum_ref[pl.ds(offset, pieces.own_rows), :].astype(LOW)
        for c in range(contexts):
            cut_ref[c] = own[c * quarter : (c + 1) * quarter]
        for d, out_ref in enumerate(out_refs):
            out_ref[:quarter, :] = cut_ref[place_ref[0] ^ d]
            out_ref[quarter:, :] = jnp.zeros_like(out_ref[quarter:, :])
            out_ref[quarter:, :wide] = small.astype(LOW)

    ins = [columns, normed_all, *db_pairs]
    outs = [((quarter + 16, width), LOW)] * contexts
    return call(
        "attention_gradient",
        kernel,
        outs,
        [place, *ins],
        in_specs=[pl.BlockSpec(memory_space=pltpu.SMEM)]
        + [pl.BlockSpec(memory_space=pltpu.VMEM)] * len(ins),
        scratch=[
            pltpu.VMEM((total, wide), LOW),
            pltpu.VMEM((total, width), LOW),
            pltpu.VMEM((wide, width), FULL),
            pltpu.VMEM((contexts, quarter, width), LOW),
        ],
        flops=4 * total * wide * width,
        far=range(contexts),
    )


def total_of(terms):
    result = terms[0].astype(FULL)
    for term in terms[1:]:
        result = result + term.astype(FULL)
    return result


def make(ring, contexts):
    def per_device(
        tokens,
        document_starts,
        attention_weights,
        projection_bias,
        norm_gains,
        hidden_weights,
        cotangent,
    ):
        rows, width = tokens.shape[1:]
        chips = ring.chips
        me = lax.axis_index("ctx")
        index = lax.axis_index("fsdp")
        place = jnp.stack([me, index // 2, index % 2]).astype(jnp.int32)
        own_rows = attention_weights.shape[0]
        quarter = own_rows // contexts
        pieces = Pieces(own_rows, ring.size)
        bias_width = projection_bias.shape[0]
        gain_width = norm_gains.shape[1]

        weight_piece = lax.dynamic_slice_in_dim(attention_weights, me * quarter, quarter, 0)
        weights = lax.all_gather(weight_piece.astype(LOW), ("fsdp", "ctx"), axis=0, tiled=True)

        packed = jnp.concatenate([projection_bias, norm_gains.reshape(-1)]).astype(LOW)
        packed = jnp.pad(packed[None], ((0, 15), (0, width - packed.shape[0])))
        upstream = cotangent[0]
        upstream_pairs = [
            ring.both(b) for b in ring.chained(jnp.concatenate([upstream, packed], axis=0))
        ]
        params = jnp.stack([p.reshape(2, -1, width)[:, rows] for p in upstream_pairs])
        params = params.reshape(ring.size, width)
        owners = jnp.arange(ring.size, dtype=jnp.int32)
        at = owners ^ (index // 2 * 2)
        params = jnp.dot(
            (at[:, None] == owners[None, :]).astype(LOW), params, preferred_element_type=FULL
        )
        bias = params[:, :bias_width].reshape(1, -1)
        gain_one = params[:, bias_width : bias_width + gain_width].reshape(1, -1)
        gain_two = params[:, bias_width + gain_width : bias_width + 2 * gain_width].reshape(1, -1)

        starts = document_starts[0]
        within = jnp.arange(rows, dtype=jnp.int32)
        positions = me * rows + within
        cosine, sine = rope_tables(positions, HEAD_DIM)
        key_positions = jnp.concatenate([(me ^ d) * rows + within for d in range(contexts)])
        mask = jnp.where(
            (segments(starts, positions)[:, None] == segments(starts, key_positions)[None, :])
            & (key_positions[None, :] <= positions[:, None]),
            0.0,
            LOWEST,
        ).astype(FULL)

        gate_rows, up_rows, down_rows = cast_call(hidden_weights)
        back_hidden, upstream_all = back_hidden_call(upstream_pairs, down_rows, rows)
        weights, back_hidden, mask, cosine, sine, bias, gain_one, gain_two = (
            lax.optimization_barrier(
                (weights, back_hidden, mask, cosine, sine, bias, gain_one, gain_two)
            )
        )
        tokens_ahead = ring.begun(after(tokens[0], weights))
        blocks = QUERY_WIDTH // WEIGHT_BLOCK
        kv = project_call(
            tokens[0], gain_one, weights, bias, cosine, sine, blocks, 2 * KEY_WIDTH // WEIGHT_BLOCK,
            far=(0,),
        )
        query = project_call(
            after(tokens[0], kv), gain_one, weights, bias, cosine, sine, 0, blocks
        )
        kv_blocks = context_send([kv] * contexts, contexts)
        lse, residual, normed_two, kv_all, mixed = attend_call(
            query, kv_blocks, mask, tokens[0], weights, gain_two
        )

        kept, back_normed_terms = (), []
        ahead = ring.chained(after(normed_two, *tokens_ahead[1:3]))
        done = ()
        for d in range(chips):
            *kept, own, other = feed_call(
                d, chips, place, ring.both(after(ahead[d], *done)), back_hidden, gate_rows,
                up_rows, kept,
            )
            summed = add_parts(place, own, ring.both(other), 1)[0]
            done = (summed, *back_normed_terms[1:][-1:])
            if d == 3:
                tokens_ahead += ring.rest(tokens_ahead, summed)
            back_normed_terms.append(ring.send(summed, d) if d else summed)
        back, normed_all = kept
        back = after(back, summed)
        hidden_term = weight_gradient_call(back, normed_all, upstream_all)
        hidden_shard = lax.psum_scatter(
            after(hidden_term, *back_normed_terms[-2:]), "ctx", scatter_dimension=0, tiled=True
        ).astype(FULL)
        back_normed_terms[0] = after(back_normed_terms[0], hidden_term)
        back_residual, back_branch, back_gain_two, da_query, *kv_back = back_attend_call(
            back_normed_terms, residual, upstream, gain_two, weights, query, kv_all, mask, lse,
            cosine, sine,
        )
        kv_terms = context_send(kv_back, contexts)
        branch_ahead = ring.ahead(back_branch)
        token_pairs = [ring.both(after(b, da_query)) for b in tokens_ahead]
        da_query = after(da_query, *token_pairs, *branch_ahead[1:3])
        back_inputs, projected_pieces = back_project_call(
            kv_terms, da_query, mixed, weights, tokens[0], back_residual, gain_one,
            back_gain_two, cosine, sine, pieces, bias_width, gain_width,
        )
        columns = lax.all_to_all(
            after(projected_pieces, *branch_ahead[1:]), "fsdp", 0, 0, tiled=True
        )
        lifted_own, lifted_other = lifted_call(place, after(back, projected_pieces), down_rows, chips)
        lifted_terms = add_parts(place, lifted_own, ring.send(lifted_other, 0, 1), chips)
        normed_one_all = normed_call(place, token_pairs, after(gain_one, lifted_terms[0]))
        branch_pairs = [ring.both(after(b, lifted_terms[0])) for b in branch_ahead]
        lifted_terms = [ring.send(block, d) if d else block for d, block in enumerate(lifted_terms)]
        output = (residual + total_of(lifted_terms)).astype(LOW)
        attention_terms = attention_gradient_call(
            place, columns, normed_one_all, branch_pairs, pieces, contexts
        )
        attention_terms = context_send(attention_terms, contexts)
        shards = total_of([after(attention_terms[0], output, hidden_shard), *attention_terms[1:]])
        own_bias = bias_width // contexts
        own_gain = gain_width // contexts
        bias_at = index * bias_width % 128 + me * own_bias
        gain_at = index * gain_width % 128 + me * own_gain
        bias_shard = lax.dynamic_slice(shards, (quarter, bias_at), (1, own_bias))[0]
        gain_shard = lax.dynamic_slice(shards, (quarter + 1, gain_at), (2, own_gain))
        return (
            output[None],
            back_inputs[None],
            shards[:quarter],
            bias_shard,
            gain_shard,
            hidden_shard,
        )

    return per_device


def solution(mesh):
    placed = (
        P("fsdp", "ctx", None),
        P("fsdp", None),
        P("fsdp", None),
        P("fsdp"),
        P(None, "fsdp"),
        P("fsdp", None),
        P("fsdp", "ctx", None),
    )
    return jax.shard_map(
        make(Ring(mesh.shape["fsdp"]), mesh.shape["ctx"]),
        mesh=mesh,
        in_specs=placed,
        out_specs=(
            P("fsdp", "ctx", None),
            P("fsdp", "ctx", None),
            P(("fsdp", "ctx"), None),
            P(("fsdp", "ctx")),
            P(None, ("fsdp", "ctx")),
            P(("fsdp", "ctx"), None),
        ),
        check_vma=False,
    )
```

```python
import math

import jax
import jax.numpy as jnp
from jax import lax
from jax.experimental import pallas as pl
from jax.experimental.pallas import tpu as pltpu
from jax.sharding import PartitionSpec as P

HEADS = 12
KV_HEADS = 2
HEAD_DIM = 128
GROUP = HEADS // KV_HEADS
QUERY_WIDTH = HEADS * HEAD_DIM
KEY_WIDTH = KV_HEADS * HEAD_DIM
PROJECTION_WIDTH = QUERY_WIDTH + 2 * KEY_WIDTH
SCALE = HEAD_DIM ** (-0.5)
WEIGHT_BLOCK = 512

EPSILON = 1e-06
THETA = 10000.0
LOWEST = -1e30
LOW = jnp.bfloat16
FULL = jnp.float32
MIB = 2**20
COST = 1


def rope_tables(positions, width):
    half = width // 2
    frequency = THETA ** (-(jnp.arange(half, dtype=jnp.float32) * 2.0 / width))
    angle = positions.astype(jnp.float32)[:, None] * frequency[None, :]
    cosine = jnp.concatenate([jnp.cos(angle), jnp.cos(angle)], axis=1)
    sine = jnp.concatenate([jnp.sin(angle), jnp.sin(angle)], axis=1)
    return (cosine, sine)


def turn(vector):
    half = vector.shape[-1] // 2
    return jnp.concatenate([-vector[:, half:], vector[:, :half]], axis=1)


def rotate(vector, cosine, sine):
    return vector * cosine + turn(vector) * sine


def unrotate(gradient, cosine, sine):
    return gradient * cosine - turn(gradient * sine)


def segments(starts, positions):
    return jnp.sum((starts[None, :] <= positions[:, None]).astype(jnp.int32), axis=1) - 1


def inverse_rms(values):
    return lax.rsqrt(jnp.mean(values * values, axis=-1, keepdims=True) + EPSILON)


def norm_backward(inputs, scale, gain, back_normed):
    weighted = back_normed * gain
    return scale * weighted - inputs * (
        scale * scale * scale * jnp.mean(inputs * weighted, axis=-1, keepdims=True)
    )


def dot(left, right, left_dim=1, right_dim=0):
    return lax.dot_general(
        left, right, (((left_dim,), (right_dim,)), ((), ())), preferred_element_type=FULL
    )


def call(
    name, kernel, outs, ins, grid=None, in_specs=None, out_specs=None, scratch=(), flops=0, limit=60,
    far=(),
):
    shapes = [
        pltpu.HBM(shape, kind) if i in far else jax.ShapeDtypeStruct(shape, kind)
        for i, (shape, kind) in enumerate(outs)
    ]
    whole = pl.BlockSpec(memory_space=pltpu.VMEM)
    moved = sum(x.size * x.dtype.itemsize for x in ins) + sum(
        math.prod(shape) * jnp.dtype(kind).itemsize for shape, kind in outs
    )
    options = dict(grid=grid) if grid else {}
    return pl.pallas_call(
        kernel,
        name=name,
        out_shape=shapes,
        in_specs=in_specs or [whole] * len(ins),
        out_specs=out_specs or [whole] * len(outs),
        scratch_shapes=list(scratch),
        compiler_params=pltpu.CompilerParams(vmem_limit_bytes=limit * MIB),
        cost_estimate=pl.CostEstimate(
            flops=flops // COST, bytes_accessed=moved // COST, transcendentals=0
        ),
        **options,
    )(*ins)


def after(value, *others):
    return lax.optimization_barrier((value, *others))[0]


def constant(shape):
    return pl.BlockSpec(shape, lambda *_: (0,) * len(shape))


class Ring:
    def __init__(self, size):
        self.size = size
        self.chips = size // 2

    def send(self, block, chips, cores=0, to=None):
        moves = [(i, i ^ (2 * chips + cores)) for i in range(self.size)]
        if to is not None:
            moves = [(i, j) for i, j in moves if j // 2 in to]
        return lax.ppermute(block, "fsdp", moves)

    def both(self, block):
        pairs = [[i, i + 1] for i in range(0, self.size, 2)]
        return lax.all_gather(block, "fsdp", axis=0, tiled=True, axis_index_groups=pairs)

    def ahead(self, block, to=None):
        return [block] + [self.send(block, d, 0, to) for d in range(1, self.chips)]

    def chained(self, block):
        blocks = self.begun(block)
        return blocks + self.rest(blocks)

    def begun(self, block):
        if self.chips != 4:
            return self.ahead(block)
        two = self.send(block, 2)
        return [block, self.send(block, 1), two]

    def rest(self, blocks, *others):
        return [] if len(blocks) == self.chips else [self.send(after(blocks[2], *others), 1)]


def add_parts(place, own, both, count):
    total, width = own.shape
    rows = total // count
    first = both.shape[0] - total

    def kernel(place_ref, own_ref, both_ref, *out_refs):
        for d, out_ref in enumerate(out_refs):
            at = pl.multiple_of((1 - place_ref[2]) * first + d * rows, 16)
            got = both_ref[pl.ds(at, rows), :].astype(FULL)
            out_ref[...] = (own_ref[d * rows : (d + 1) * rows, :].astype(FULL) + got).astype(LOW)

    return call(
        "add_parts",
        kernel,
        [((rows, width), LOW)] * count,
        [place, own, both],
        in_specs=[pl.BlockSpec(memory_space=pltpu.SMEM)]
        + [pl.BlockSpec(memory_space=pltpu.VMEM)] * 2,
        limit=24,
        far=range(count),
    )


def context_send(blocks, count):
    return [blocks[0]] + [
        lax.ppermute(blocks[d], "ctx", [(i, i ^ d) for i in range(count)]) for d in range(1, count)
    ]


def cast_call(hidden_weights):
    units, width = hidden_weights.shape[0], hidden_weights.shape[1] // 3
    chunk = max(c for c in range(16, 257, 16) if units % c == 0)

    def kernel(w_ref, *out_refs):
        for i, ref in enumerate(out_refs):
            ref[...] = w_ref[:, i * width : (i + 1) * width].astype(LOW)

    return call(
        "cast",
        kernel,
        [((units, width), LOW)] * 3,
        [hidden_weights],
        grid=(units // chunk,),
        in_specs=[pl.BlockSpec((chunk, 3 * width), lambda j: (j, 0))],
        out_specs=[pl.BlockSpec((chunk, width), lambda j: (j, 0))] * 3,
        limit=24,
    )


def back_hidden_call(pairs, down, rows):
    pair_rows, width = pairs[0].shape
    units = down.shape[0]
    chips = len(pairs)
    second = pair_rows // 2

    def kernel(*refs):
        down_ref, e_ref, all_ref = refs[-3:]
        for d in range(chips):

            @pl.when(pl.program_id(0) == d)
            def _():
                all_ref[:rows, :] = refs[d][:rows, :]
                all_ref[rows:, :] = refs[d][second : second + rows, :]

        e_ref[...] = dot(all_ref[...], down_ref[...], 1, 1).astype(LOW)

    return call(
        "back_hidden",
        kernel,
        [((2 * chips * rows, units), LOW), ((2 * chips * rows, width), LOW)],
        [*pairs, down],
        grid=(chips,),
        in_specs=[constant((pair_rows, width))] * chips + [constant((units, width))],
        out_specs=[
            pl.BlockSpec((2 * rows, units), lambda j: (j, 0)),
            pl.BlockSpec((2 * rows, width), lambda j: (j, 0)),
        ],
        flops=4 * chips * rows * width * units,
        limit=32,
    )


def feed_call(d, chips, place, tokens, back_hidden, gate_rows, up_rows, kept):
    pair, width = tokens.shape
    units = gate_rows.shape[0]
    rows = pair // 2

    def kernel(*refs):
        place_ref, tokens_ref, e_ref, gate_ref, up_ref = refs[:5]
        back_ref, all_ref, own_ref, other_ref, sum_ref = refs[-5:]
        normed = tokens_ref[...]
        all_ref[...] = normed
        gate = dot(normed, gate_ref[...], 1, 1)
        up = dot(normed, up_ref[...], 1, 1)
        back = e_ref[...].astype(FULL)
        sigmoid = jax.nn.sigmoid(gate)
        silu = gate * sigmoid
        back_ref[2] = (silu * up).astype(LOW)
        back_ref[1] = (back * silu).astype(LOW)
        back_ref[0] = (back * up * (sigmoid * (1.0 + gate * (1.0 - sigmoid)))).astype(LOW)
        sum_ref[...] = (dot(back_ref[0], gate_ref[...]) + dot(back_ref[1], up_ref[...])).astype(LOW)
        core = place_ref[2]
        own_ref[...] = sum_ref[pl.ds(pl.multiple_of(core * rows, 16), rows), :]
        other_ref[...] = sum_ref[pl.ds(pl.multiple_of((1 - core) * rows, 16), rows), :]

    ins = [place, tokens, back_hidden, gate_rows, up_rows, *kept]
    outs = [
        ((3, chips * pair, units), LOW),
        ((chips * pair, width), LOW),
        ((rows, width), LOW),
        ((rows, width), LOW),
    ]
    return pl.pallas_call(
        kernel,
        name="feed",
        grid=(1,),
        out_shape=[jax.ShapeDtypeStruct(shape, kind) for shape, kind in outs],
        in_specs=[
            pl.BlockSpec(memory_space=pltpu.SMEM),
            constant((pair, width)),
            pl.BlockSpec((pair, units), lambda j: (d, 0)),
        ]
        + [constant((units, width))] * 2
        + [pl.BlockSpec(memory_space=pl.ANY)] * len(kept),
        out_specs=[
            pl.BlockSpec((3, pair, units), lambda j: (0, d, 0)),
            pl.BlockSpec((pair, width), lambda j: (d, 0)),
            constant((rows, width)),
            constant((rows, width)),
        ],
        scratch_shapes=[pltpu.VMEM((pair, width), LOW)],
        input_output_aliases={5 + i: i for i in range(len(kept))},
        compiler_params=pltpu.CompilerParams(vmem_limit_bytes=36 * MIB),
        cost_estimate=pl.CostEstimate(
            flops=8 * pair * width * units // COST,
            bytes_accessed=(4 * units * width + 16 * pair * width) // COST,
            transcendentals=0,
        ),
    )(*ins)


def weight_gradient_call(back, normed_all, upstream_all):
    _, total, units = back.shape
    width = normed_all.shape[1]
    steps = 1
    part = width // steps

    def kernel(back_ref, normed_ref, upstream_ref, out_ref):
        step = pl.program_id(0)

        @pl.when(step < 2 * steps)
        def _():
            out_ref[...] = dot(back_ref[0], normed_ref[...], 0, 0).astype(LOW)

        @pl.when(step >= 2 * steps)
        def _():
            out_ref[...] = dot(back_ref[0], upstream_ref[...], 0, 0).astype(LOW)

    return call(
        "weight_gradient",
        kernel,
        [((units, 3 * width), LOW)],
        [back, normed_all, upstream_all],
        grid=(3 * steps,),
        in_specs=[
            pl.BlockSpec((1, total, units), lambda j: (j // steps, 0, 0)),
            pl.BlockSpec((total, part), lambda j: (0, jnp.where(j < 2 * steps, j % steps, steps - 1))),
            pl.BlockSpec((total, part), lambda j: (0, jnp.maximum(j - 2 * steps, 0))),
        ],
        out_specs=[pl.BlockSpec((units, part), lambda j: (0, j))],
        limit=60,
        flops=6 * total * width * units,
    )[0]


def lifted_call(place, back, down, chips):
    _, total, units = back.shape
    width = down.shape[1]
    rows = total // (2 * chips)

    def kernel(place_ref, z_ref, down_ref, own_ref, other_ref, sum_ref):
        sum_ref[...] = dot(z_ref[0], down_ref[...]).astype(LOW)
        core = place_ref[2]
        own_ref[...] = sum_ref[pl.ds(pl.multiple_of(core * rows, 16), rows), :]
        other_ref[...] = sum_ref[pl.ds(pl.multiple_of((1 - core) * rows, 16), rows), :]

    return call(
        "lifted",
        kernel,
        [((total // 2, width), LOW)] * 2,
        [place, back, down],
        grid=(chips,),
        in_specs=[
            pl.BlockSpec(memory_space=pltpu.SMEM),
            pl.BlockSpec((1, 2 * rows, units), lambda j: (2, j, 0)),
            constant((units, width)),
        ],
        out_specs=[pl.BlockSpec((rows, width), lambda j: (j, 0))] * 2,
        scratch=[pltpu.VMEM((2 * rows, width), LOW)],
        flops=2 * total * width * units,
        far=(1,),
    )


def project_call(tokens, gain, weights, bias, cosine, sine, first, count, far=()):
    rows, width = tokens.shape
    heads = WEIGHT_BLOCK // HEAD_DIM

    def kernel(x_ref, gain_ref, w_ref, bias_ref, cos_ref, sin_ref, out_ref, n_ref):
        step = pl.program_id(0)

        @pl.when(step == 0)
        def _():
            x = x_ref[...].astype(FULL)
            n_ref[...] = (x * inverse_rms(x) * gain_ref[...]).astype(LOW)

        a = dot(n_ref[...], w_ref[...], 1, 1) + bias_ref[...]
        for h in range(heads):
            one = a[:, h * HEAD_DIM : (h + 1) * HEAD_DIM]
            turned = rotate(one, cos_ref[...], sin_ref[...])
            is_value = (first + step) * heads + h >= HEADS + KV_HEADS
            out_ref[:, h * HEAD_DIM : (h + 1) * HEAD_DIM] = jnp.where(
                is_value, one, turned
            ).astype(LOW)

    return call(
        "project",
        kernel,
        [((rows, count * WEIGHT_BLOCK), LOW)],
        [tokens, gain, weights, bias, cosine, sine],
        grid=(count,),
        in_specs=[
            constant((rows, width)),
            constant((1, width)),
            pl.BlockSpec((WEIGHT_BLOCK, width), lambda j: (first + j, 0)),
            pl.BlockSpec((1, WEIGHT_BLOCK), lambda j: (0, first + j)),
            constant((rows, HEAD_DIM)),
            constant((rows, HEAD_DIM)),
        ],
        out_specs=[pl.BlockSpec((rows, WEIGHT_BLOCK), lambda j: (0, j))],
        scratch=[pltpu.VMEM((rows, width), LOW)],
        limit=54,
        flops=2 * rows * width * count * WEIGHT_BLOCK,
        far=far,
    )[0]


def stacked(ref, kv_head):
    return jnp.concatenate(
        [
            ref[:, h * HEAD_DIM : (h + 1) * HEAD_DIM]
            for h in range(kv_head * GROUP, (kv_head + 1) * GROUP)
        ],
        axis=0,
    )


def masked_scores(query, key, mask):
    rows = mask.shape[0]
    raw = dot(query, key, 1, 1) * SCALE
    return (raw.reshape(GROUP, rows, -1) + mask[None]).reshape(raw.shape)


def output_weight_specs(width):
    first = PROJECTION_WIDTH // WEIGHT_BLOCK
    return [
        pl.BlockSpec((WEIGHT_BLOCK, width), lambda j, i=i: (first + i, 0))
        for i in range(QUERY_WIDTH // WEIGHT_BLOCK)
    ]


class Pieces:
    def __init__(self, own_rows, size):
        self.own_rows, self.size = own_rows, size
        starts = [f * own_rows // 128 * 128 for f in range(size)]
        self.wide = max(-(-((f + 1) * own_rows) // 128) * 128 - starts[f] for f in range(size))
        self.padded = max(starts) + self.wide

    def start_of(self, owner):
        return owner * self.own_rows // 128 * 128

    def start(self, owner):
        return pl.multiple_of(owner * self.own_rows // 128 * 128, 128)


def owner_at(place_ref, place):
    return (place_ref[1] ^ (place // 2)) * 2 + place % 2


def attend_call(query, kv_blocks, mask, tokens, weights, gain):
    rows, width = tokens.shape
    parts = len(kv_blocks)
    count = rows * parts
    weight_specs = output_weight_specs(width)
    blocks = len(weight_specs)

    def kernel(*refs):
        q_ref = refs[0]
        kv_refs = refs[1 : 1 + parts]
        mask_ref, x_ref, gain_ref = refs[1 + parts : 4 + parts]
        w_refs = refs[4 + parts : 4 + parts + blocks]
        lse_ref, h_ref, n_ref, kv_ref, m_ref = refs[4 + parts + blocks :]
        for i, ref in enumerate(kv_refs):
            kv_ref[pl.ds(i * rows, rows), :] = ref[...]
        for g in range(KV_HEADS):
            key = kv_ref[:, g * HEAD_DIM : (g + 1) * HEAD_DIM]
            value = kv_ref[:, KEY_WIDTH + g * HEAD_DIM : KEY_WIDTH + (g + 1) * HEAD_DIM]
            scores = masked_scores(stacked(q_ref, g), key, mask_ref[...])
            top = jnp.max(scores, axis=-1, keepdims=True)
            raised = jnp.exp(scores - top)
            total = jnp.sum(raised, axis=-1, keepdims=True)
            lse_ref[g] = top + jnp.log(total)
            mixed = dot((raised / total).astype(LOW), value).astype(LOW)
            for i in range(GROUP):
                at = (g * GROUP + i) * HEAD_DIM
                m_ref[:, at : at + HEAD_DIM] = mixed[i * rows : (i + 1) * rows]
        h = x_ref[...].astype(FULL)
        for i, w_ref in enumerate(w_refs):
            at = i * WEIGHT_BLOCK
            h = h + dot(m_ref[:, at : at + WEIGHT_BLOCK], w_ref[...])
        h_ref[...] = h
        n_ref[...] = (h * inverse_rms(h) * gain_ref[...]).astype(LOW)

    full = [constant((rows, QUERY_WIDTH))] + [constant((rows, 2 * KEY_WIDTH))] * parts
    return call(
        "attend",
        kernel,
        [
            ((KV_HEADS, GROUP * rows, 1), FULL),
            ((rows, width), FULL),
            ((rows, width), LOW),
            ((count, 2 * KEY_WIDTH), LOW),
            ((rows, QUERY_WIDTH), LOW),
        ],
        [query, *kv_blocks, mask, tokens, gain] + [weights] * blocks,
        grid=(1,),
        in_specs=full
        + [constant((rows, count)), constant((rows, width)), constant((1, width))]
        + weight_specs,
        out_specs=[
            constant((KV_HEADS, GROUP * rows, 1)),
            constant((rows, width)),
            constant((rows, width)),
            constant((count, 2 * KEY_WIDTH)),
            constant((rows, QUERY_WIDTH)),
        ],
        far=(2,),
        limit=54,
        flops=2 * rows * width * QUERY_WIDTH + 4 * rows * count * QUERY_WIDTH,
    )


def back_attend_call(terms, residual, upstream, gain, weights, query, kv, mask, lse, cosine, sine):
    rows, width = residual.shape
    count = kv.shape[0]
    parts = count // rows
    given = len(terms)
    weight_specs = output_weight_specs(width)
    blocks = len(weight_specs)

    def kernel(*refs):
        term_refs = refs[:given]
        h_ref, c_ref, gain_ref, q_ref, kv_ref, mask_ref, lse_ref, cos_ref, sin_ref = refs[
            given : given + 9
        ]
        w_refs = refs[given + 9 : given + 9 + blocks]
        dh_ref, db_ref, gain_back_ref, da_ref = refs[given + 9 + blocks : given + 13 + blocks]
        kv_back_refs = refs[given + 13 + blocks : given + 13 + blocks + parts]
        dm_ref = refs[-1]
        back = term_refs[0][...].astype(FULL)
        for ref in term_refs[1:]:
            back = back + ref[...].astype(FULL)
        h = h_ref[...]
        scale = inverse_rms(h)
        dh = c_ref[...].astype(FULL) + norm_backward(h, scale, gain_ref[...], back)
        gain_back_ref[...] = jnp.sum(back * h * scale, axis=0, keepdims=True)
        dh_ref[...] = dh
        db = dh.astype(LOW)
        db_ref[...] = db
        for i, w_ref in enumerate(w_refs):
            at = i * WEIGHT_BLOCK
            dm_ref[:, at : at + WEIGHT_BLOCK] = dot(db, w_ref[...], 1, 1).astype(LOW)
        for g in range(KV_HEADS):
            key = kv_ref[:, g * HEAD_DIM : (g + 1) * HEAD_DIM]
            value = kv_ref[:, KEY_WIDTH + g * HEAD_DIM : KEY_WIDTH + (g + 1) * HEAD_DIM]
            q = stacked(q_ref, g)
            dm = stacked(dm_ref, g)
            scores = masked_scores(q, key, mask_ref[...])
            probability = jnp.exp(scores - lse_ref[g])
            low = probability.astype(LOW)
            back_probability = dot(dm, value, 1, 1)
            delta = jnp.sum(low.astype(FULL) * back_probability, axis=-1, keepdims=True)
            back_scores = (probability * (back_probability - delta)).astype(LOW)
            back_query = dot(back_scores, key) * SCALE
            for i in range(GROUP):
                at = (g * GROUP + i) * HEAD_DIM
                da_ref[:, at : at + HEAD_DIM] = unrotate(
                    back_query[i * rows : (i + 1) * rows], cos_ref[...], sin_ref[...]
                ).astype(LOW)
            back_key = (dot(back_scores, q, 0, 0) * SCALE).astype(LOW)
            back_value = dot(low, dm, 0, 0).astype(LOW)
            for i, ref in enumerate(kv_back_refs):
                ref[:, g * HEAD_DIM : (g + 1) * HEAD_DIM] = back_key[i * rows : (i + 1) * rows]
                ref[:, KEY_WIDTH + g * HEAD_DIM : KEY_WIDTH + (g + 1) * HEAD_DIM] = back_value[
                    i * rows : (i + 1) * rows
                ]

    ins = [*terms, residual, upstream, gain, query, kv, mask, lse, cosine, sine]
    outs = [
        ((rows, width), FULL),
        ((rows, width), LOW),
        ((1, width), FULL),
        ((rows, QUERY_WIDTH), LOW),
    ] + [((rows, 2 * KEY_WIDTH), LOW)] * parts
    return call(
        "back_attend",
        kernel,
        outs,
        ins + [weights] * blocks,
        grid=(1,),
        in_specs=[constant(x.shape) for x in ins] + weight_specs,
        out_specs=[constant(shape) for shape, _ in outs],
        scratch=[pltpu.VMEM((rows, QUERY_WIDTH), LOW)],
        far=[1, *range(4, 4 + parts)],
        flops=2 * rows * width * QUERY_WIDTH + 10 * rows * count * QUERY_WIDTH,
    )


def back_project_call(
    terms, da_query, mixed, weights, tokens, back_residual, gain, gain_back, cosine, sine, pieces,
    bias_width, gain_width,
):
    rows, width = tokens.shape
    given = len(terms)
    owners = pieces.size
    span = 256

    def kernel(*refs):
        term_refs = refs[:given]
        daq_ref, m_ref, w_ref, x_ref, dh_ref, gain_ref, gain_back_ref, cos_ref, sin_ref = refs[
            given : 9 + given
        ]
        dx_ref, piece_ref = refs[9 + given : 11 + given]
        da_ref, small_ref = refs[-2:]
        back = term_refs[0][...].astype(FULL)
        for ref in term_refs[1:]:
            back = back + ref[...].astype(FULL)
        used = PROJECTION_WIDTH + QUERY_WIDTH
        da_ref[:, PROJECTION_WIDTH:used] = m_ref[...]
        if da_ref.shape[1] > used:
            da_ref[:, used:] = jnp.zeros_like(da_ref[:, used:])
        da_ref[:, :QUERY_WIDTH] = daq_ref[...]
        for g in range(KV_HEADS):
            at = QUERY_WIDTH + g * HEAD_DIM
            da_ref[:, at : at + HEAD_DIM] = unrotate(
                back[:, g * HEAD_DIM : (g + 1) * HEAD_DIM], cos_ref[...], sin_ref[...]
            ).astype(LOW)
        da_ref[:, QUERY_WIDTH + KEY_WIDTH : PROJECTION_WIDTH] = back[:, KEY_WIDTH:].astype(LOW)
        da = da_ref[:, :PROJECTION_WIDTH]
        x = x_ref[...].astype(FULL)
        scale = inverse_rms(x)
        back_normed = dot(da, w_ref[...])
        dx_ref[...] = dh_ref[...] + norm_backward(x, scale, gain_ref[...], back_normed)
        small_ref[...] = jnp.zeros_like(small_ref)
        small_ref[0:1, :PROJECTION_WIDTH] = jnp.sum(da.astype(FULL), axis=0, keepdims=True)
        small_ref[1:2, :width] = jnp.sum(back_normed * x * scale, axis=0, keepdims=True)
        small_ref[2:3, :width] = gain_back_ref[...]
        for owner in range(owners):
            start = pieces.start_of(owner)
            piece_ref[owner, :rows, :] = da_ref[:, start : start + pieces.wide]
            piece_ref[owner, rows:, :] = jnp.zeros_like(piece_ref[owner, rows:, :])
            bias_at = owner * bias_width // 128 * 128
            gain_at = owner * gain_width // 128 * 128
            small = jnp.concatenate(
                [
                    small_ref[0:1, bias_at : bias_at + span],
                    small_ref[1:3, gain_at : gain_at + span],
                    jnp.zeros((13, span), FULL),
                ],
                axis=0,
            )
            piece_ref[owner, rows:, :span] = small.astype(LOW)

    ins = [*terms, da_query, mixed]
    more = [tokens, back_residual, gain, gain_back, cosine, sine]
    outs = [((rows, width), FULL)] + [((owners, rows + 16, pieces.wide), LOW)]
    return call(
        "back_project",
        kernel,
        outs,
        [*ins, weights, *more],
        grid=(1,),
        in_specs=[constant(x.shape) for x in ins]
        + [pl.BlockSpec((PROJECTION_WIDTH, width), lambda j: (0, 0))]
        + [constant(x.shape) for x in more],
        out_specs=[constant(shape) for shape, _ in outs],
        scratch=[
            pltpu.VMEM((rows, max(pieces.padded, PROJECTION_WIDTH + QUERY_WIDTH)), LOW),
            pltpu.VMEM((8, PROJECTION_WIDTH + span), FULL),
        ],
        flops=2 * rows * width * PROJECTION_WIDTH,
        far=(1,),
    )


def normed_call(place, pairs, gain):
    pair, width = pairs[0].shape
    chips = len(pairs)

    def kernel(place_ref, *refs):
        gain_ref, out_ref = refs[-2:]
        for d in range(chips):
            x = refs[d][...].astype(FULL)
            at = pl.ds(pl.multiple_of((place_ref[1] ^ d) * pair, 16), pair)
            out_ref[at, :] = (x * inverse_rms(x) * gain_ref[...]).astype(LOW)

    return call(
        "normed",
        kernel,
        [((pair * chips, width), LOW)],
        [place, *pairs, gain],
        in_specs=[pl.BlockSpec(memory_space=pltpu.SMEM)]
        + [pl.BlockSpec(memory_space=pltpu.VMEM)] * (chips + 1),
    )[0]


def attention_gradient_call(place, columns, normed_all, db_pairs, pieces, contexts):
    pair, width = db_pairs[0].shape
    rows = pair // 2
    chips = len(db_pairs)
    count = 2 * chips
    quarter = pieces.own_rows // contexts
    total = rows * count
    wide = pieces.wide

    def kernel(*refs):
        place_ref = refs[0]
        columns_ref, n_ref = refs[1:3]
        db_refs = refs[3 : 3 + chips]
        out_refs = refs[3 + chips : 3 + chips + contexts]
        left_ref, right_ref, sum_ref, cut_ref = refs[3 + chips + contexts :]
        owner = place_ref[1] * 2 + place_ref[2]
        start = pieces.start(owner)
        small = jnp.zeros((16, wide), FULL)
        for i in range(count):
            left_ref[pl.ds(i * rows, rows), :] = columns_ref[i, :rows, :]
            small = small + columns_ref[i, rows:, :].astype(FULL)
        for d, ref in enumerate(db_refs):
            at = pl.multiple_of((place_ref[1] ^ d) * pair, 16)
            right_ref[pl.ds(at, pair), :] = ref[...]
        of_project = start + lax.broadcasted_iota(jnp.int32, (wide, width), 0) < PROJECTION_WIDTH
        sum_ref[...] = jnp.where(
            of_project, dot(left_ref[...], n_ref[...], 0, 0), dot(left_ref[...], right_ref[...], 0, 0)
        )
        offset = pl.multiple_of(
            owner * pieces.own_rows - start, math.gcd(pieces.own_rows, 128)
        )
        own = sum_ref[pl.ds(offset, pieces.own_rows), :].astype(LOW)
        for c in range(contexts):
            cut_ref[c] = own[c * quarter : (c + 1) * quarter]
        for d, out_ref in enumerate(out_refs):
            out_ref[:quarter, :] = cut_ref[place_ref[0] ^ d]
            out_ref[quarter:, :] = jnp.zeros_like(out_ref[quarter:, :])
            out_ref[quarter:, :wide] = small.astype(LOW)

    ins = [columns, normed_all, *db_pairs]
    outs = [((quarter + 16, width), LOW)] * contexts
    return call(
        "attention_gradient",
        kernel,
        outs,
        [place, *ins],
        in_specs=[pl.BlockSpec(memory_space=pltpu.SMEM)]
        + [pl.BlockSpec(memory_space=pltpu.VMEM)] * len(ins),
        scratch=[
            pltpu.VMEM((total, wide), LOW),
            pltpu.VMEM((total, width), LOW),
            pltpu.VMEM((wide, width), FULL),
            pltpu.VMEM((contexts, quarter, width), LOW),
        ],
        flops=4 * total * wide * width,
        far=range(contexts),
    )


def total_of(terms):
    result = terms[0].astype(FULL)
    for term in terms[1:]:
        result = result + term.astype(FULL)
    return result


def make(ring, contexts):
    def per_device(
        tokens,
        document_starts,
        attention_weights,
        projection_bias,
        norm_gains,
        hidden_weights,
        cotangent,
    ):
        rows, width = tokens.shape[1:]
        chips = ring.chips
        me = lax.axis_index("ctx")
        index = lax.axis_index("fsdp")
        place = jnp.stack([me, index // 2, index % 2]).astype(jnp.int32)
        own_rows = attention_weights.shape[0]
        quarter = own_rows // contexts
        pieces = Pieces(own_rows, ring.size)
        bias_width = projection_bias.shape[0]
        gain_width = norm_gains.shape[1]

        weight_piece = lax.dynamic_slice_in_dim(attention_weights, me * quarter, quarter, 0)
        weights = lax.all_gather(weight_piece.astype(LOW), ("fsdp", "ctx"), axis=0, tiled=True)

        packed = jnp.concatenate([projection_bias, norm_gains.reshape(-1)]).astype(LOW)
        packed = jnp.pad(packed[None], ((0, 15), (0, width - packed.shape[0])))
        upstream = cotangent[0]
        upstream_pairs = [
            ring.both(b) for b in ring.chained(jnp.concatenate([upstream, packed], axis=0))
        ]
        params = jnp.stack([p.reshape(2, -1, width)[:, rows] for p in upstream_pairs])
        params = params.reshape(ring.size, width)
        owners = jnp.arange(ring.size, dtype=jnp.int32)
        at = owners ^ (index // 2 * 2)
        params = jnp.dot(
            (at[:, None] == owners[None, :]).astype(LOW), params, preferred_element_type=FULL
        )
        bias = params[:, :bias_width].reshape(1, -1)
        gain_one = params[:, bias_width : bias_width + gain_width].reshape(1, -1)
        gain_two = params[:, bias_width + gain_width : bias_width + 2 * gain_width].reshape(1, -1)

        starts = document_starts[0]
        within = jnp.arange(rows, dtype=jnp.int32)
        positions = me * rows + within
        cosine, sine = rope_tables(positions, HEAD_DIM)
        key_positions = jnp.concatenate([(me ^ d) * rows + within for d in range(contexts)])
        mask = jnp.where(
            (segments(starts, positions)[:, None] == segments(starts, key_positions)[None, :])
            & (key_positions[None, :] <= positions[:, None]),
            0.0,
            LOWEST,
        ).astype(FULL)

        gate_rows, up_rows, down_rows = cast_call(hidden_weights)
        back_hidden, upstream_all = back_hidden_call(upstream_pairs, down_rows, rows)
        weights, back_hidden, mask, cosine, sine, bias, gain_one, gain_two = (
            lax.optimization_barrier(
                (weights, back_hidden, mask, cosine, sine, bias, gain_one, gain_two)
            )
        )
        tokens_ahead = ring.begun(after(tokens[0], weights))
        blocks = QUERY_WIDTH // WEIGHT_BLOCK
        kv = project_call(
            tokens[0], gain_one, weights, bias, cosine, sine, blocks, 2 * KEY_WIDTH // WEIGHT_BLOCK,
            far=(0,),
        )
        query = project_call(
            after(tokens[0], kv), gain_one, weights, bias, cosine, sine, 0, blocks
        )
        kv_blocks = context_send([kv] * contexts, contexts)
        lse, residual, normed_two, kv_all, mixed = attend_call(
            query, kv_blocks, mask, tokens[0], weights, gain_two
        )

        kept, back_normed_terms = (), []
        ahead = ring.ahead(after(normed_two, *tokens_ahead[1:3]))
        done = ()
        for d in range(chips):
            *kept, own, other = feed_call(
                d, chips, place, ring.both(after(ahead[d], *done)), back_hidden, gate_rows,
                up_rows, kept,
            )
            summed = add_parts(place, own, ring.both(other), 1)[0]
            done = (summed, *back_normed_terms[1:][-1:])
            if d == 3:
                tokens_ahead += ring.rest(tokens_ahead, summed)
            back_normed_terms.append(ring.send(summed, d) if d else summed)
        back, normed_all = kept
        back = after(back, summed)
        hidden_term = weight_gradient_call(back, normed_all, upstream_all)
        hidden_shard = lax.psum_scatter(
            after(hidden_term, *back_normed_terms[-2:]), "ctx", scatter_dimension=0, tiled=True
        ).astype(FULL)
        back_normed_terms[0] = after(back_normed_terms[0], hidden_term)
        back_residual, back_branch, back_gain_two, da_query, *kv_back = back_attend_call(
            back_normed_terms, residual, upstream, gain_two, weights, query, kv_all, mask, lse,
            cosine, sine,
        )
        kv_terms = context_send(kv_back, contexts)
        branch_ahead = ring.ahead(back_branch)
        token_pairs = [ring.both(after(b, da_query)) for b in tokens_ahead]
        da_query = after(da_query, *token_pairs, *branch_ahead[1:3])
        back_inputs, projected_pieces = back_project_call(
            kv_terms, da_query, mixed, weights, tokens[0], back_residual, gain_one,
            back_gain_two, cosine, sine, pieces, bias_width, gain_width,
        )
        columns = lax.all_to_all(
            after(projected_pieces, *branch_ahead[1:]), "fsdp", 0, 0, tiled=True
        )
        lifted_own, lifted_other = lifted_call(place, after(back, projected_pieces), down_rows, chips)
        lifted_terms = add_parts(place, lifted_own, ring.send(lifted_other, 0, 1), chips)
        normed_one_all = normed_call(place, token_pairs, after(gain_one, lifted_terms[0]))
        branch_pairs = [ring.both(after(b, lifted_terms[0])) for b in branch_ahead]
        lifted_terms = [ring.send(block, d) if d else block for d, block in enumerate(lifted_terms)]
        output = (residual + total_of(lifted_terms)).astype(LOW)
        attention_terms = attention_gradient_call(
            place, columns, normed_one_all, branch_pairs, pieces, contexts
        )
        attention_terms = context_send(attention_terms, contexts)
        shards = total_of([after(attention_terms[0], output, hidden_shard), *attention_terms[1:]])
        own_bias = bias_width // contexts
        own_gain = gain_width // contexts
        bias_at = index * bias_width % 128 + me * own_bias
        gain_at = index * gain_width % 128 + me * own_gain
        bias_shard = lax.dynamic_slice(shards, (quarter, bias_at), (1, own_bias))[0]
        gain_shard = lax.dynamic_slice(shards, (quarter + 1, gain_at), (2, own_gain))
        return (
            output[None],
            back_inputs[None],
            shards[:quarter],
            bias_shard,
            gain_shard,
            hidden_shard,
        )

    return per_device


def solution(mesh):
    placed = (
        P("fsdp", "ctx", None),
        P("fsdp", None),
        P("fsdp", None),
        P("fsdp"),
        P(None, "fsdp"),
        P("fsdp", None),
        P("fsdp", "ctx", None),
    )
    return jax.shard_map(
        make(Ring(mesh.shape["fsdp"]), mesh.shape["ctx"]),
        mesh=mesh,
        in_specs=placed,
        out_specs=(
            P("fsdp", "ctx", None),
            P("fsdp", "ctx", None),
            P(("fsdp", "ctx"), None),
            P(("fsdp", "ctx")),
            P(None, ("fsdp", "ctx")),
            P(("fsdp", "ctx"), None),
        ),
        check_vma=False,
    )
```

```python
import math

import jax
import jax.numpy as jnp
from jax import lax
from jax.experimental import pallas as pl
from jax.experimental.pallas import tpu as pltpu
from jax.sharding import PartitionSpec as P

HEADS = 12
KV_HEADS = 2
HEAD_DIM = 128
GROUP = HEADS // KV_HEADS
QUERY_WIDTH = HEADS * HEAD_DIM
KEY_WIDTH = KV_HEADS * HEAD_DIM
PROJECTION_WIDTH = QUERY_WIDTH + 2 * KEY_WIDTH
SCALE = HEAD_DIM ** (-0.5)
WEIGHT_BLOCK = 512

EPSILON = 1e-06
THETA = 10000.0
LOWEST = -1e30
LOW = jnp.bfloat16
FULL = jnp.float32
MIB = 2**20
COST = 1


def rope_tables(positions, width):
    half = width // 2
    frequency = THETA ** (-(jnp.arange(half, dtype=jnp.float32) * 2.0 / width))
    angle = positions.astype(jnp.float32)[:, None] * frequency[None, :]
    cosine = jnp.concatenate([jnp.cos(angle), jnp.cos(angle)], axis=1)
    sine = jnp.concatenate([jnp.sin(angle), jnp.sin(angle)], axis=1)
    return (cosine, sine)


def turn(vector):
    half = vector.shape[-1] // 2
    return jnp.concatenate([-vector[:, half:], vector[:, :half]], axis=1)


def rotate(vector, cosine, sine):
    return vector * cosine + turn(vector) * sine


def unrotate(gradient, cosine, sine):
    return gradient * cosine - turn(gradient * sine)


def segments(starts, positions):
    return jnp.sum((starts[None, :] <= positions[:, None]).astype(jnp.int32), axis=1) - 1


def inverse_rms(values):
    return lax.rsqrt(jnp.mean(values * values, axis=-1, keepdims=True) + EPSILON)


def norm_backward(inputs, scale, gain, back_normed):
    weighted = back_normed * gain
    return scale * weighted - inputs * (
        scale * scale * scale * jnp.mean(inputs * weighted, axis=-1, keepdims=True)
    )


def dot(left, right, left_dim=1, right_dim=0):
    return lax.dot_general(
        left, right, (((left_dim,), (right_dim,)), ((), ())), preferred_element_type=FULL
    )


def call(
    name, kernel, outs, ins, grid=None, in_specs=None, out_specs=None, scratch=(), flops=0, limit=60,
    far=(),
):
    shapes = [
        pltpu.HBM(shape, kind) if i in far else jax.ShapeDtypeStruct(shape, kind)
        for i, (shape, kind) in enumerate(outs)
    ]
    whole = pl.BlockSpec(memory_space=pltpu.VMEM)
    moved = sum(x.size * x.dtype.itemsize for x in ins) + sum(
        math.prod(shape) * jnp.dtype(kind).itemsize for shape, kind in outs
    )
    options = dict(grid=grid) if grid else {}
    return pl.pallas_call(
        kernel,
        name=name,
        out_shape=shapes,
        in_specs=in_specs or [whole] * len(ins),
        out_specs=out_specs or [whole] * len(outs),
        scratch_shapes=list(scratch),
        compiler_params=pltpu.CompilerParams(vmem_limit_bytes=limit * MIB),
        cost_estimate=pl.CostEstimate(
            flops=flops // COST, bytes_accessed=moved // COST, transcendentals=0
        ),
        **options,
    )(*ins)


def after(value, *others):
    return lax.optimization_barrier((value, *others))[0]


def constant(shape):
    return pl.BlockSpec(shape, lambda *_: (0,) * len(shape))


class Ring:
    def __init__(self, size):
        self.size = size
        self.chips = size // 2

    def send(self, block, chips, cores=0, to=None):
        moves = [(i, i ^ (2 * chips + cores)) for i in range(self.size)]
        if to is not None:
            moves = [(i, j) for i, j in moves if j // 2 in to]
        return lax.ppermute(block, "fsdp", moves)

    def both(self, block):
        pairs = [[i, i + 1] for i in range(0, self.size, 2)]
        return lax.all_gather(block, "fsdp", axis=0, tiled=True, axis_index_groups=pairs)

    def ahead(self, block, to=None):
        return [block] + [self.send(block, d, 0, to) for d in range(1, self.chips)]

    def chained(self, block):
        blocks = self.begun(block)
        return blocks + self.rest(blocks)

    def begun(self, block):
        if self.chips != 4:
            return self.ahead(block)
        two = self.send(block, 2)
        return [block, self.send(block, 1), two]

    def rest(self, blocks, *others):
        return [] if len(blocks) == self.chips else [self.send(after(blocks[2], *others), 1)]


def add_parts(place, own, both, count):
    total, width = own.shape
    rows = total // count
    first = both.shape[0] - total

    def kernel(place_ref, own_ref, both_ref, *out_refs):
        for d, out_ref in enumerate(out_refs):
            at = pl.multiple_of((1 - place_ref[2]) * first + d * rows, 16)
            got = both_ref[pl.ds(at, rows), :].astype(FULL)
            out_ref[...] = (own_ref[d * rows : (d + 1) * rows, :].astype(FULL) + got).astype(LOW)

    return call(
        "add_parts",
        kernel,
        [((rows, width), LOW)] * count,
        [place, own, both],
        in_specs=[pl.BlockSpec(memory_space=pltpu.SMEM)]
        + [pl.BlockSpec(memory_space=pltpu.VMEM)] * 2,
        limit=24,
        far=range(count),
    )


def context_send(blocks, count):
    return [blocks[0]] + [
        lax.ppermute(blocks[d], "ctx", [(i, i ^ d) for i in range(count)]) for d in range(1, count)
    ]


def cast_call(hidden_weights):
    units, width = hidden_weights.shape[0], hidden_weights.shape[1] // 3
    chunk = max(c for c in range(16, 257, 16) if units % c == 0)

    def kernel(w_ref, *out_refs):
        for i, ref in enumerate(out_refs):
            ref[...] = w_ref[:, i * width : (i + 1) * width].astype(LOW)

    return call(
        "cast",
        kernel,
        [((units, width), LOW)] * 3,
        [hidden_weights],
        grid=(units // chunk,),
        in_specs=[pl.BlockSpec((chunk, 3 * width), lambda j: (j, 0))],
        out_specs=[pl.BlockSpec((chunk, width), lambda j: (j, 0))] * 3,
        limit=24,
    )


def back_hidden_call(pairs, down, rows):
    pair_rows, width = pairs[0].shape
    units = down.shape[0]
    chips = len(pairs)
    second = pair_rows // 2

    def kernel(*refs):
        down_ref, e_ref, all_ref = refs[-3:]
        for d in range(chips):

            @pl.when(pl.program_id(0) == d)
            def _():
                all_ref[:rows, :] = refs[d][:rows, :]
                all_ref[rows:, :] = refs[d][second : second + rows, :]

        e_ref[...] = dot(all_ref[...], down_ref[...], 1, 1).astype(LOW)

    return call(
        "back_hidden",
        kernel,
        [((2 * chips * rows, units), LOW), ((2 * chips * rows, width), LOW)],
        [*pairs, down],
        grid=(chips,),
        in_specs=[constant((pair_rows, width))] * chips + [constant((units, width))],
        out_specs=[
            pl.BlockSpec((2 * rows, units), lambda j: (j, 0)),
            pl.BlockSpec((2 * rows, width), lambda j: (j, 0)),
        ],
        flops=4 * chips * rows * width * units,
        limit=32,
    )


def feed_call(d, chips, place, tokens, back_hidden, gate_rows, up_rows, kept):
    pair, width = tokens.shape
    units = gate_rows.shape[0]
    rows = pair // 2

    def kernel(*refs):
        place_ref, tokens_ref, e_ref, gate_ref, up_ref = refs[:5]
        back_ref, all_ref, own_ref, other_ref, sum_ref = refs[-5:]
        normed = tokens_ref[...]
        all_ref[...] = normed
        gate = dot(normed, gate_ref[...], 1, 1)
        up = dot(normed, up_ref[...], 1, 1)
        back = e_ref[...].astype(FULL)
        sigmoid = jax.nn.sigmoid(gate)
        silu = gate * sigmoid
        back_ref[2] = (silu * up).astype(LOW)
        back_ref[1] = (back * silu).astype(LOW)
        back_ref[0] = (back * up * (sigmoid * (1.0 + gate * (1.0 - sigmoid)))).astype(LOW)
        sum_ref[...] = (dot(back_ref[0], gate_ref[...]) + dot(back_ref[1], up_ref[...])).astype(LOW)
        core = place_ref[2]
        own_ref[...] = sum_ref[pl.ds(pl.multiple_of(core * rows, 16), rows), :]
        other_ref[...] = sum_ref[pl.ds(pl.multiple_of((1 - core) * rows, 16), rows), :]

    ins = [place, tokens, back_hidden, gate_rows, up_rows, *kept]
    outs = [
        ((3, chips * pair, units), LOW),
        ((chips * pair, width), LOW),
        ((rows, width), LOW),
        ((rows, width), LOW),
    ]
    return pl.pallas_call(
        kernel,
        name="feed",
        grid=(1,),
        out_shape=[jax.ShapeDtypeStruct(shape, kind) for shape, kind in outs],
        in_specs=[
            pl.BlockSpec(memory_space=pltpu.SMEM),
            constant((pair, width)),
            pl.BlockSpec((pair, units), lambda j: (d, 0)),
        ]
        + [constant((units, width))] * 2
        + [pl.BlockSpec(memory_space=pl.ANY)] * len(kept),
        out_specs=[
            pl.BlockSpec((3, pair, units), lambda j: (0, d, 0)),
            pl.BlockSpec((pair, width), lambda j: (d, 0)),
            constant((rows, width)),
            constant((rows, width)),
        ],
        scratch_shapes=[pltpu.VMEM((pair, width), LOW)],
        input_output_aliases={5 + i: i for i in range(len(kept))},
        compiler_params=pltpu.CompilerParams(vmem_limit_bytes=36 * MIB),
        cost_estimate=pl.CostEstimate(
            flops=8 * pair * width * units // COST,
            bytes_accessed=(4 * units * width + 16 * pair * width) // COST,
            transcendentals=0,
        ),
    )(*ins)


def weight_gradient_call(back, normed_all, upstream_all):
    _, total, units = back.shape
    width = normed_all.shape[1]
    steps = 1
    part = width // steps

    def kernel(back_ref, normed_ref, upstream_ref, out_ref):
        step = pl.program_id(0)

        @pl.when(step < 2 * steps)
        def _():
            out_ref[...] = dot(back_ref[0], normed_ref[...], 0, 0).astype(LOW)

        @pl.when(step >= 2 * steps)
        def _():
            out_ref[...] = dot(back_ref[0], upstream_ref[...], 0, 0).astype(LOW)

    return call(
        "weight_gradient",
        kernel,
        [((units, 3 * width), LOW)],
        [back, normed_all, upstream_all],
        grid=(3 * steps,),
        in_specs=[
            pl.BlockSpec((1, total, units), lambda j: (j // steps, 0, 0)),
            pl.BlockSpec((total, part), lambda j: (0, jnp.where(j < 2 * steps, j % steps, steps - 1))),
            pl.BlockSpec((total, part), lambda j: (0, jnp.maximum(j - 2 * steps, 0))),
        ],
        out_specs=[pl.BlockSpec((units, part), lambda j: (0, j))],
        limit=60,
        flops=6 * total * width * units,
    )[0]


def lifted_call(place, back, down, chips):
    _, total, units = back.shape
    width = down.shape[1]
    rows = total // (2 * chips)

    def kernel(place_ref, z_ref, down_ref, own_ref, other_ref, sum_ref):
        sum_ref[...] = dot(z_ref[0], down_ref[...]).astype(LOW)
        core = place_ref[2]
        own_ref[...] = sum_ref[pl.ds(pl.multiple_of(core * rows, 16), rows), :]
        other_ref[...] = sum_ref[pl.ds(pl.multiple_of((1 - core) * rows, 16), rows), :]

    return call(
        "lifted",
        kernel,
        [((total // 2, width), LOW)] * 2,
        [place, back, down],
        grid=(chips,),
        in_specs=[
            pl.BlockSpec(memory_space=pltpu.SMEM),
            pl.BlockSpec((1, 2 * rows, units), lambda j: (2, j, 0)),
            constant((units, width)),
        ],
        out_specs=[pl.BlockSpec((rows, width), lambda j: (j, 0))] * 2,
        scratch=[pltpu.VMEM((2 * rows, width), LOW)],
        flops=2 * total * width * units,
        far=(1,),
    )


def project_call(tokens, gain, weights, bias, cosine, sine, first, count, far=()):
    rows, width = tokens.shape
    heads = WEIGHT_BLOCK // HEAD_DIM

    def kernel(x_ref, gain_ref, w_ref, bias_ref, cos_ref, sin_ref, out_ref, n_ref):
        step = pl.program_id(0)

        @pl.when(step == 0)
        def _():
            x = x_ref[...].astype(FULL)
            n_ref[...] = (x * inverse_rms(x) * gain_ref[...]).astype(LOW)

        a = dot(n_ref[...], w_ref[...], 1, 1) + bias_ref[...]
        for h in range(heads):
            one = a[:, h * HEAD_DIM : (h + 1) * HEAD_DIM]
            turned = rotate(one, cos_ref[...], sin_ref[...])
            is_value = (first + step) * heads + h >= HEADS + KV_HEADS
            out_ref[:, h * HEAD_DIM : (h + 1) * HEAD_DIM] = jnp.where(
                is_value, one, turned
            ).astype(LOW)

    return call(
        "project",
        kernel,
        [((rows, count * WEIGHT_BLOCK), LOW)],
        [tokens, gain, weights, bias, cosine, sine],
        grid=(count,),
        in_specs=[
            constant((rows, width)),
            constant((1, width)),
            pl.BlockSpec((WEIGHT_BLOCK, width), lambda j: (first + j, 0)),
            pl.BlockSpec((1, WEIGHT_BLOCK), lambda j: (0, first + j)),
            constant((rows, HEAD_DIM)),
            constant((rows, HEAD_DIM)),
        ],
        out_specs=[pl.BlockSpec((rows, WEIGHT_BLOCK), lambda j: (0, j))],
        scratch=[pltpu.VMEM((rows, width), LOW)],
        limit=54,
        flops=2 * rows * width * count * WEIGHT_BLOCK,
        far=far,
    )[0]


def stacked(ref, kv_head):
    return jnp.concatenate(
        [
            ref[:, h * HEAD_DIM : (h + 1) * HEAD_DIM]
            for h in range(kv_head * GROUP, (kv_head + 1) * GROUP)
        ],
        axis=0,
    )


def masked_scores(query, key, mask):
    rows = mask.shape[0]
    raw = dot(query, key, 1, 1) * SCALE
    return (raw.reshape(GROUP, rows, -1) + mask[None]).reshape(raw.shape)


def output_weight_specs(width):
    first = PROJECTION_WIDTH // WEIGHT_BLOCK
    return [
        pl.BlockSpec((WEIGHT_BLOCK, width), lambda j, i=i: (first + i, 0))
        for i in range(QUERY_WIDTH // WEIGHT_BLOCK)
    ]


class Pieces:
    def __init__(self, own_rows, size):
        self.own_rows, self.size = own_rows, size
        starts = [f * own_rows // 128 * 128 for f in range(size)]
        self.wide = max(-(-((f + 1) * own_rows) // 128) * 128 - starts[f] for f in range(size))
        self.padded = max(starts) + self.wide

    def start_of(self, owner):
        return owner * self.own_rows // 128 * 128

    def start(self, owner):
        return pl.multiple_of(owner * self.own_rows // 128 * 128, 128)


def owner_at(place_ref, place):
    return (place_ref[1] ^ (place // 2)) * 2 + place % 2


def attend_call(query, kv_blocks, mask, tokens, weights, gain):
    rows, width = tokens.shape
    parts = len(kv_blocks)
    count = rows * parts
    weight_specs = output_weight_specs(width)
    blocks = len(weight_specs)

    def kernel(*refs):
        q_ref = refs[0]
        kv_refs = refs[1 : 1 + parts]
        mask_ref, x_ref, gain_ref = refs[1 + parts : 4 + parts]
        w_refs = refs[4 + parts : 4 + parts + blocks]
        lse_ref, h_ref, n_ref, kv_ref, m_ref = refs[4 + parts + blocks :]
        for i, ref in enumerate(kv_refs):
            kv_ref[pl.ds(i * rows, rows), :] = ref[...]
        for g in range(KV_HEADS):
            key = kv_ref[:, g * HEAD_DIM : (g + 1) * HEAD_DIM]
            value = kv_ref[:, KEY_WIDTH + g * HEAD_DIM : KEY_WIDTH + (g + 1) * HEAD_DIM]
            scores = masked_scores(stacked(q_ref, g), key, mask_ref[...])
            top = jnp.max(scores, axis=-1, keepdims=True)
            raised = jnp.exp(scores - top)
            total = jnp.sum(raised, axis=-1, keepdims=True)
            lse_ref[g] = top + jnp.log(total)
            mixed = dot((raised / total).astype(LOW), value).astype(LOW)
            for i in range(GROUP):
                at = (g * GROUP + i) * HEAD_DIM
                m_ref[:, at : at + HEAD_DIM] = mixed[i * rows : (i + 1) * rows]
        h = x_ref[...].astype(FULL)
        for i, w_ref in enumerate(w_refs):
            at = i * WEIGHT_BLOCK
            h = h + dot(m_ref[:, at : at + WEIGHT_BLOCK], w_ref[...])
        h_ref[...] = h
        n_ref[...] = (h * inverse_rms(h) * gain_ref[...]).astype(LOW)

    full = [constant((rows, QUERY_WIDTH))] + [constant((rows, 2 * KEY_WIDTH))] * parts
    return call(
        "attend",
        kernel,
        [
            ((KV_HEADS, GROUP * rows, 1), FULL),
            ((rows, width), FULL),
            ((rows, width), LOW),
            ((count, 2 * KEY_WIDTH), LOW),
            ((rows, QUERY_WIDTH), LOW),
        ],
        [query, *kv_blocks, mask, tokens, gain] + [weights] * blocks,
        grid=(1,),
        in_specs=full
        + [constant((rows, count)), constant((rows, width)), constant((1, width))]
        + weight_specs,
        out_specs=[
            constant((KV_HEADS, GROUP * rows, 1)),
            constant((rows, width)),
            constant((rows, width)),
            constant((count, 2 * KEY_WIDTH)),
            constant((rows, QUERY_WIDTH)),
        ],
        far=(2,),
        limit=54,
        flops=2 * rows * width * QUERY_WIDTH + 4 * rows * count * QUERY_WIDTH,
    )


def back_attend_call(terms, residual, upstream, gain, weights, query, kv, mask, lse, cosine, sine):
    rows, width = residual.shape
    count = kv.shape[0]
    parts = count // rows
    given = len(terms)
    weight_specs = output_weight_specs(width)
    blocks = len(weight_specs)

    def kernel(*refs):
        term_refs = refs[:given]
        h_ref, c_ref, gain_ref, q_ref, kv_ref, mask_ref, lse_ref, cos_ref, sin_ref = refs[
            given : given + 9
        ]
        w_refs = refs[given + 9 : given + 9 + blocks]
        dh_ref, db_ref, gain_back_ref, da_ref = refs[given + 9 + blocks : given + 13 + blocks]
        kv_back_refs = refs[given + 13 + blocks : given + 13 + blocks + parts]
        dm_ref = refs[-1]
        back = term_refs[0][...].astype(FULL)
        for ref in term_refs[1:]:
            back = back + ref[...].astype(FULL)
        h = h_ref[...]
        scale = inverse_rms(h)
        dh = c_ref[...].astype(FULL) + norm_backward(h, scale, gain_ref[...], back)
        gain_back_ref[...] = jnp.sum(back * h * scale, axis=0, keepdims=True)
        dh_ref[...] = dh
        db = dh.astype(LOW)
        db_ref[...] = db
        for i, w_ref in enumerate(w_refs):
            at = i * WEIGHT_BLOCK
            dm_ref[:, at : at + WEIGHT_BLOCK] = dot(db, w_ref[...], 1, 1).astype(LOW)
        for g in range(KV_HEADS):
            key = kv_ref[:, g * HEAD_DIM : (g + 1) * HEAD_DIM]
            value = kv_ref[:, KEY_WIDTH + g * HEAD_DIM : KEY_WIDTH + (g + 1) * HEAD_DIM]
            q = stacked(q_ref, g)
            dm = stacked(dm_ref, g)
            scores = masked_scores(q, key, mask_ref[...])
            probability = jnp.exp(scores - lse_ref[g])
            low = probability.astype(LOW)
            back_probability = dot(dm, value, 1, 1)
            delta = jnp.sum(low.astype(FULL) * back_probability, axis=-1, keepdims=True)
            back_scores = (probability * (back_probability - delta)).astype(LOW)
            back_query = dot(back_scores, key) * SCALE
            for i in range(GROUP):
                at = (g * GROUP + i) * HEAD_DIM
                da_ref[:, at : at + HEAD_DIM] = unrotate(
                    back_query[i * rows : (i + 1) * rows], cos_ref[...], sin_ref[...]
                ).astype(LOW)
            back_key = (dot(back_scores, q, 0, 0) * SCALE).astype(LOW)
            back_value = dot(low, dm, 0, 0).astype(LOW)
            for i, ref in enumerate(kv_back_refs):
                ref[:, g * HEAD_DIM : (g + 1) * HEAD_DIM] = back_key[i * rows : (i + 1) * rows]
                ref[:, KEY_WIDTH + g * HEAD_DIM : KEY_WIDTH + (g + 1) * HEAD_DIM] = back_value[
                    i * rows : (i + 1) * rows
                ]

    ins = [*terms, residual, upstream, gain, query, kv, mask, lse, cosine, sine]
    outs = [
        ((rows, width), FULL),
        ((rows, width), LOW),
        ((1, width), FULL),
        ((rows, QUERY_WIDTH), LOW),
    ] + [((rows, 2 * KEY_WIDTH), LOW)] * parts
    return call(
        "back_attend",
        kernel,
        outs,
        ins + [weights] * blocks,
        grid=(1,),
        in_specs=[constant(x.shape) for x in ins] + weight_specs,
        out_specs=[constant(shape) for shape, _ in outs],
        scratch=[pltpu.VMEM((rows, QUERY_WIDTH), LOW)],
        far=[1, *range(4, 4 + parts)],
        flops=2 * rows * width * QUERY_WIDTH + 10 * rows * count * QUERY_WIDTH,
    )


def back_project_call(
    terms, da_query, mixed, weights, tokens, back_residual, gain, gain_back, cosine, sine, pieces,
    bias_width, gain_width,
):
    rows, width = tokens.shape
    given = len(terms)
    owners = pieces.size
    span = 256

    def kernel(*refs):
        term_refs = refs[:given]
        daq_ref, m_ref, w_ref, x_ref, dh_ref, gain_ref, gain_back_ref, cos_ref, sin_ref = refs[
            given : 9 + given
        ]
        dx_ref, piece_ref = refs[9 + given : 11 + given]
        da_ref, small_ref = refs[-2:]
        back = term_refs[0][...].astype(FULL)
        for ref in term_refs[1:]:
            back = back + ref[...].astype(FULL)
        used = PROJECTION_WIDTH + QUERY_WIDTH
        da_ref[:, PROJECTION_WIDTH:used] = m_ref[...]
        if da_ref.shape[1] > used:
            da_ref[:, used:] = jnp.zeros_like(da_ref[:, used:])
        da_ref[:, :QUERY_WIDTH] = daq_ref[...]
        for g in range(KV_HEADS):
            at = QUERY_WIDTH + g * HEAD_DIM
            da_ref[:, at : at + HEAD_DIM] = unrotate(
                back[:, g * HEAD_DIM : (g + 1) * HEAD_DIM], cos_ref[...], sin_ref[...]
            ).astype(LOW)
        da_ref[:, QUERY_WIDTH + KEY_WIDTH : PROJECTION_WIDTH] = back[:, KEY_WIDTH:].astype(LOW)
        da = da_ref[:, :PROJECTION_WIDTH]
        x = x_ref[...].astype(FULL)
        scale = inverse_rms(x)
        back_normed = dot(da, w_ref[...])
        dx_ref[...] = dh_ref[...] + norm_backward(x, scale, gain_ref[...], back_normed)
        small_ref[...] = jnp.zeros_like(small_ref)
        small_ref[0:1, :PROJECTION_WIDTH] = jnp.sum(da.astype(FULL), axis=0, keepdims=True)
        small_ref[1:2, :width] = jnp.sum(back_normed * x * scale, axis=0, keepdims=True)
        small_ref[2:3, :width] = gain_back_ref[...]
        for owner in range(owners):
            start = pieces.start_of(owner)
            piece_ref[owner, :rows, :] = da_ref[:, start : start + pieces.wide]
            piece_ref[owner, rows:, :] = jnp.zeros_like(piece_ref[owner, rows:, :])
            bias_at = owner * bias_width // 128 * 128
            gain_at = owner * gain_width // 128 * 128
            small = jnp.concatenate(
                [
                    small_ref[0:1, bias_at : bias_at + span],
                    small_ref[1:3, gain_at : gain_at + span],
                    jnp.zeros((13, span), FULL),
                ],
                axis=0,
            )
            piece_ref[owner, rows:, :span] = small.astype(LOW)

    ins = [*terms, da_query, mixed]
    more = [tokens, back_residual, gain, gain_back, cosine, sine]
    outs = [((rows, width), FULL)] + [((owners, rows + 16, pieces.wide), LOW)]
    return call(
        "back_project",
        kernel,
        outs,
        [*ins, weights, *more],
        grid=(1,),
        in_specs=[constant(x.shape) for x in ins]
        + [pl.BlockSpec((PROJECTION_WIDTH, width), lambda j: (0, 0))]
        + [constant(x.shape) for x in more],
        out_specs=[constant(shape) for shape, _ in outs],
        scratch=[
            pltpu.VMEM((rows, max(pieces.padded, PROJECTION_WIDTH + QUERY_WIDTH)), LOW),
            pltpu.VMEM((8, PROJECTION_WIDTH + span), FULL),
        ],
        flops=2 * rows * width * PROJECTION_WIDTH,
        far=(1,),
    )


def normed_call(place, pairs, gain):
    pair, width = pairs[0].shape
    chips = len(pairs)

    def kernel(place_ref, *refs):
        gain_ref, out_ref = refs[-2:]
        for d in range(chips):
            x = refs[d][...].astype(FULL)
            at = pl.ds(pl.multiple_of((place_ref[1] ^ d) * pair, 16), pair)
            out_ref[at, :] = (x * inverse_rms(x) * gain_ref[...]).astype(LOW)

    return call(
        "normed",
        kernel,
        [((pair * chips, width), LOW)],
        [place, *pairs, gain],
        in_specs=[pl.BlockSpec(memory_space=pltpu.SMEM)]
        + [pl.BlockSpec(memory_space=pltpu.VMEM)] * (chips + 1),
    )[0]


def attention_gradient_call(place, columns, normed_all, db_pairs, pieces, contexts):
    pair, width = db_pairs[0].shape
    rows = pair // 2
    chips = len(db_pairs)
    count = 2 * chips
    quarter = pieces.own_rows // contexts
    total = rows * count
    wide = pieces.wide

    def kernel(*refs):
        place_ref = refs[0]
        columns_ref, n_ref = refs[1:3]
        db_refs = refs[3 : 3 + chips]
        out_refs = refs[3 + chips : 3 + chips + contexts]
        left_ref, right_ref, sum_ref, cut_ref = refs[3 + chips + contexts :]
        owner = place_ref[1] * 2 + place_ref[2]
        start = pieces.start(owner)
        small = jnp.zeros((16, wide), FULL)
        for i in range(count):
            left_ref[pl.ds(i * rows, rows), :] = columns_ref[i, :rows, :]
            small = small + columns_ref[i, rows:, :].astype(FULL)
        for d, ref in enumerate(db_refs):
            at = pl.multiple_of((place_ref[1] ^ d) * pair, 16)
            right_ref[pl.ds(at, pair), :] = ref[...]
        of_project = start + lax.broadcasted_iota(jnp.int32, (wide, width), 0) < PROJECTION_WIDTH
        sum_ref[...] = jnp.where(
            of_project, dot(left_ref[...], n_ref[...], 0, 0), dot(left_ref[...], right_ref[...], 0, 0)
        )
        offset = pl.multiple_of(
            owner * pieces.own_rows - start, math.gcd(pieces.own_rows, 128)
        )
        own = sum_ref[pl.ds(offset, pieces.own_rows), :].astype(LOW)
        for c in range(contexts):
            cut_ref[c] = own[c * quarter : (c + 1) * quarter]
        for d, out_ref in enumerate(out_refs):
            out_ref[:quarter, :] = cut_ref[place_ref[0] ^ d]
            out_ref[quarter:, :] = jnp.zeros_like(out_ref[quarter:, :])
            out_ref[quarter:, :wide] = small.astype(LOW)

    ins = [columns, normed_all, *db_pairs]
    outs = [((quarter + 16, width), LOW)] * contexts
    return call(
        "attention_gradient",
        kernel,
        outs,
        [place, *ins],
        in_specs=[pl.BlockSpec(memory_space=pltpu.SMEM)]
        + [pl.BlockSpec(memory_space=pltpu.VMEM)] * len(ins),
        scratch=[
            pltpu.VMEM((total, wide), LOW),
            pltpu.VMEM((total, width), LOW),
            pltpu.VMEM((wide, width), FULL),
            pltpu.VMEM((contexts, quarter, width), LOW),
        ],
        flops=4 * total * wide * width,
        far=range(contexts),
    )


def total_of(terms):
    result = terms[0].astype(FULL)
    for term in terms[1:]:
        result = result + term.astype(FULL)
    return result


def make(ring, contexts):
    def per_device(
        tokens,
        document_starts,
        attention_weights,
        projection_bias,
        norm_gains,
        hidden_weights,
        cotangent,
    ):
        rows, width = tokens.shape[1:]
        chips = ring.chips
        me = lax.axis_index("ctx")
        index = lax.axis_index("fsdp")
        place = jnp.stack([me, index // 2, index % 2]).astype(jnp.int32)
        own_rows = attention_weights.shape[0]
        quarter = own_rows // contexts
        pieces = Pieces(own_rows, ring.size)
        bias_width = projection_bias.shape[0]
        gain_width = norm_gains.shape[1]

        weight_piece = lax.dynamic_slice_in_dim(attention_weights, me * quarter, quarter, 0)
        weights = lax.all_gather(weight_piece.astype(LOW), ("fsdp", "ctx"), axis=0, tiled=True)

        packed = jnp.concatenate([projection_bias, norm_gains.reshape(-1)]).astype(LOW)
        packed = jnp.pad(packed[None], ((0, 15), (0, width - packed.shape[0])))
        upstream = cotangent[0]
        upstream_pairs = [
            ring.both(b) for b in ring.chained(jnp.concatenate([upstream, packed], axis=0))
        ]
        params = jnp.stack([p.reshape(2, -1, width)[:, rows] for p in upstream_pairs])
        params = params.reshape(ring.size, width)
        owners = jnp.arange(ring.size, dtype=jnp.int32)
        at = owners ^ (index // 2 * 2)
        params = jnp.dot(
            (at[:, None] == owners[None, :]).astype(LOW), params, preferred_element_type=FULL
        )
        bias = params[:, :bias_width].reshape(1, -1)
        gain_one = params[:, bias_width : bias_width + gain_width].reshape(1, -1)
        gain_two = params[:, bias_width + gain_width : bias_width + 2 * gain_width].reshape(1, -1)

        starts = document_starts[0]
        within = jnp.arange(rows, dtype=jnp.int32)
        positions = me * rows + within
        cosine, sine = rope_tables(positions, HEAD_DIM)
        key_positions = jnp.concatenate([(me ^ d) * rows + within for d in range(contexts)])
        mask = jnp.where(
            (segments(starts, positions)[:, None] == segments(starts, key_positions)[None, :])
            & (key_positions[None, :] <= positions[:, None]),
            0.0,
            LOWEST,
        ).astype(FULL)

        gate_rows, up_rows, down_rows = cast_call(hidden_weights)
        back_hidden, upstream_all = back_hidden_call(upstream_pairs, down_rows, rows)
        weights, back_hidden, mask, cosine, sine, bias, gain_one, gain_two = (
            lax.optimization_barrier(
                (weights, back_hidden, mask, cosine, sine, bias, gain_one, gain_two)
            )
        )
        tokens_ahead = ring.begun(after(tokens[0], weights))
        blocks = QUERY_WIDTH // WEIGHT_BLOCK
        kv = project_call(
            tokens[0], gain_one, weights, bias, cosine, sine, blocks, 2 * KEY_WIDTH // WEIGHT_BLOCK,
            far=(0,),
        )
        query = project_call(
            after(tokens[0], kv), gain_one, weights, bias, cosine, sine, 0, blocks
        )
        kv_blocks = context_send([kv] * contexts, contexts)
        lse, residual, normed_two, kv_all, mixed = attend_call(
            query, kv_blocks, mask, tokens[0], weights, gain_two
        )

        kept, back_normed_terms = (), []
        ahead = ring.ahead(after(normed_two, *tokens_ahead[1:3]))
        done = ()
        for d in range(chips):
            *kept, own, other = feed_call(
                d, chips, place, ring.both(after(ahead[d], *done)), back_hidden, gate_rows,
                up_rows, kept,
            )
            if d == 0:
                held = own, other
                done = (own,)
                back_normed_terms.append(own)
                continue
            summed = add_parts(place, own, ring.both(other), 1)[0]
            done = (summed, *back_normed_terms[1:][-1:])
            if d == 3:
                tokens_ahead += ring.rest(tokens_ahead, summed)
            back_normed_terms.append(ring.send(summed, d) if d else summed)
        back, normed_all = kept
        back = after(back, summed)
        hidden_term = weight_gradient_call(back, normed_all, upstream_all)
        hidden_shard = lax.psum_scatter(
            after(hidden_term, *back_normed_terms[-2:]), "ctx", scatter_dimension=0, tiled=True
        ).astype(FULL)
        own, other = held
        back_normed_terms[0] = add_parts(place, own, ring.both(after(other, hidden_term)), 1)[0]
        back_residual, back_branch, back_gain_two, da_query, *kv_back = back_attend_call(
            back_normed_terms, residual, upstream, gain_two, weights, query, kv_all, mask, lse,
            cosine, sine,
        )
        kv_terms = context_send(kv_back, contexts)
        branch_ahead = ring.ahead(back_branch)
        token_pairs = [ring.both(after(b, da_query)) for b in tokens_ahead]
        da_query = after(da_query, *token_pairs, *branch_ahead[1:3])
        back_inputs, projected_pieces = back_project_call(
            kv_terms, da_query, mixed, weights, tokens[0], back_residual, gain_one,
            back_gain_two, cosine, sine, pieces, bias_width, gain_width,
        )
        columns = lax.all_to_all(
            after(projected_pieces, *branch_ahead[1:]), "fsdp", 0, 0, tiled=True
        )
        lifted_own, lifted_other = lifted_call(place, after(back, projected_pieces), down_rows, chips)
        lifted_terms = add_parts(place, lifted_own, ring.send(lifted_other, 0, 1), chips)
        normed_one_all = normed_call(place, token_pairs, after(gain_one, lifted_terms[0]))
        branch_pairs = [ring.both(after(b, lifted_terms[0])) for b in branch_ahead]
        lifted_terms = [ring.send(block, d) if d else block for d, block in enumerate(lifted_terms)]
        output = (residual + total_of(lifted_terms)).astype(LOW)
        attention_terms = attention_gradient_call(
            place, columns, normed_one_all, branch_pairs, pieces, contexts
        )
        attention_terms = context_send(attention_terms, contexts)
        shards = total_of([after(attention_terms[0], output, hidden_shard), *attention_terms[1:]])
        own_bias = bias_width // contexts
        own_gain = gain_width // contexts
        bias_at = index * bias_width % 128 + me * own_bias
        gain_at = index * gain_width % 128 + me * own_gain
        bias_shard = lax.dynamic_slice(shards, (quarter, bias_at), (1, own_bias))[0]
        gain_shard = lax.dynamic_slice(shards, (quarter + 1, gain_at), (2, own_gain))
        return (
            output[None],
            back_inputs[None],
            shards[:quarter],
            bias_shard,
            gain_shard,
            hidden_shard,
        )

    return per_device


def solution(mesh):
    placed = (
        P("fsdp", "ctx", None),
        P("fsdp", None),
        P("fsdp", None),
        P("fsdp"),
        P(None, "fsdp"),
        P("fsdp", None),
        P("fsdp", "ctx", None),
    )
    return jax.shard_map(
        make(Ring(mesh.shape["fsdp"]), mesh.shape["ctx"]),
        mesh=mesh,
        in_specs=placed,
        out_specs=(
            P("fsdp", "ctx", None),
            P("fsdp", "ctx", None),
            P(("fsdp", "ctx"), None),
            P(("fsdp", "ctx")),
            P(None, ("fsdp", "ctx")),
            P(("fsdp", "ctx"), None),
        ),
        check_vma=False,
    )
```
